32 devices in a mesh: layer: 4 (over y, core), phi: 8 (over z, x).
Axes of the slice: x: 2, y: 2, z: 4, core: 2. Of those that a mesh axis runs over, the one named last changes fastest.
Arguments:
- features: bfloat16 [8192, 256], P(('layer', 'phi')), may hold values from -6 to 6
- w_layers: bfloat16 [4, 256, 256], replicated, may hold values from -0.375 to 0.375
- b_layers: float32 [4, 256], replicated, may hold values from -1.5 to 1.5
- w_coord: bfloat16 [16, 256], replicated, may hold values from -0.09375 to 0.09375
- w_beta: bfloat16 [256], replicated, may hold values from -0.375 to 0.375
- point_hit: int32 [256], P(('layer', 'phi')), may hold values from 0 to 255
- track: int32 [8192], P(('layer', 'phi')), may hold values from 0 to 255
- noise: int32 [8192], P(('layer', 'phi')), may hold values 0 or 1
Outputs:
- grad_w_layers: float32 [4, 256, 256], replicated
- grad_b_layers: float32 [4, 256], replicated
- grad_w_coord: float32 [16, 256], replicated
- grad_w_beta: float32 [256], replicated
- loss: float32 [], replicated
The draws below stay inside these ranges and needn't reach their ends.
Inputs may be any that keep to these rules, and one draw needn't show every extreme that they name: `point_hit`: an index among the 256 hits of the device holding the entry. A non-noise hit of track k is attracted to point k.
All inputs are finite; a program needn't handle non-finite values. No bound on the sum of `noise` on one device may be relied on, other than what follows from the above.
Results may differ from the reference program's by a relative error of at most 0.0013.
Values sent between devices are 32-bit elements; how exact they have to be, the bound alone decides.
No kernel may reach another device: no remote copies, remote signals or barrier semaphores. Data moves between devices by JAX's collectives and lax.ppermute only.
A program may use at most 64 MiB of HBM per device.

```python
import jax
import jax.numpy as jnp
from jax import lax

WIDTH = 256
LAYERS = 4
CDIM = 16
HITS_DEV = 256
P_DEV = 8
HITS = 8192
K = 256
N_LAYER = 4
N_PHI = 8


def set_ends(drawn, rng, smallest, high):
    longest = drawn.shape.index(max(drawn.shape))
    spots = []
    for shift in (0, 1):
        where = [jax.random.randint(jax.random.fold_in(rng, axis), (), 0, length) for axis, length in enumerate(drawn.shape)]
        where[longest] = (where[longest] + shift) % drawn.shape[longest]
        spots.append(tuple(where))
    return drawn.at[spots[0]].set(smallest).at[spots[1]].set(high)


def levels(stream_key, shape, pieces, smallest, top_value):
    loudness = 1.0
    for dim, blocks in pieces:
        draws = jax.random.uniform(jax.random.fold_in(jax.random.fold_in(stream_key, 6), dim), (blocks,), jnp.float32, smallest / len(pieces), top_value / len(pieces))
        loudness = loudness * jnp.repeat(jnp.exp(draws), shape[dim] // blocks).reshape((-1,) + (1,) * (len(shape) - 1 - dim))
    return loudness


def normal_values(rng, extent, scale, most, cuts=(), held_as=jnp.bfloat16):
    values = jax.random.normal(rng, extent, jnp.float32) * scale
    if len(cuts) > 0:
        values = levels(rng, extent, cuts, -0.22, 0.18) * values
    return jnp.clip(values, min=-most, max=most).astype(held_as)


def setup_inputs(seed: int = 0) -> dict:
    arg_keys = jax.random.split(jax.random.key(seed), 9)
    return {
        "features": normal_values(arg_keys[0], (HITS, WIDTH), 1.0, 6.0, ((0, 32),)),
        "w_layers": normal_values(arg_keys[1], (LAYERS, WIDTH, WIDTH), WIDTH ** -0.5, 0.375),
        "b_layers": normal_values(arg_keys[2], (LAYERS, WIDTH), 0.3, 1.5, (), jnp.float32),
        "w_coord": normal_values(arg_keys[3], (CDIM, WIDTH), (16 * WIDTH) ** -0.5, 0.09375),
        "w_beta": normal_values(arg_keys[4], (WIDTH,), WIDTH ** -0.5, 0.375),
        "point_hit": set_ends(jax.random.randint(arg_keys[5], (K,), 0, HITS_DEV), jax.random.fold_in(arg_keys[5], 1), 0, HITS_DEV - 1).astype(jnp.int32),
        "track": set_ends(jax.random.randint(arg_keys[6], (HITS,), 0, K), jax.random.fold_in(arg_keys[6], 1), 0, K - 1).astype(jnp.int32),
        "noise": set_ends((jax.random.randint(arg_keys[7], (HITS,), 0, 5) < 1).astype(jnp.int32), jax.random.fold_in(arg_keys[7], 1), 0, 1),
    }


dist_eps = 0.0001
charge_floor = 0.5

def mlp_forward(features, w_layers, b_layers, w_coord, w_beta):
    hidden = features
    states = [features]
    preacts = []
    for layer_num in range(w_layers.shape[0]):
        pre = jnp.dot(hidden, w_layers[layer_num], preferred_element_type=jnp.float32) + b_layers[layer_num]
        preacts.append(pre)
        hidden = jax.nn.silu(pre).astype(jnp.bfloat16)
        states.append(hidden)
    coords = lax.dot_general(w_coord, hidden, (((1,), (1,)), ((), ())), preferred_element_type=jnp.float32)
    logits = jnp.dot(hidden, w_beta, preferred_element_type=jnp.float32)
    return (states, preacts, coords, logits)

def charges(logits):
    expz = jnp.exp(logits)
    spread = jnp.log1p(2.0 * expz)
    charge = 0.25 * spread * spread + charge_floor
    slope = 0.5 * spread * (2.0 * expz / (1.0 + 2.0 * expz))
    return (jax.nn.sigmoid(logits), charge, slope)

def pair_terms(coords, charge, track, live, point_rows, first, hits_all):
    point_y = point_rows[:-1]
    point_q = point_rows[-1]
    width = point_rows.shape[1]
    hit_sq = lax.optimization_barrier(jnp.sum(coords * coords, 0))
    point_sq = lax.optimization_barrier(jnp.sum(point_y * point_y, 0))
    cross = lax.dot_general(coords, point_y, (((0,), (0,)), ((), ())), precision=lax.Precision.HIGHEST, preferred_element_type=jnp.float32)
    dist_sq = jnp.maximum(hit_sq[:, None] + point_sq[None, :] - 2.0 * cross, 0.0)
    dist = jnp.sqrt(dist_sq + dist_eps)
    index = first + lax.iota(jnp.int32, width)
    match = jnp.where((track[:, None] == index[None, :]) & (live[:, None] > 0), 1.0, 0.0)
    reach = jnp.maximum(1.0 - dist, 0.0)
    potential = match * dist_sq + (1.0 - match) * reach * reach
    pot_rows = lax.optimization_barrier(jnp.sum(potential * point_q[None, :], 1))
    coef = (charge / hits_all)[:, None] * point_q[None, :] * (2.0 * match - (1.0 - match) * 2.0 * reach / dist)
    row_sums = lax.optimization_barrier(jnp.sum(coef, 1))
    col_sums = lax.optimization_barrier(jnp.sum(coef, 0))
    pulls = lax.dot_general(point_y, coef, (((1,), (1,)), ((), ())), precision=lax.Precision.HIGHEST, preferred_element_type=jnp.float32)
    point_grad = point_y * col_sums[None, :] - lax.dot_general(coords, coef, (((1,), (0,)), ((), ())), precision=lax.Precision.HIGHEST, preferred_element_type=jnp.float32)
    charge_grad = jnp.dot(charge, potential, precision=lax.Precision.HIGHEST) / hits_all
    return (row_sums, pot_rows, pulls, jnp.concatenate([point_grad, charge_grad[None, :]], 0))

def head_backward(states, preacts, w_layers, w_coord, w_beta, coord_grad, logit_grad):
    coord_low = coord_grad.astype(jnp.bfloat16)
    logit_low = logit_grad.astype(jnp.bfloat16)
    hidden = states[-1]
    grad_coord_w = lax.dot_general(coord_low, hidden, (((1,), (0,)), ((), ())), preferred_element_type=jnp.float32)
    grad_beta_w = jnp.dot(logit_low, hidden, preferred_element_type=jnp.float32)
    upstream = lax.dot_general(coord_low, w_coord, (((0,), (0,)), ((), ())), preferred_element_type=jnp.float32)
    upstream = upstream + logit_low.astype(jnp.float32)[:, None] * w_beta.astype(jnp.float32)[None, :]
    count = w_layers.shape[0]
    weight_grads = [None] * count
    bias_grads = [None] * count
    for layer_num in range(count - 1, -1, -1):
        pre = preacts[layer_num]
        sig = jax.nn.sigmoid(pre)
        local = (upstream * sig * (1.0 + pre * (1.0 - sig))).astype(jnp.bfloat16)
        weight_grads[layer_num] = lax.dot_general(states[layer_num], local, (((0,), (0,)), ((), ())), preferred_element_type=jnp.float32)
        bias_grads[layer_num] = lax.optimization_barrier(jnp.sum(local.astype(jnp.float32), 0))
        if layer_num > 0:
            upstream = lax.dot_general(local, w_layers[layer_num], (((1,), (1,)), ((), ())), preferred_element_type=jnp.float32)
    return (jnp.stack(weight_grads), jnp.stack(bias_grads), grad_coord_w, grad_beta_w)

def reference(features, w_layers, b_layers, w_coord, w_beta, point_hit, track, noise):
    ndev = N_LAYER * N_PHI
    hits_all = HITS * 1.0
    feat_blocks = features.reshape(ndev, HITS_DEV, WIDTH)

    def forward_one(feat):
        states, preacts, coords, logits = mlp_forward(feat, w_layers, b_layers, w_coord, w_beta)
        return (coords, logits)
    coords_all, logits_all = lax.map(forward_one, feat_blocks)
    beta_all, charge_all, slope_all = charges(logits_all)
    owner = jnp.arange(K, dtype=jnp.int32) // P_DEV
    point_y = coords_all[owner, :, point_hit]
    point_rows = jnp.concatenate([point_y.T, charge_all[owner, point_hit][None, :]], 0)
    track_blocks = track.reshape(ndev, HITS_DEV)
    noise_blocks = noise.reshape(ndev, HITS_DEV)
    live_blocks = 1 - noise_blocks

    def scan_pairs(carry, items):
        grads, loss_acc = carry
        coords, charge, trk, live = items
        row_sums, pot_rows, pulls, point_grads = pair_terms(coords, charge, trk, live, point_rows, 0, hits_all)
        coord_grad = coords * row_sums[None, :] - pulls
        return ((grads + point_grads, loss_acc + jnp.sum(charge * pot_rows) / hits_all), (coord_grad, pot_rows))
    init = (jnp.zeros((CDIM + 1, K), jnp.float32), jnp.zeros((), jnp.float32))
    (point_grads, loss_pot), (coord_grads, pot_all) = lax.scan(scan_pairs, init, (coords_all, charge_all, track_blocks, live_blocks))
    coord_grads = coord_grads.at[owner, :, point_hit].add(point_grads[:CDIM].T)
    charge_grad = (pot_all / hits_all).at[owner, point_hit].add(point_grads[CDIM])
    noise_float = noise_blocks.astype(jnp.float32)
    beta_grad = (noise_float / hits_all).at[owner, point_hit].add(-1.0 / K)
    logit_grads = charge_grad * slope_all + beta_grad * beta_all * (1.0 - beta_all)
    loss = loss_pot + jnp.sum(1.0 - beta_all[owner, point_hit]) / K + jnp.sum(noise_float * beta_all) / hits_all

    def scan_back(carry, items):
        feat, coord_grad, logit_grad = items
        states, preacts, coords, logits = mlp_forward(feat, w_layers, b_layers, w_coord, w_beta)
        parts = head_backward(states, preacts, w_layers, w_coord, w_beta, coord_grad, logit_grad)
        return (tuple((total + part for total, part in zip(carry, parts))), None)
    zeros = (jnp.zeros((LAYERS, WIDTH, WIDTH), jnp.float32), jnp.zeros((LAYERS, WIDTH), jnp.float32), jnp.zeros((CDIM, WIDTH), jnp.float32), jnp.zeros((WIDTH,), jnp.float32))
    totals, unused = lax.scan(scan_back, zeros, (feat_blocks, coord_grads, logit_grads))
    return (totals[0], totals[1], totals[2], totals[3], loss)
```

```python
import functools

import jax
import jax.numpy as jnp
from jax import lax
from jax.experimental import pallas as pl
from jax.experimental.pallas import tpu as pltpu
from jax.sharding import PartitionSpec as P

dist_eps = 0.0001
charge_floor = 0.5
AXES = ("layer", "phi")
VMEM = pl.BlockSpec(memory_space=pltpu.VMEM)
SMEM = pl.BlockSpec(memory_space=pltpu.SMEM)
HIGH = lax.Precision.HIGHEST
PARAMS = pltpu.CompilerParams(vmem_limit_bytes=48 * 1024 * 1024)


def matmul(a, b, ca=1, cb=0, precision=None):
    return lax.dot_general(
        a, b, (((ca,), (cb,)), ((), ())), precision=precision, preferred_element_type=jnp.float32
    )


def iota(shape, dim):
    return lax.broadcasted_iota(jnp.int32, shape, dim)


def head_rows(wc_ref, wb_ref):
    dim = wc_ref.shape[0]
    width = wc_ref.shape[1]
    beta_row = jnp.broadcast_to(wb_ref[...].astype(jnp.float32), (dim, width))
    tail = jnp.where(iota((dim, width), 0) == 0, beta_row, 0.0).astype(jnp.bfloat16)
    return jnp.concatenate([wc_ref[...], tail], 0)


def point_column(hit_ref, shift, shape):
    count = hit_ref.shape[0]
    rows = iota(shape, 0)
    col = jnp.zeros(shape, jnp.int32)
    for p in range(count):
        col = jnp.where(rows == (p + shift) % count, hit_ref[p], col)
    return col


def embed_kernel(
    pos_ref, hit_ref, feat_ref, w_ref, b_ref, wc_ref, wb_ref, track_ref, noise_ref,
    pay_ref, act_ref, aux_ref,
):
    dim = wc_ref.shape[0]
    hits = feat_ref.shape[0]
    points = hit_ref.shape[0]
    h = feat_ref[...]
    for l in range(w_ref.shape[0]):
        a = matmul(h, w_ref[l]) + b_ref[l : l + 1, :]
        act_ref[l] = a
        h = (a * jax.nn.sigmoid(a)).astype(jnp.bfloat16)
    xz = matmul(head_rows(wc_ref, wb_ref), h, 1, 1)
    z = xz[dim : dim + 1]
    expz = jnp.exp(z)
    spread = jnp.log1p(2.0 * expz)
    q = 0.25 * spread * spread + charge_floor
    slope = 0.5 * spread * (2.0 * expz / (1.0 + 2.0 * expz))
    beta = jax.nn.sigmoid(z)
    noise = noise_ref[...]
    label = jnp.where(noise == 0, track_ref[...], -1).astype(jnp.float32)
    rows8 = iota((8, hits), 0)
    aux_ref[...] = jnp.where(
        rows8 == 0, beta, jnp.where(rows8 == 1, slope, noise.astype(jnp.float32))
    )
    sel = iota((points, hits), 1) == point_column(hit_ref, 2, (points, hits))
    lane = iota((points, 128), 1)
    order = lax.rem(iota((points, 128), 0) + (points - 2), points)
    pts = jnp.where(lane == dim + 1, (pos_ref[0] * points + order).astype(jnp.float32), 0.0)
    for c in range(dim):
        v = jnp.sum(jnp.where(sel, xz[c : c + 1], 0.0), axis=1, keepdims=True)
        pts = jnp.where(lane == c, v, pts)
    v = jnp.sum(jnp.where(sel, q, 0.0), axis=1, keepdims=True)
    pts = jnp.where(lane == dim, v, pts)
    row = iota((points, 128), 0)
    moved = pltpu.roll(pts, 2, 0)
    left = jnp.where(row == 0, q[:, :128], jnp.where(row == 1, label[:, :128], pts))
    right = jnp.where(row == 0, q[:, 128:], jnp.where(row == 1, label[:, 128:], moved))
    pay_ref[0:dim, :] = xz[0:dim]
    pay_ref[dim : dim + 8, 0:128] = left
    pay_ref[dim : dim + 8, 128:256] = right


def residual_kernel(act_ref, feat_ref, w_ref, slope_ref, ht_ref, last_ref, wt_ref):
    layers = w_ref.shape[0]
    ht_ref[0] = feat_ref[...].T
    for l in range(layers):
        a = act_ref[l]
        sig = jax.nn.sigmoid(a)
        slope_ref[l] = sig * (1.0 + a * (1.0 - sig))
        h = (a * sig).astype(jnp.bfloat16)
        if l < layers - 1:
            ht_ref[l + 1] = h.T
            wt_ref[l] = w_ref[l + 1].T
        else:
            last_ref[...] = h


def point_tile(left, right):
    rows = iota(left.shape, 0)
    return jnp.where(rows < 2, pltpu.roll(right, 6, 0), left)


def pair_weights(dist_sq, match):
    shifted = dist_sq + dist_eps
    inv = lax.rsqrt(shifted)
    reach = jnp.maximum(1.0 - shifted * inv, 0.0)
    potential = jnp.where(match, dist_sq, reach * reach)
    weight = jnp.where(match, 2.0, -2.0 * jnp.maximum(inv - 1.0, 0.0))
    return potential, weight


def backward_kernel(
    hits_all, points_all, parts,
    pos_ref, hit_ref, pay_ref, aux_ref, slope_ref, ht_ref, last_ref, wt_ref, wc_ref, wb_ref, *rest,
):
    groups = rest[:parts]
    keep_ref, send_ref, xb, yb, gx_ref, stack, ext = rest[parts:]
    dim = wc_ref.shape[0]
    points = hit_ref.shape[0]
    hits = pay_ref.shape[1]
    layers = slope_ref.shape[0]
    full = (8, hits)
    own = pay_ref[dim : dim + 8, :]
    q_row = own[0:1]
    label_row = own[1:2]
    own = point_tile(own[:, :128], own[:, 128:])
    for c in range(dim):
        xb[c] = jnp.broadcast_to(pay_ref[c : c + 1, :], full)
        yb[c] = jnp.broadcast_to(own[:, c : c + 1], full)
    label_b = jnp.broadcast_to(label_row, full)
    index_b = jnp.broadcast_to(own[:, dim + 1 : dim + 2], full)
    zero = jnp.zeros(full, jnp.float32)

    def hit_side(ref):
        def body(j, carry):
            pot_acc, acc = carry
            tile = ref[j, dim : dim + 8, :]
            tile = point_tile(tile[:, :128], tile[:, 128:])
            diffs = []
            dist_sq = zero
            for c in range(dim):
                diff = xb[c] - tile[:, c : c + 1]
                diffs.append(diff)
                dist_sq = dist_sq + diff * diff
            point_q = tile[:, dim : dim + 1]
            potential, weight = pair_weights(dist_sq, label_b == tile[:, dim + 1 : dim + 2])
            weight = weight * point_q
            return pot_acc + potential * point_q, tuple(
                s + weight * diff for s, diff in zip(acc, diffs)
            )

        return body

    def point_side(ref):
        def body(j, carry):
            pot_acc, acc = carry
            diffs = []
            dist_sq = zero
            for c in range(dim):
                diff = yb[c] - ref[j, c : c + 1, :]
                diffs.append(diff)
                dist_sq = dist_sq + diff * diff
            hit_q = ref[j, dim : dim + 1, :]
            potential, weight = pair_weights(dist_sq, index_b == ref[j, dim + 1 : dim + 2, :])
            weight = weight * hit_q
            potential = potential * hit_q
            new = []
            for s, diff in zip(acc, diffs):
                term = weight * diff
                new.append(s + term[:, :128] + term[:, 128:])
            return pot_acc + potential[:, :128] + potential[:, 128:], tuple(new)

        return body

    carry = (zero, (zero,) * dim)
    for ref in groups:
        carry = lax.fori_loop(0, ref.shape[0], hit_side(ref), carry)
    pot_row = jnp.sum(carry[0], axis=0, keepdims=True)
    scaled = q_row * (1.0 / hits_all)
    for c in range(dim):
        gx_ref[c : c + 1, :] = jnp.sum(carry[1][c], axis=0, keepdims=True) * scaled

    half = jnp.zeros((8, 128), jnp.float32)
    carry = (half, (half,) * dim)
    for ref in groups:
        carry = lax.fori_loop(0, ref.shape[0], point_side(ref), carry)
    lane = iota((8, 128), 1)
    own_q = own[:, dim : dim + 1] * (1.0 / hits_all)
    grads = jnp.where(lane == dim + 1, 1.0, 0.0)
    for c in range(dim):
        v = jnp.sum(carry[1][c], axis=1, keepdims=True) * own_q
        grads = jnp.where(lane == c, v, grads)
    v = jnp.sum(carry[0], axis=1, keepdims=True) * (1.0 / hits_all)
    grads = jnp.where(lane == dim, v, grads)
    sel = iota(full, 1) == point_column(hit_ref, 2, full)
    added = matmul(grads, jnp.where(sel, 1.0, 0.0), 0, 0, HIGH)

    beta = aux_ref[0:1, :]
    noise = aux_ref[2:3, :]
    count = added[dim + 1 : dim + 2]
    grad_q = pot_row * (1.0 / hits_all) + added[dim : dim + 1]
    grad_b = noise * (1.0 / hits_all) - count * (1.0 / points_all)
    grad_z = grad_q * aux_ref[1:2, :] + grad_b * beta * (1.0 - beta)
    per_hit = q_row * pot_row * (1.0 / hits_all) + noise * beta * (1.0 / hits_all)
    per_hit = per_hit - count * beta * (1.0 / points_all)
    loss = jnp.sum(per_hit, axis=1, keepdims=True) + points * 1.0 / points_all

    grad_x = gx_ref[...] + added[0:dim]
    tail = jnp.where(iota((dim, hits), 0) == 0, grad_z, 0.0)
    low = jnp.concatenate([grad_x, tail], 0).astype(jnp.bfloat16)
    head = head_rows(wc_ref, wb_ref)
    grad_head = matmul(low, last_ref[...])
    up = matmul(low, head, 0, 0)
    ext[...] = jnp.zeros(ext.shape, jnp.float32)
    cols = [slice(0, 128), slice(128, 256)]
    base = 2 * layers
    for h, col in enumerate(cols):
        ext[base + h * dim : base + (h + 1) * dim, :] = grad_head[0:dim, col]
        ext[base + 2 * dim + h : base + 2 * dim + h + 1, :] = grad_head[dim : dim + 1, col]
    ext[base + 2 * dim + 2 : base + 2 * dim + 3, :] = jnp.broadcast_to(loss, (1, 128))
    blocks = stack.shape[0]
    rows = layers * hits // blocks
    per_layer = blocks // layers
    for l in range(layers - 1, -1, -1):
        err = (up * slope_ref[l]).astype(jnp.bfloat16)
        if l > 0:
            up = matmul(err, wt_ref[l - 1])
        grad_w = matmul(ht_ref[l], err)
        bias = jnp.sum(err.astype(jnp.float32), axis=0, keepdims=True)
        for h, col in enumerate(cols):
            ext[h * layers + l : h * layers + l + 1, :] = bias[:, col]
            for s in range(per_layer):
                stack[l * per_layer + s, h * rows : (h + 1) * rows, :] = grad_w[
                    s * rows : (s + 1) * rows, col
                ]
    for b in range(blocks):
        stack[b, 2 * rows : 2 * rows + 8, :] = ext[8 * b : 8 * b + 8, :]
    me = pos_ref[1]
    for j in range(blocks // 2):
        keep_ref[j] = stack[jnp.bitwise_xor(me, j)]
        send_ref[j] = stack[jnp.bitwise_xor(me, j + blocks // 2)]


def finish_kernel(pos_ref, *refs):
    quarter = refs[:-7]
    other, gw_ref, gb_ref, gc_ref, gbeta_ref, loss_ref, ext = refs[-7:]
    blocks = 2 * len(quarter)
    rows = gw_ref.shape[1]
    dim = gc_ref.shape[0]
    layers = gb_ref.shape[0]
    me = pos_ref[1]
    for r in range(blocks):
        if r < len(quarter):
            block = quarter[r][...]
        else:
            block = other[r - len(quarter)]
        place = jnp.bitwise_xor(me, r)
        gw_ref[place, :, 0:128] = block[0:rows]
        gw_ref[place, :, 128:256] = block[rows : 2 * rows]
        ext[place] = block[2 * rows :]
    flat = [ext[b] for b in range(blocks)]
    flat = jnp.concatenate(flat, 0)
    base = 2 * layers
    for h, col in enumerate([slice(0, 128), slice(128, 256)]):
        gb_ref[:, col] = flat[h * layers : (h + 1) * layers]
        gc_ref[:, col] = flat[base + h * dim : base + (h + 1) * dim]
        gbeta_ref[:, col] = flat[base + 2 * dim + h : base + 2 * dim + h + 1]
    loss_ref[...] = flat[base + 2 * dim + 2 : base + 2 * dim + 3, 0:1]


def bits_of(size):
    return [1 << t for t in range(size.bit_length() - 1)]


def on_device(layer_size, phi_size, features, w_layers, b_layers, w_coord, w_beta, point_hit, track, noise):
    ndev = layer_size * phi_size
    hits, width = features.shape
    layers = w_layers.shape[0]
    dim = w_coord.shape[0]
    points = point_hit.shape[0]
    hits_all = hits * ndev * 1.0
    points_all = points * ndev * 1.0
    f32 = jnp.float32
    core = phi_size
    plane = [1, 2 * phi_size]
    others = [b for b in bits_of(ndev) if b != core and b not in plane]

    def swap(x, mask):
        return lax.ppermute(x, AXES, [(i, i ^ mask) for i in range(ndev)])

    me = lax.axis_index("layer") * phi_size + lax.axis_index("phi")
    slot = (me // core) % 2 * 4 + (me // plane[1]) % 2 * 2 + me % 2
    pos = jnp.stack([me, slot]).astype(jnp.int32)
    w_beta = w_beta.reshape(1, width)
    track = track.reshape(1, hits)
    noise = noise.reshape(1, hits)

    pay, act, aux = pl.pallas_call(
        embed_kernel,
        out_shape=(
            jax.ShapeDtypeStruct((dim + 8, hits), f32),
            jax.ShapeDtypeStruct((layers, hits, width), f32),
            jax.ShapeDtypeStruct((8, hits), f32),
        ),
        in_specs=[SMEM, SMEM] + [VMEM] * 7,
        out_specs=(VMEM,) * 3,
        compiler_params=PARAMS,
        name="embed",
    )(pos, point_hit, features, w_layers, b_layers, w_coord, w_beta, track, noise)

    slope, ht, last, wt = pl.pallas_call(
        residual_kernel,
        out_shape=(
            jax.ShapeDtypeStruct((layers, hits, width), f32),
            jax.ShapeDtypeStruct((layers, width, hits), jnp.bfloat16),
            jax.ShapeDtypeStruct((hits, width), jnp.bfloat16),
            jax.ShapeDtypeStruct((layers - 1, width, width), jnp.bfloat16),
        ),
        in_specs=[VMEM] * 3,
        out_specs=(VMEM,) * 4,
        compiler_params=PARAMS,
        cost_estimate=pl.CostEstimate(
            flops=20 * layers * hits * width, bytes_accessed=6 * layers * hits * width,
            transcendentals=layers * hits * width,
        ),
        name="residuals",
    )(act, features, w_layers)

    rows_all = pay[None]
    stages = [others[i : i + 2] for i in range(0, len(others), 2)] + [plane]
    for stage in stages:
        masks = stage + ([stage[0] ^ stage[1]] if len(stage) > 1 else [])
        rows_all = jnp.concatenate([rows_all] + [swap(rows_all, m) for m in masks], 0)
    rows_far = swap(rows_all, core)

    blocks = 8
    block_rows = 2 * (layers * width // blocks) + 8
    half = jax.ShapeDtypeStruct((blocks // 2, block_rows, 128), f32)
    keep, send = pl.pallas_call(
        functools.partial(backward_kernel, hits_all, points_all, 2),
        out_shape=(half, half),
        in_specs=[SMEM, SMEM] + [VMEM] * 10,
        out_specs=(VMEM, VMEM),
        scratch_shapes=[
            pltpu.VMEM((dim, 8, hits), f32),
            pltpu.VMEM((dim, 8, hits), f32),
            pltpu.VMEM((dim, hits), f32),
            pltpu.VMEM((blocks, block_rows, 128), f32),
            pltpu.VMEM((8 * blocks, 128), f32),
        ],
        compiler_params=PARAMS,
        name="pairs_backward",
    )(pos, point_hit, pay, aux, slope, ht, last, wt, w_coord, w_beta, rows_all, rows_far)

    total = keep + swap(send, core)
    masks = [plane[0], plane[1], plane[0] ^ plane[1]]
    mine = total[0]
    arrived = [swap(total[r + 1], m) for r, m in enumerate(masks)]
    mine = (mine + arrived[0]) + (arrived[1] + arrived[2])
    for m in others:
        mine = mine + swap(mine, m)
    quarter = [mine] + [swap(mine, m) for m in masks]
    far = swap(jnp.stack(quarter), core)

    gw, gb, gc, gbeta, loss = pl.pallas_call(
        finish_kernel,
        out_shape=(
            jax.ShapeDtypeStruct((blocks, layers * width // blocks, width), f32),
            jax.ShapeDtypeStruct((layers, width), f32),
            jax.ShapeDtypeStruct((dim, width), f32),
            jax.ShapeDtypeStruct((1, width), f32),
            jax.ShapeDtypeStruct((1, 1), f32),
        ),
        in_specs=[SMEM] + [VMEM] * 5,
        out_specs=(VMEM,) * 5,
        scratch_shapes=[pltpu.VMEM((blocks, 8, 128), f32)],
        compiler_params=PARAMS,
        name="finish",
    )(pos, *quarter, far)
    return (
        gw.reshape(layers, width, width),
        gb,
        gc,
        gbeta.reshape(width),
        loss.reshape(()),
    )


def solution(mesh):
    split = P(AXES)
    return jax.shard_map(
        functools.partial(on_device, mesh.shape["layer"], mesh.shape["phi"]),
        mesh=mesh,
        in_specs=(P(AXES, None), P(), P(), P(), P(), split, split, split),
        out_specs=(P(), P(), P(), P(), P()),
        check_vma=False,
    )
```

```python
import functools

import jax
import jax.numpy as jnp
from jax import lax
from jax.experimental import pallas as pl
from jax.experimental.pallas import tpu as pltpu
from jax.sharding import PartitionSpec as P

dist_eps = 0.0001
charge_floor = 0.5
AXES = ("layer", "phi")
VMEM = pl.BlockSpec(memory_space=pltpu.VMEM)
HBM = pl.BlockSpec(memory_space=pltpu.HBM)
UNROLL = 4
EMBED_VMEM = 63400000
HIGH = lax.Precision.HIGHEST
PARAMS = pltpu.CompilerParams(vmem_limit_bytes=48 * 1024 * 1024)


def matmul(a, b, ca=1, cb=0, precision=None):
    return lax.dot_general(
        a, b, (((ca,), (cb,)), ((), ())), precision=precision, preferred_element_type=jnp.float32
    )


def iota(shape, dim):
    return lax.broadcasted_iota(jnp.int32, shape, dim)


def head_rows(wc_ref, wb_ref):
    dim = wc_ref.shape[0]
    width = wc_ref.shape[1]
    beta_row = jnp.broadcast_to(wb_ref[...].astype(jnp.float32).reshape(1, width), (dim, width))
    tail = jnp.where(iota((dim, width), 0) == 0, beta_row, 0.0).astype(jnp.bfloat16)
    return jnp.concatenate([wc_ref[...], tail], 0)


def flat_index(axis_sizes):
    return lax.axis_index("layer") * axis_sizes[1] + lax.axis_index("phi")


def block_index(axis_sizes):
    me = flat_index(axis_sizes)
    core = lax.shift_right_logical(me, axis_sizes[1].bit_length() - 1) & 1
    upper = lax.shift_right_logical(me, axis_sizes[1].bit_length()) & 1
    return core * 4 + upper * 2 + (me & 1)


def embed_kernel(
    sizes,
    hit_hbm, feat_hbm, w_hbm, b_hbm, wc_hbm, wb_hbm, track_hbm, noise_hbm,
    pay_ref, aux_ref,
    hit_ref, feat_ref, w_ref, b_ref, wc_ref, wb_ref, track_ref, noise_ref, sems,
):
    dim = wc_ref.shape[0]
    hits = feat_ref.shape[0]
    points = hit_ref.shape[0]
    layers = w_ref.shape[0]
    pairs = [(feat_hbm, feat_ref)] + [(w_hbm.at[l], w_ref.at[l]) for l in range(layers)]
    pairs = pairs[:2] + [(b_hbm, b_ref)] + pairs[2:]
    pairs += [(wc_hbm, wc_ref), (wb_hbm, wb_ref), (track_hbm, track_ref)]
    pairs += [(noise_hbm, noise_ref), (hit_hbm, hit_ref)]
    copies = [
        pltpu.make_async_copy(src, dst, sems.at[i]) for i, (src, dst) in enumerate(pairs)
    ]
    for copy in copies:
        copy.start()
    for copy in copies[:3]:
        copy.wait()
    h = feat_ref[...]
    for l in range(layers):
        if l > 0:
            copies[l + 2].wait()
        a = matmul(h, w_ref[l]) + b_ref[l : l + 1, :]
        h = (a * jax.nn.sigmoid(a)).astype(jnp.bfloat16)
    for copy in copies[layers + 2 :]:
        copy.wait()
    xz = matmul(head_rows(wc_ref, wb_ref), h, 1, 1)
    z = xz[dim : dim + 1]
    expz = jnp.exp(z)
    spread = jnp.log1p(2.0 * expz)
    q = 0.25 * spread * spread + charge_floor
    slope = 0.5 * spread * (2.0 * expz / (1.0 + 2.0 * expz))
    beta = jax.nn.sigmoid(z)
    noise = noise_ref[...]
    label = jnp.where(noise == 0, track_ref[...], -1).astype(jnp.float32)
    rows8 = iota((8, hits), 0)
    aux_ref[0:8, :] = jnp.where(
        rows8 == 0, beta, jnp.where(rows8 == 1, slope, noise.astype(jnp.float32))
    )
    col = jnp.zeros((points, hits), jnp.int32)
    for p in range(points):
        col = jnp.where(rows8 == (p + 2) % points, hit_ref[p], col)
    sel = iota((points, hits), 1) == col
    aux_ref[8:16, :] = jnp.where(sel, 1.0, 0.0)
    lane = iota((points, 128), 1)
    row = iota((points, 128), 0)
    order = jnp.where(row < 2, row + points - 2, row - 2)
    pts = jnp.where(lane == dim + 1, (flat_index(sizes) * points + order).astype(jnp.float32), 0.0)
    for c in range(dim):
        v = jnp.sum(jnp.where(sel, xz[c : c + 1], 0.0), axis=1, keepdims=True)
        pts = jnp.where(lane == c, v, pts)
    v = jnp.sum(jnp.where(sel, q, 0.0), axis=1, keepdims=True)
    pts = jnp.where(lane == dim, v, pts)
    moved = pltpu.roll(pts, 2, 0)
    left = jnp.where(row == 0, q[:, :128], jnp.where(row == 1, label[:, :128], pts))
    right = jnp.where(row == 0, q[:, 128:], jnp.where(row == 1, label[:, 128:], moved))
    pay_ref[0:dim, :] = xz[0:dim]
    pay_ref[dim : dim + 8, 0:128] = left
    pay_ref[dim : dim + 8, 128:256] = right


def residual_kernel(
    feat_ref, w_ref, b_ref, wc_ref, wb_ref, slope_ref, ht_ref, last_ref, wt_ref, head_ref
):
    head_ref[...] = head_rows(wc_ref, wb_ref)
    layers = w_ref.shape[0]
    h = feat_ref[...]
    ht_ref[0] = h.T
    for l in range(layers):
        a = matmul(h, w_ref[l]) + b_ref[l : l + 1, :]
        sig = jax.nn.sigmoid(a)
        slope_ref[l] = sig * (1.0 + a * (1.0 - sig))
        h = (a * sig).astype(jnp.bfloat16)
        if l < layers - 1:
            ht_ref[l + 1] = h.T
            wt_ref[l] = w_ref[l + 1].T
        else:
            last_ref[...] = h


def point_tile(left, right):
    rows = iota(left.shape, 0)
    return jnp.where(rows < 2, pltpu.roll(right, 6, 0), left)


def pair_weights(dist_sq, match):
    shifted = dist_sq + dist_eps
    inv = lax.rsqrt(shifted)
    reach = jnp.maximum(1.0 - shifted * inv, 0.0)
    potential = jnp.where(match, dist_sq, reach * reach)
    weight = jnp.where(match, 2.0, -2.0 * jnp.maximum(inv - 1.0, 0.0))
    return potential, weight


def spread_kernel(pay_ref, copy_ref, own_ref, xb, yb):
    dim = xb.shape[0]
    full = xb.shape[1:]
    copy_ref[...] = pay_ref[...]
    own = pay_ref[dim : dim + 8, :]
    own = point_tile(own[:, :128], own[:, 128:])
    own_ref[...] = own
    for c in range(dim):
        xb[c] = jnp.broadcast_to(pay_ref[c : c + 1, :], full)
        yb[c] = jnp.broadcast_to(own[:, c : c + 1], full)


def pair_sums(pay_ref, own, ref, xb, yb, hit_acc, point_acc):
    dim = xb.shape[0]
    full = xb.shape[1:]
    label_b = jnp.broadcast_to(pay_ref[dim + 1 : dim + 2, :], full)
    index_b = jnp.broadcast_to(own[:, dim + 1 : dim + 2], full)
    zero = jnp.zeros(full, jnp.float32)

    def hit_side(j, acc):
        tile = ref[j, dim : dim + 8, :]
        tile = point_tile(tile[:, :128], tile[:, 128:])
        diffs = []
        dist_sq = zero
        for c in range(dim):
            diff = xb[c] - tile[:, c : c + 1]
            diffs.append(diff)
            dist_sq = dist_sq + diff * diff
        point_q = tile[:, dim : dim + 1]
        potential, weight = pair_weights(dist_sq, label_b == tile[:, dim + 1 : dim + 2])
        weight = weight * point_q
        terms = [weight * diff for diff in diffs] + [potential * point_q]
        return tuple(s + term for s, term in zip(acc, terms))

    def point_side(j, acc):
        diffs = []
        dist_sq = zero
        for c in range(dim):
            diff = yb[c] - ref[j, c : c + 1, :]
            diffs.append(diff)
            dist_sq = dist_sq + diff * diff
        hit_q = ref[j, dim : dim + 1, :]
        potential, weight = pair_weights(dist_sq, index_b == ref[j, dim + 1 : dim + 2, :])
        weight = weight * hit_q
        terms = [weight * diff for diff in diffs] + [potential * hit_q]
        return tuple(s + term[:, :128] + term[:, 128:] for s, term in zip(acc, terms))

    hit_acc = lax.fori_loop(0, ref.shape[0], hit_side, hit_acc, unroll=UNROLL)
    point_acc = lax.fori_loop(0, ref.shape[0], point_side, point_acc, unroll=UNROLL)
    return hit_acc, point_acc


def near_kernel(pay_ref, own_ref, xb, yb, rows_ref, hit_ref, point_ref):
    dim = xb.shape[0]
    own = own_ref[...]
    hit_acc = (jnp.zeros(hit_ref.shape[1:], jnp.float32),) * (dim + 1)
    point_acc = (jnp.zeros(point_ref.shape[1:], jnp.float32),) * (dim + 1)
    hit_acc, point_acc = pair_sums(pay_ref, own, rows_ref, xb, yb, hit_acc, point_acc)
    for c in range(dim + 1):
        hit_ref[c] = hit_acc[c]
        point_ref[c] = point_acc[c]


def backward_kernel(
    sizes, hits_all, points_all,
    pay_ref, own_ref, xb, yb, aux_ref, slope_ref, ht_ref, last_ref, wt_ref, head_ref, rows_ref, hit_ref, point_ref,
    keep_ref, send_ref, gx_ref, stack, ext,
):
    dim = xb.shape[0]
    hits = pay_ref.shape[1]
    layers = slope_ref.shape[0]
    points = own_ref.shape[0]
    own = own_ref[...]
    q_row = pay_ref[dim : dim + 1, :]
    hit_acc = tuple(hit_ref[c] for c in range(dim + 1))
    point_acc = tuple(point_ref[c] for c in range(dim + 1))
    hit_acc, point_acc = pair_sums(pay_ref, own, rows_ref, xb, yb, hit_acc, point_acc)

    pot_row = jnp.sum(hit_acc[dim], axis=0, keepdims=True)
    scaled = q_row * (1.0 / hits_all)
    for c in range(dim):
        gx_ref[c : c + 1, :] = jnp.sum(hit_acc[c], axis=0, keepdims=True) * scaled
    lane = iota((8, 128), 1)
    own_q = own[:, dim : dim + 1] * (1.0 / hits_all)
    grads = jnp.where(lane == dim + 1, 1.0, 0.0)
    for c in range(dim):
        v = jnp.sum(point_acc[c], axis=1, keepdims=True) * own_q
        grads = jnp.where(lane == c, v, grads)
    v = jnp.sum(point_acc[dim], axis=1, keepdims=True) * (1.0 / hits_all)
    grads = jnp.where(lane == dim, v, grads)
    added = matmul(grads, aux_ref[8:16, :], 0, 0, HIGH)

    beta = aux_ref[0:1, :]
    noise = aux_ref[2:3, :]
    count = added[dim + 1 : dim + 2]
    grad_q = pot_row * (1.0 / hits_all) + added[dim : dim + 1]
    grad_b = noise * (1.0 / hits_all) - count * (1.0 / points_all)
    grad_z = grad_q * aux_ref[1:2, :] + grad_b * beta * (1.0 - beta)
    per_hit = q_row * pot_row * (1.0 / hits_all) + noise * beta * (1.0 / hits_all)
    per_hit = per_hit - count * beta * (1.0 / points_all)
    loss = jnp.sum(per_hit, axis=1, keepdims=True) + points * 1.0 / points_all

    grad_x = gx_ref[...] + added[0:dim]
    tail = jnp.where(iota((dim, hits), 0) == 0, grad_z, 0.0)
    low = jnp.concatenate([grad_x, tail], 0).astype(jnp.bfloat16)
    head = head_ref[...]
    grad_head = matmul(low, last_ref[...])
    up = matmul(low, head, 0, 0)
    ext[...] = jnp.zeros(ext.shape, jnp.float32)
    cols = [slice(0, 128), slice(128, 256)]
    base = 2 * layers
    for h, col in enumerate(cols):
        ext[base + h * dim : base + (h + 1) * dim, :] = grad_head[0:dim, col]
        ext[base + 2 * dim + h : base + 2 * dim + h + 1, :] = grad_head[dim : dim + 1, col]
    ext[base + 2 * dim + 2 : base + 2 * dim + 3, :] = jnp.broadcast_to(loss, (1, 128))
    blocks = stack.shape[0]
    rows = layers * hits // blocks
    per_layer = blocks // layers
    for l in range(layers - 1, -1, -1):
        err = (up * slope_ref[l]).astype(jnp.bfloat16)
        if l > 0:
            up = matmul(err, wt_ref[l - 1])
        grad_w = matmul(ht_ref[l], err)
        bias = jnp.sum(err.astype(jnp.float32), axis=0, keepdims=True)
        for h, col in enumerate(cols):
            ext[h * layers + l : h * layers + l + 1, :] = bias[:, col]
            for s in range(per_layer):
                stack[l * per_layer + s, h * rows : (h + 1) * rows, :] = grad_w[
                    s * rows : (s + 1) * rows, col
                ]
    for b in range(blocks):
        stack[b, 2 * rows : 2 * rows + 8, :] = ext[8 * b : 8 * b + 8, :]
    me = block_index(sizes)
    for j in range(blocks // 2):
        keep_ref[j] = stack[jnp.bitwise_xor(me, j)]
        send_ref[j] = stack[jnp.bitwise_xor(me, j + blocks // 2)]


def place_copies(sizes, blocks, first, gw_ref, sems):
    rows = gw_ref.shape[1]
    me = block_index(sizes)
    copies = []
    for r, block in enumerate(blocks):
        place = jnp.bitwise_xor(me, first + r)
        for h in range(2):
            copies.append(
                pltpu.make_async_copy(
                    block.at[pl.ds(h * rows, rows)],
                    gw_ref.at[place, :, pl.ds(h * 128, 128)],
                    sems.at[2 * r + h],
                )
            )
    for copy in copies:
        copy.start()
    return copies


def place_near_kernel(sizes, *refs):
    blocks = refs[:4]
    gw_ref, ext_ref, sems = refs[4:]
    rows = gw_ref.shape[1]
    copies = place_copies(sizes, blocks, 0, gw_ref, sems)
    for r, block in enumerate(blocks):
        ext_ref[r] = block[2 * rows :, :]
    for copy in copies:
        copy.wait()


def place_far_kernel(
    sizes, far_ref, near_ref, gw_in, gw_ref, *rest
):
    outs, scratch, (ext, sems, small_sems) = rest[:4], rest[4:8], rest[8:]
    gb_ref, gc_ref, gbeta_ref, loss_ref = scratch
    rows = gw_ref.shape[1]
    half = far_ref.shape[0]
    dim = gc_ref.shape[0]
    layers = gb_ref.shape[0]
    blocks = [far_ref.at[r] for r in range(half)]
    copies = place_copies(sizes, blocks, half, gw_ref, sems)
    me = block_index(sizes)
    for r in range(half):
        ext[jnp.bitwise_xor(me, r)] = near_ref[r]
        ext[jnp.bitwise_xor(me, half + r)] = far_ref[r, 2 * rows :, :]
    flat = jnp.concatenate([ext[b] for b in range(2 * half)], 0)
    base = 2 * layers
    for h, col in enumerate([slice(0, 128), slice(128, 256)]):
        gb_ref[:, col] = flat[h * layers : (h + 1) * layers]
        gc_ref[:, col] = flat[base + h * dim : base + (h + 1) * dim]
        gbeta_ref[:, col] = flat[base + 2 * dim + h : base + 2 * dim + h + 1]
    loss_ref[...] = flat[base + 2 * dim + 2 : base + 2 * dim + 3, 0:1]
    for i in range(4):
        copies.append(pltpu.make_async_copy(scratch[i], outs[i], small_sems.at[i]))
        copies[-1].start()
    for copy in copies:
        copy.wait()


def bits_of(size):
    return [1 << t for t in range(size.bit_length() - 1)]


def on_device(layer_size, phi_size, features, w_layers, b_layers, w_coord, w_beta, point_hit, track, noise):
    ndev = layer_size * phi_size
    hits, width = features.shape
    layers = w_layers.shape[0]
    dim = w_coord.shape[0]
    points = point_hit.shape[0]
    hits_all = hits * ndev * 1.0
    points_all = points * ndev * 1.0
    f32 = jnp.float32
    core = phi_size
    plane = [1, 2 * phi_size]
    others = [b for b in bits_of(ndev) if b != core and b not in plane]

    def swap(x, mask):
        return lax.ppermute(x, AXES, [(i, i ^ mask) for i in range(ndev)])

    sizes = (layer_size, phi_size)
    track = track.reshape(1, hits)
    noise = noise.reshape(1, hits)
    low = jnp.bfloat16

    pay, aux = pl.pallas_call(
        functools.partial(embed_kernel, sizes),
        out_shape=(
            jax.ShapeDtypeStruct((dim + 8, hits), f32),
            jax.ShapeDtypeStruct((16, hits), f32),
        ),
        in_specs=[HBM] * 8,
        out_specs=(VMEM,) * 2,
        scratch_shapes=[
            pltpu.SMEM((points,), jnp.int32),
            pltpu.VMEM((hits, width), low),
            pltpu.VMEM((layers, width, width), low),
            pltpu.VMEM((layers, width), f32),
            pltpu.VMEM((dim, width), low),
            pltpu.VMEM(w_beta.shape, low),
            pltpu.VMEM((1, hits), jnp.int32),
            pltpu.VMEM((1, hits), jnp.int32),
            pltpu.SemaphoreType.DMA((layers + 7,)),
        ],
        compiler_params=pltpu.CompilerParams(vmem_limit_bytes=EMBED_VMEM),
        name="embed",
    )(point_hit, features, w_layers, b_layers, w_coord, w_beta, track, noise)

    def residuals(early):
        return pl.pallas_call(
            residual_kernel,
            out_shape=(
                jax.ShapeDtypeStruct((layers, hits, width), f32),
                jax.ShapeDtypeStruct((layers, width, hits), low),
                jax.ShapeDtypeStruct((hits, width), low),
                jax.ShapeDtypeStruct((layers - 1, width, width), low),
                jax.ShapeDtypeStruct((2 * dim, width), low),
            ),
            in_specs=[VMEM] * 5,
            out_specs=(VMEM,) * 5,
            compiler_params=PARAMS,
            cost_estimate=pl.CostEstimate(
                flops=20 * layers * hits * width, bytes_accessed=6 * layers * hits * width,
                transcendentals=layers * hits * width,
            ),
            name="residuals",
        )(*early)

    pay_own, own, xb, yb = pl.pallas_call(
        spread_kernel,
        out_shape=(
            jax.ShapeDtypeStruct((dim + 8, hits), f32),
            jax.ShapeDtypeStruct((8, 128), f32),
            jax.ShapeDtypeStruct((dim, 8, hits), f32),
            jax.ShapeDtypeStruct((dim, 8, hits), f32),
        ),
        in_specs=[VMEM],
        out_specs=(VMEM,) * 4,
        compiler_params=PARAMS,
        cost_estimate=pl.CostEstimate(flops=0, bytes_accessed=80 * dim * hits, transcendentals=0),
        name="spread",
    )(pay)
    rows_all = pay[None]
    kept = pay_own[None]
    stages = [others[i : i + 2] for i in range(0, len(others), 2)] + [plane]
    for stage in stages:
        masks = stage + ([stage[0] ^ stage[1]] if len(stage) > 1 else [])
        if stage is plane:
            rows_all, *early = lax.optimization_barrier((rows_all, features, w_layers, b_layers))
            kept = rows_all
        arrived = [swap(rows_all, m) for m in masks]
        kept = rows_all = jnp.concatenate([kept] + arrived, 0)
    slope, ht, last, wt, head = residuals(early + [w_coord, w_beta])
    rows_all, slope = lax.optimization_barrier((rows_all, slope))
    rows_far = swap(rows_all, core)

    partial_sums = (
        jax.ShapeDtypeStruct((dim + 1, 8, hits), f32),
        jax.ShapeDtypeStruct((dim + 1, 8, 128), f32),
    )
    hit_sums, point_sums = pl.pallas_call(
        near_kernel,
        out_shape=partial_sums,
        in_specs=[VMEM] * 5,
        out_specs=(VMEM, VMEM),
        compiler_params=PARAMS,
        cost_estimate=pl.CostEstimate(
            flops=200 * points * hits * ndev, bytes_accessed=ndev * hits * 64,
            transcendentals=2 * points * hits * ndev,
        ),
        name="near_pairs",
    )(pay_own, own, xb, yb, rows_all)

    blocks = 8
    block_rows = 2 * (layers * width // blocks) + 8
    half = jax.ShapeDtypeStruct((blocks // 2, block_rows, 128), f32)
    keep, send = pl.pallas_call(
        functools.partial(backward_kernel, sizes, hits_all, points_all),
        out_shape=(half, half),
        in_specs=[VMEM] * 13,
        out_specs=(VMEM, VMEM),
        scratch_shapes=[
            pltpu.VMEM((dim, hits), f32),
            pltpu.VMEM((blocks, block_rows, 128), f32),
            pltpu.VMEM((8 * blocks, 128), f32),
        ],
        compiler_params=PARAMS,
        name="pairs_backward",
    )(pay_own, own, xb, yb, aux, slope, ht, last, wt, head, rows_far, hit_sums, point_sums)

    total = keep + swap(send, core)
    masks = [plane[0], plane[1], plane[0] ^ plane[1]]
    mine = total[0]
    arrived = [swap(total[r + 1], m) for r, m in enumerate(masks)]
    mine = (mine + arrived[0]) + (arrived[1] + arrived[2])
    for m in others:
        mine = mine + swap(mine, m)
    quarter = [mine] + [swap(mine, m) for m in masks]
    far = swap(jnp.stack(quarter), core)

    weights = jax.ShapeDtypeStruct((blocks, layers * width // blocks, width), f32)
    gw, near_ext = pl.pallas_call(
        functools.partial(place_near_kernel, sizes),
        out_shape=(weights, jax.ShapeDtypeStruct((blocks // 2, 8, 128), f32)),
        in_specs=[VMEM] * 4,
        out_specs=(HBM, VMEM),
        scratch_shapes=[pltpu.SemaphoreType.DMA((blocks,))],
        compiler_params=PARAMS,
        cost_estimate=pl.CostEstimate(flops=0, bytes_accessed=4 * layers * width * width, transcendentals=0),
        name="place_near",
    )(*quarter)
    gw, gb, gc, gbeta, loss = pl.pallas_call(
        functools.partial(place_far_kernel, sizes),
        out_shape=(
            weights,
            jax.ShapeDtypeStruct((layers, width), f32),
            jax.ShapeDtypeStruct((dim, width), f32),
            jax.ShapeDtypeStruct((1, width), f32),
            jax.ShapeDtypeStruct((1, 1), f32),
        ),
        in_specs=[VMEM, VMEM, HBM],
        out_specs=(HBM,) * 5,
        scratch_shapes=[
            pltpu.VMEM((layers, width), f32),
            pltpu.VMEM((dim, width), f32),
            pltpu.VMEM((1, width), f32),
            pltpu.VMEM((1, 1), f32),
            pltpu.VMEM((blocks, 8, 128), f32),
            pltpu.SemaphoreType.DMA((blocks,)),
            pltpu.SemaphoreType.DMA((4,)),
        ],
        input_output_aliases={2: 0},
        compiler_params=PARAMS,
        name="place_far",
    )(far, near_ext, gw)
    return (
        gw.reshape(layers, width, width),
        gb,
        gc,
        gbeta.reshape(width),
        loss.reshape(()),
    )


def solution(mesh):
    split = P(AXES)
    return jax.shard_map(
        functools.partial(on_device, mesh.shape["layer"], mesh.shape["phi"]),
        mesh=mesh,
        in_specs=(P(AXES, None), P(), P(), P(), P(), split, split, split),
        out_specs=(P(), P(), P(), P(), P()),
        check_vma=False,
    )
```

```python
import functools

import jax
import jax.numpy as jnp
from jax import lax
from jax.experimental import pallas as pl
from jax.experimental.pallas import tpu as pltpu
from jax.sharding import PartitionSpec as P

dist_eps = 0.0001
charge_floor = 0.5
AXES = ("layer", "phi")
VMEM = pl.BlockSpec(memory_space=pltpu.VMEM)
HBM = pl.BlockSpec(memory_space=pltpu.HBM)
UNROLL = 4
EMBED_VMEM = 63400000
HIGH = lax.Precision.HIGHEST
PARAMS = pltpu.CompilerParams(vmem_limit_bytes=48 * 1024 * 1024)


def matmul(a, b, ca=1, cb=0, precision=None):
    return lax.dot_general(
        a, b, (((ca,), (cb,)), ((), ())), precision=precision, preferred_element_type=jnp.float32
    )


def iota(shape, dim):
    return lax.broadcasted_iota(jnp.int32, shape, dim)


def head_rows(wc_ref, wb_ref):
    dim = wc_ref.shape[0]
    width = wc_ref.shape[1]
    beta_row = jnp.broadcast_to(wb_ref[...].astype(jnp.float32).reshape(1, width), (dim, width))
    tail = jnp.where(iota((dim, width), 0) == 0, beta_row, 0.0).astype(jnp.bfloat16)
    return jnp.concatenate([wc_ref[...], tail], 0)


def flat_index(axis_sizes):
    return lax.axis_index("layer") * axis_sizes[1] + lax.axis_index("phi")


def block_index(axis_sizes):
    me = flat_index(axis_sizes)
    core = lax.shift_right_logical(me, axis_sizes[1].bit_length() - 1) & 1
    upper = lax.shift_right_logical(me, axis_sizes[1].bit_length()) & 1
    return core * 4 + upper * 2 + (me & 1)


def embed_kernel(
    sizes,
    hit_hbm, feat_hbm, w_hbm, b_hbm, wc_hbm, wb_hbm, track_hbm, noise_hbm,
    pay_ref, aux_ref,
    hit_ref, feat_ref, w_ref, b_ref, wc_ref, wb_ref, track_ref, noise_ref, sems,
):
    dim = wc_ref.shape[0]
    hits = feat_ref.shape[0]
    points = hit_ref.shape[0]
    layers = w_ref.shape[0]
    pairs = [(feat_hbm, feat_ref)] + [(w_hbm.at[l], w_ref.at[l]) for l in range(layers)]
    pairs = pairs[:2] + [(b_hbm, b_ref)] + pairs[2:]
    pairs += [(wc_hbm, wc_ref), (wb_hbm, wb_ref), (track_hbm, track_ref)]
    pairs += [(noise_hbm, noise_ref), (hit_hbm, hit_ref)]
    copies = [
        pltpu.make_async_copy(src, dst, sems.at[i]) for i, (src, dst) in enumerate(pairs)
    ]
    for copy in copies:
        copy.start()
    for copy in copies[:3]:
        copy.wait()
    h = feat_ref[...]
    for l in range(layers):
        if l > 0:
            copies[l + 2].wait()
        a = matmul(h, w_ref[l]) + b_ref[l : l + 1, :]
        h = (a * jax.nn.sigmoid(a)).astype(jnp.bfloat16)
    for copy in copies[layers + 2 :]:
        copy.wait()
    xz = matmul(head_rows(wc_ref, wb_ref), h, 1, 1)
    z = xz[dim : dim + 1]
    expz = jnp.exp(z)
    spread = jnp.log1p(2.0 * expz)
    q = 0.25 * spread * spread + charge_floor
    slope = 0.5 * spread * (2.0 * expz / (1.0 + 2.0 * expz))
    beta = jax.nn.sigmoid(z)
    noise = noise_ref[...]
    label = jnp.where(noise == 0, track_ref[...], -1).astype(jnp.float32)
    rows8 = iota((8, hits), 0)
    aux_ref[0:8, :] = jnp.where(
        rows8 == 0, beta, jnp.where(rows8 == 1, slope, noise.astype(jnp.float32))
    )
    col = jnp.zeros((points, hits), jnp.int32)
    for p in range(points):
        col = jnp.where(rows8 == (p + 2) % points, hit_ref[p], col)
    sel = iota((points, hits), 1) == col
    aux_ref[8:16, :] = jnp.where(sel, 1.0, 0.0)
    lane = iota((points, 128), 1)
    row = iota((points, 128), 0)
    order = jnp.where(row < 2, row + points - 2, row - 2)
    pts = jnp.where(lane == dim + 1, (flat_index(sizes) * points + order).astype(jnp.float32), 0.0)
    for c in range(dim):
        v = jnp.sum(jnp.where(sel, xz[c : c + 1], 0.0), axis=1, keepdims=True)
        pts = jnp.where(lane == c, v, pts)
    v = jnp.sum(jnp.where(sel, q, 0.0), axis=1, keepdims=True)
    pts = jnp.where(lane == dim, v, pts)
    moved = pltpu.roll(pts, 2, 0)
    left = jnp.where(row == 0, q[:, :128], jnp.where(row == 1, label[:, :128], pts))
    right = jnp.where(row == 0, q[:, 128:], jnp.where(row == 1, label[:, 128:], moved))
    pay_ref[0:dim, :] = xz[0:dim]
    pay_ref[dim : dim + 8, 0:128] = left
    pay_ref[dim : dim + 8, 128:256] = right


def residual_kernel(
    feat_ref, w_ref, b_ref, wc_ref, wb_ref, slope_ref, ht_ref, last_ref, wt_ref, head_ref
):
    head_ref[...] = head_rows(wc_ref, wb_ref)
    layers = w_ref.shape[0]
    h = feat_ref[...]
    ht_ref[0] = h.T
    for l in range(layers):
        a = matmul(h, w_ref[l]) + b_ref[l : l + 1, :]
        sig = jax.nn.sigmoid(a)
        slope_ref[l] = sig * (1.0 + a * (1.0 - sig))
        h = (a * sig).astype(jnp.bfloat16)
        if l < layers - 1:
            ht_ref[l + 1] = h.T
            wt_ref[l] = w_ref[l + 1].T
        else:
            last_ref[...] = h


def point_tile(left, right):
    rows = iota(left.shape, 0)
    return jnp.where(rows < 2, pltpu.roll(right, 6, 0), left)


def pair_weights(dist_sq, match):
    shifted = dist_sq + dist_eps
    inv = lax.rsqrt(shifted)
    reach = jnp.maximum(1.0 - shifted * inv, 0.0)
    potential = jnp.where(match, dist_sq, reach * reach)
    weight = jnp.where(match, 2.0, -2.0 * jnp.maximum(inv - 1.0, 0.0))
    return potential, weight


def spread_kernel(pay_ref, copy_ref, own_ref, xb, yb):
    dim = xb.shape[0]
    full = xb.shape[1:]
    copy_ref[...] = pay_ref[...]
    own = pay_ref[dim : dim + 8, :]
    own = point_tile(own[:, :128], own[:, 128:])
    own_ref[...] = own
    for c in range(dim):
        xb[c] = jnp.broadcast_to(pay_ref[c : c + 1, :], full)
        yb[c] = jnp.broadcast_to(own[:, c : c + 1], full)


def pair_sums(pay_ref, own, ref, xb, yb, hit_acc, point_acc):
    dim = xb.shape[0]
    full = xb.shape[1:]
    label_b = jnp.broadcast_to(pay_ref[dim + 1 : dim + 2, :], full)
    index_b = jnp.broadcast_to(own[:, dim + 1 : dim + 2], full)
    zero = jnp.zeros(full, jnp.float32)

    def hit_side(j, acc):
        tile = ref[j, dim : dim + 8, :]
        tile = point_tile(tile[:, :128], tile[:, 128:])
        diffs = []
        dist_sq = zero
        for c in range(dim):
            diff = xb[c] - tile[:, c : c + 1]
            diffs.append(diff)
            dist_sq = dist_sq + diff * diff
        point_q = tile[:, dim : dim + 1]
        potential, weight = pair_weights(dist_sq, label_b == tile[:, dim + 1 : dim + 2])
        weight = weight * point_q
        terms = [weight * diff for diff in diffs] + [potential * point_q]
        return tuple(s + term for s, term in zip(acc, terms))

    def point_side(j, acc):
        diffs = []
        dist_sq = zero
        for c in range(dim):
            diff = yb[c] - ref[j, c : c + 1, :]
            diffs.append(diff)
            dist_sq = dist_sq + diff * diff
        hit_q = ref[j, dim : dim + 1, :]
        potential, weight = pair_weights(dist_sq, index_b == ref[j, dim + 1 : dim + 2, :])
        weight = weight * hit_q
        terms = [weight * diff for diff in diffs] + [potential * hit_q]
        return tuple(s + term[:, :128] + term[:, 128:] for s, term in zip(acc, terms))

    hit_acc = lax.fori_loop(0, ref.shape[0], hit_side, hit_acc, unroll=UNROLL)
    point_acc = lax.fori_loop(0, ref.shape[0], point_side, point_acc, unroll=UNROLL)
    return hit_acc, point_acc


def near_kernel(pay_ref, own_ref, xb, yb, rows_ref, hit_ref, point_ref):
    dim = xb.shape[0]
    own = own_ref[...]
    hit_acc = (jnp.zeros(hit_ref.shape[1:], jnp.float32),) * (dim + 1)
    point_acc = (jnp.zeros(point_ref.shape[1:], jnp.float32),) * (dim + 1)
    hit_acc, point_acc = pair_sums(pay_ref, own, rows_ref, xb, yb, hit_acc, point_acc)
    for c in range(dim + 1):
        hit_ref[c] = hit_acc[c]
        point_ref[c] = point_acc[c]


def backward_kernel(
    sizes, hits_all, points_all,
    pay_ref, own_ref, xb, yb, aux_ref, slope_ref, ht_ref, last_ref, wt_ref, head_ref, rows_ref, hit_ref, point_ref,
    keep_ref, send_ref, gx_ref, stack, ext,
):
    dim = xb.shape[0]
    hits = pay_ref.shape[1]
    layers = slope_ref.shape[0]
    points = own_ref.shape[0]
    own = own_ref[...]
    q_row = pay_ref[dim : dim + 1, :]
    hit_acc = tuple(hit_ref[c] for c in range(dim + 1))
    point_acc = tuple(point_ref[c] for c in range(dim + 1))
    hit_acc, point_acc = pair_sums(pay_ref, own, rows_ref, xb, yb, hit_acc, point_acc)

    pot_row = jnp.sum(hit_acc[dim], axis=0, keepdims=True)
    scaled = q_row * (1.0 / hits_all)
    for c in range(dim):
        gx_ref[c : c + 1, :] = jnp.sum(hit_acc[c], axis=0, keepdims=True) * scaled
    lane = iota((8, 128), 1)
    own_q = own[:, dim : dim + 1] * (1.0 / hits_all)
    grads = jnp.where(lane == dim + 1, 1.0, 0.0)
    for c in range(dim):
        v = jnp.sum(point_acc[c], axis=1, keepdims=True) * own_q
        grads = jnp.where(lane == c, v, grads)
    v = jnp.sum(point_acc[dim], axis=1, keepdims=True) * (1.0 / hits_all)
    grads = jnp.where(lane == dim, v, grads)
    added = matmul(grads, aux_ref[8:16, :], 0, 0, HIGH)

    beta = aux_ref[0:1, :]
    noise = aux_ref[2:3, :]
    count = added[dim + 1 : dim + 2]
    grad_q = pot_row * (1.0 / hits_all) + added[dim : dim + 1]
    grad_b = noise * (1.0 / hits_all) - count * (1.0 / points_all)
    grad_z = grad_q * aux_ref[1:2, :] + grad_b * beta * (1.0 - beta)
    per_hit = q_row * pot_row * (1.0 / hits_all) + noise * beta * (1.0 / hits_all)
    per_hit = per_hit - count * beta * (1.0 / points_all)
    loss = jnp.sum(per_hit, axis=1, keepdims=True) + points * 1.0 / points_all

    grad_x = gx_ref[...] + added[0:dim]
    tail = jnp.where(iota((dim, hits), 0) == 0, grad_z, 0.0)
    low = jnp.concatenate([grad_x, tail], 0).astype(jnp.bfloat16)
    head = head_ref[...]
    grad_head = matmul(low, last_ref[...])
    up = matmul(low, head, 0, 0)
    ext[...] = jnp.zeros(ext.shape, jnp.float32)
    cols = [slice(0, 128), slice(128, 256)]
    base = 2 * layers
    for h, col in enumerate(cols):
        ext[base + h * dim : base + (h + 1) * dim, :] = grad_head[0:dim, col]
        ext[base + 2 * dim + h : base + 2 * dim + h + 1, :] = grad_head[dim : dim + 1, col]
    ext[base + 2 * dim + 2 : base + 2 * dim + 3, :] = jnp.broadcast_to(loss, (1, 128))
    blocks = stack.shape[0]
    rows = layers * hits // blocks
    per_layer = blocks // layers
    for l in range(layers - 1, -1, -1):
        err = (up * slope_ref[l]).astype(jnp.bfloat16)
        if l > 0:
            up = matmul(err, wt_ref[l - 1])
        grad_w = matmul(ht_ref[l], err)
        bias = jnp.sum(err.astype(jnp.float32), axis=0, keepdims=True)
        for h, col in enumerate(cols):
            ext[h * layers + l : h * layers + l + 1, :] = bias[:, col]
            for s in range(per_layer):
                stack[l * per_layer + s, h * rows : (h + 1) * rows, :] = grad_w[
                    s * rows : (s + 1) * rows, col
                ]
    for b in range(blocks):
        stack[b, 2 * rows : 2 * rows + 8, :] = ext[8 * b : 8 * b + 8, :]
    me = block_index(sizes)
    for j in range(blocks // 2):
        keep_ref[j] = stack[jnp.bitwise_xor(me, j)]
        send_ref[j] = stack[jnp.bitwise_xor(me, j + blocks // 2)]


def place_copies(sizes, blocks, first, gw_ref, sems):
    rows = gw_ref.shape[1]
    me = block_index(sizes)
    copies = []
    for r, block in enumerate(blocks):
        place = jnp.bitwise_xor(me, first + r)
        for h in range(2):
            copies.append(
                pltpu.make_async_copy(
                    block.at[pl.ds(h * rows, rows)],
                    gw_ref.at[place, :, pl.ds(h * 128, 128)],
                    sems.at[2 * r + h],
                )
            )
    for copy in copies:
        copy.start()
    return copies


def place_near_kernel(sizes, *refs):
    blocks = refs[:4]
    gw_ref, ext_ref, sems = refs[4:]
    rows = gw_ref.shape[1]
    copies = place_copies(sizes, blocks, 0, gw_ref, sems)
    for r, block in enumerate(blocks):
        ext_ref[r] = block[2 * rows :, :]
    for copy in copies:
        copy.wait()


def place_far_kernel(
    sizes, far_ref, near_ref, gw_in, gw_ref, *rest
):
    outs, scratch, (ext, sems, small_sems) = rest[:4], rest[4:8], rest[8:]
    gb_ref, gc_ref, gbeta_ref, loss_ref = scratch
    rows = gw_ref.shape[1]
    half = far_ref.shape[0]
    dim = gc_ref.shape[0]
    layers = gb_ref.shape[0]
    blocks = [far_ref.at[r] for r in range(half)]
    copies = place_copies(sizes, blocks, half, gw_ref, sems)
    me = block_index(sizes)
    for r in range(half):
        ext[jnp.bitwise_xor(me, r)] = near_ref[r]
        ext[jnp.bitwise_xor(me, half + r)] = far_ref[r, 2 * rows :, :]
    flat = jnp.concatenate([ext[b] for b in range(2 * half)], 0)
    base = 2 * layers
    for h, col in enumerate([slice(0, 128), slice(128, 256)]):
        gb_ref[:, col] = flat[h * layers : (h + 1) * layers]
        gc_ref[:, col] = flat[base + h * dim : base + (h + 1) * dim]
        gbeta_ref[:, col] = flat[base + 2 * dim + h : base + 2 * dim + h + 1]
    loss_ref[...] = flat[base + 2 * dim + 2 : base + 2 * dim + 3, 0:1]
    for i in range(4):
        copies.append(pltpu.make_async_copy(scratch[i], outs[i], small_sems.at[i]))
        copies[-1].start()
    for copy in copies:
        copy.wait()


def bits_of(size):
    return [1 << t for t in range(size.bit_length() - 1)]


def on_device(layer_size, phi_size, features, w_layers, b_layers, w_coord, w_beta, point_hit, track, noise):
    ndev = layer_size * phi_size
    hits, width = features.shape
    layers = w_layers.shape[0]
    dim = w_coord.shape[0]
    points = point_hit.shape[0]
    hits_all = hits * ndev * 1.0
    points_all = points * ndev * 1.0
    f32 = jnp.float32
    core = phi_size
    plane = [1, 2 * phi_size]
    others = [b for b in bits_of(ndev) if b != core and b not in plane]

    def swap(x, mask):
        return lax.ppermute(x, AXES, [(i, i ^ mask) for i in range(ndev)])

    sizes = (layer_size, phi_size)
    track = track.reshape(1, hits)
    noise = noise.reshape(1, hits)
    low = jnp.bfloat16

    pay, aux = pl.pallas_call(
        functools.partial(embed_kernel, sizes),
        out_shape=(
            jax.ShapeDtypeStruct((dim + 8, hits), f32),
            jax.ShapeDtypeStruct((16, hits), f32),
        ),
        in_specs=[HBM] * 8,
        out_specs=(VMEM,) * 2,
        scratch_shapes=[
            pltpu.SMEM((points,), jnp.int32),
            pltpu.VMEM((hits, width), low),
            pltpu.VMEM((layers, width, width), low),
            pltpu.VMEM((layers, width), f32),
            pltpu.VMEM((dim, width), low),
            pltpu.VMEM(w_beta.shape, low),
            pltpu.VMEM((1, hits), jnp.int32),
            pltpu.VMEM((1, hits), jnp.int32),
            pltpu.SemaphoreType.DMA((layers + 7,)),
        ],
        compiler_params=pltpu.CompilerParams(vmem_limit_bytes=EMBED_VMEM),
        name="embed",
    )(point_hit, features, w_layers, b_layers, w_coord, w_beta, track, noise)

    def residuals(early):
        return pl.pallas_call(
            residual_kernel,
            out_shape=(
                jax.ShapeDtypeStruct((layers, hits, width), f32),
                jax.ShapeDtypeStruct((layers, width, hits), low),
                jax.ShapeDtypeStruct((hits, width), low),
                jax.ShapeDtypeStruct((layers - 1, width, width), low),
                jax.ShapeDtypeStruct((2 * dim, width), low),
            ),
            in_specs=[VMEM] * 5,
            out_specs=(VMEM,) * 5,
            compiler_params=PARAMS,
            cost_estimate=pl.CostEstimate(
                flops=20 * layers * hits * width, bytes_accessed=6 * layers * hits * width,
                transcendentals=layers * hits * width,
            ),
            name="residuals",
        )(*early)

    pay_own, own, xb, yb = pl.pallas_call(
        spread_kernel,
        out_shape=(
            jax.ShapeDtypeStruct((dim + 8, hits), f32),
            jax.ShapeDtypeStruct((8, 128), f32),
            jax.ShapeDtypeStruct((dim, 8, hits), f32),
            jax.ShapeDtypeStruct((dim, 8, hits), f32),
        ),
        in_specs=[VMEM],
        out_specs=(VMEM,) * 4,
        compiler_params=PARAMS,
        cost_estimate=pl.CostEstimate(flops=0, bytes_accessed=80 * dim * hits, transcendentals=0),
        name="spread",
    )(pay)
    rows_all = pay[None]
    kept = pay_own[None]
    stages = [others[i : i + 2] for i in range(0, len(others), 2)] + [plane]
    for stage in stages:
        masks = stage[:1] + ([stage[0] ^ stage[1]] if len(stage) > 1 else []) + stage[1:]
        if stage is plane:
            rows_all, *early = lax.optimization_barrier((rows_all, features, w_layers, b_layers))
            kept = rows_all
        arrived = [swap(rows_all, m) for m in masks]
        kept = rows_all = jnp.concatenate([kept] + arrived, 0)
    slope, ht, last, wt, head = residuals(early + [w_coord, w_beta])
    rows_all, slope = lax.optimization_barrier((rows_all, slope))
    rows_far = swap(rows_all, core)

    partial_sums = (
        jax.ShapeDtypeStruct((dim + 1, 8, hits), f32),
        jax.ShapeDtypeStruct((dim + 1, 8, 128), f32),
    )
    hit_sums, point_sums = pl.pallas_call(
        near_kernel,
        out_shape=partial_sums,
        in_specs=[VMEM] * 5,
        out_specs=(VMEM, VMEM),
        compiler_params=PARAMS,
        cost_estimate=pl.CostEstimate(
            flops=200 * points * hits * ndev, bytes_accessed=ndev * hits * 64,
            transcendentals=2 * points * hits * ndev,
        ),
        name="near_pairs",
    )(pay_own, own, xb, yb, rows_all)

    blocks = 8
    block_rows = 2 * (layers * width // blocks) + 8
    half = jax.ShapeDtypeStruct((blocks // 2, block_rows, 128), f32)
    keep, send = pl.pallas_call(
        functools.partial(backward_kernel, sizes, hits_all, points_all),
        out_shape=(half, half),
        in_specs=[VMEM] * 13,
        out_specs=(VMEM, VMEM),
        scratch_shapes=[
            pltpu.VMEM((dim, hits), f32),
            pltpu.VMEM((blocks, block_rows, 128), f32),
            pltpu.VMEM((8 * blocks, 128), f32),
        ],
        compiler_params=PARAMS,
        name="pairs_backward",
    )(pay_own, own, xb, yb, aux, slope, ht, last, wt, head, rows_far, hit_sums, point_sums)

    total = keep + swap(send, core)
    masks = [plane[0], plane[1], plane[0] ^ plane[1]]
    mine = total[0]
    arrived = [swap(total[r + 1], masks[r]) for r in (2, 1, 0)]
    mine = (mine + arrived[2]) + (arrived[1] + arrived[0])
    for i, m in enumerate(others):
        mine = mine + swap(mine, m ^ others[0] if i > 0 else m)
    quarter = [swap(mine, masks[r]) for r in (2, 1, 0)] + [mine]
    quarter = quarter[::-1]
    far = swap(jnp.stack(quarter), core)

    weights = jax.ShapeDtypeStruct((blocks, layers * width // blocks, width), f32)
    gw, near_ext = pl.pallas_call(
        functools.partial(place_near_kernel, sizes),
        out_shape=(weights, jax.ShapeDtypeStruct((blocks // 2, 8, 128), f32)),
        in_specs=[VMEM] * 4,
        out_specs=(HBM, VMEM),
        scratch_shapes=[pltpu.SemaphoreType.DMA((blocks,))],
        compiler_params=PARAMS,
        cost_estimate=pl.CostEstimate(flops=0, bytes_accessed=4 * layers * width * width, transcendentals=0),
        name="place_near",
    )(*quarter)
    gw, gb, gc, gbeta, loss = pl.pallas_call(
        functools.partial(place_far_kernel, sizes),
        out_shape=(
            weights,
            jax.ShapeDtypeStruct((layers, width), f32),
            jax.ShapeDtypeStruct((dim, width), f32),
            jax.ShapeDtypeStruct((1, width), f32),
            jax.ShapeDtypeStruct((1, 1), f32),
        ),
        in_specs=[VMEM, VMEM, HBM],
        out_specs=(HBM,) * 5,
        scratch_shapes=[
            pltpu.VMEM((layers, width), f32),
            pltpu.VMEM((dim, width), f32),
            pltpu.VMEM((1, width), f32),
            pltpu.VMEM((1, 1), f32),
            pltpu.VMEM((blocks, 8, 128), f32),
            pltpu.SemaphoreType.DMA((blocks,)),
            pltpu.SemaphoreType.DMA((4,)),
        ],
        input_output_aliases={2: 0},
        compiler_params=PARAMS,
        name="place_far",
    )(far, near_ext, gw)
    return (
        gw.reshape(layers, width, width),
        gb,
        gc,
        gbeta.reshape(width),
        loss.reshape(()),
    )


def solution(mesh):
    split = P(AXES)
    return jax.shard_map(
        functools.partial(on_device, mesh.shape["layer"], mesh.shape["phi"]),
        mesh=mesh,
        in_specs=(P(AXES, None), P(), P(), P(), P(), split, split, split),
        out_specs=(P(), P(), P(), P(), P()),
        check_vma=False,
    )
```

```python
import functools

import jax
import jax.numpy as jnp
from jax import lax
from jax.experimental import pallas as pl
from jax.experimental.pallas import tpu as pltpu
from jax.sharding import PartitionSpec as P

dist_eps = 0.0001
charge_floor = 0.5
AXES = ("layer", "phi")
VMEM = pl.BlockSpec(memory_space=pltpu.VMEM)
HBM = pl.BlockSpec(memory_space=pltpu.HBM)
UNROLL = 16
EMBED_VMEM = 63400000
HIGH = lax.Precision.HIGHEST
PARAMS = pltpu.CompilerParams(vmem_limit_bytes=48 * 1024 * 1024)


def matmul(a, b, ca=1, cb=0, precision=None):
    return lax.dot_general(
        a, b, (((ca,), (cb,)), ((), ())), precision=precision, preferred_element_type=jnp.float32
    )


def iota(shape, dim):
    return lax.broadcasted_iota(jnp.int32, shape, dim)


def head_rows(wc_ref, wb_ref):
    dim = wc_ref.shape[0]
    width = wc_ref.shape[1]
    beta_row = jnp.broadcast_to(wb_ref[...].astype(jnp.float32).reshape(1, width), (dim, width))
    tail = jnp.where(iota((dim, width), 0) == 0, beta_row, 0.0).astype(jnp.bfloat16)
    return jnp.concatenate([wc_ref[...], tail], 0)


def flat_index(axis_sizes):
    return lax.axis_index("layer") * axis_sizes[1] + lax.axis_index("phi")


def block_places(axis_sizes):
    me = flat_index(axis_sizes)
    shift = axis_sizes[1].bit_length() - 1
    core = lax.shift_right_logical(me, shift) & 1
    flat = (lax.shift_right_logical(me, shift + 1) & 1) * 2 + (me & 1)
    line = lax.shift_right_logical(me, 1) & 3
    mine = flat + core * (line - flat)
    return (core * 4, mine), (4 - core * 4, flat + line - mine)


def embed_kernel(
    sizes,
    hit_hbm, feat_hbm, w_hbm, b_hbm, wc_hbm, wb_hbm, track_hbm, noise_hbm,
    pay_ref, aux_ref,
    hit_ref, feat_ref, w_ref, b_ref, wc_ref, wb_ref, track_ref, noise_ref, sems,
):
    dim = wc_ref.shape[0]
    hits = feat_ref.shape[0]
    points = hit_ref.shape[0]
    layers = w_ref.shape[0]
    pairs = [(feat_hbm, feat_ref)] + [(w_hbm.at[l], w_ref.at[l]) for l in range(layers)]
    pairs = pairs[:2] + [(b_hbm, b_ref)] + pairs[2:]
    pairs += [(wc_hbm, wc_ref), (wb_hbm, wb_ref), (track_hbm, track_ref)]
    pairs += [(noise_hbm, noise_ref), (hit_hbm, hit_ref)]
    copies = [
        pltpu.make_async_copy(src, dst, sems.at[i]) for i, (src, dst) in enumerate(pairs)
    ]
    for copy in copies:
        copy.start()
    for copy in copies[:3]:
        copy.wait()
    h = feat_ref[...]
    for l in range(layers):
        if l > 0:
            copies[l + 2].wait()
        a = matmul(h, w_ref[l]) + b_ref[l : l + 1, :]
        h = (a * jax.nn.sigmoid(a)).astype(jnp.bfloat16)
    for copy in copies[layers + 2 :]:
        copy.wait()
    xz = matmul(head_rows(wc_ref, wb_ref), h, 1, 1)
    z = xz[dim : dim + 1]
    expz = jnp.exp(z)
    spread = jnp.log1p(2.0 * expz)
    q = 0.25 * spread * spread + charge_floor
    slope = 0.5 * spread * (2.0 * expz / (1.0 + 2.0 * expz))
    beta = jax.nn.sigmoid(z)
    noise = noise_ref[...]
    label = jnp.where(noise == 0, track_ref[...], -1).astype(jnp.float32)
    rows8 = iota((8, hits), 0)
    aux_ref[0:8, :] = jnp.where(
        rows8 == 0, beta, jnp.where(rows8 == 1, slope, noise.astype(jnp.float32))
    )
    col = jnp.zeros((points, hits), jnp.int32)
    for p in range(points):
        col = jnp.where(rows8 == (p + 2) % points, hit_ref[p], col)
    sel = iota((points, hits), 1) == col
    aux_ref[8:16, :] = jnp.where(sel, 1.0, 0.0)
    lane = iota((points, 128), 1)
    row = iota((points, 128), 0)
    order = jnp.where(row < 2, row + points - 2, row - 2)
    pts = jnp.where(lane == dim + 1, (flat_index(sizes) * points + order).astype(jnp.float32), 0.0)
    for c in range(dim):
        v = jnp.sum(jnp.where(sel, xz[c : c + 1], 0.0), axis=1, keepdims=True)
        pts = jnp.where(lane == c, v, pts)
    v = jnp.sum(jnp.where(sel, q, 0.0), axis=1, keepdims=True)
    pts = jnp.where(lane == dim, v, pts)
    moved = pltpu.roll(pts, 2, 0)
    left = jnp.where(row == 0, q[:, :128], jnp.where(row == 1, label[:, :128], pts))
    right = jnp.where(row == 0, q[:, 128:], jnp.where(row == 1, label[:, 128:], moved))
    pay_ref[0:dim, :] = xz[0:dim]
    pay_ref[dim : dim + 8, 0:128] = left
    pay_ref[dim : dim + 8, 128:256] = right


def residual_kernel(
    feat_ref, w_ref, b_ref, wc_ref, wb_ref, slope_ref, ht_ref, last_ref, wt_ref, head_ref
):
    head_ref[...] = head_rows(wc_ref, wb_ref)
    layers = w_ref.shape[0]
    h = feat_ref[...]
    ht_ref[0] = h.T
    for l in range(layers):
        a = matmul(h, w_ref[l]) + b_ref[l : l + 1, :]
        sig = jax.nn.sigmoid(a)
        slope_ref[l] = sig * (1.0 + a * (1.0 - sig))
        h = (a * sig).astype(jnp.bfloat16)
        if l < layers - 1:
            ht_ref[l + 1] = h.T
            wt_ref[l] = w_ref[l + 1].T
        else:
            last_ref[...] = h


def point_tile(left, right):
    rows = iota(left.shape, 0)
    return jnp.where(rows < 2, pltpu.roll(right, 6, 0), left)


def pair_weights(dist_sq, match):
    shifted = dist_sq + dist_eps
    inv = lax.rsqrt(shifted)
    reach = jnp.maximum(1.0 - shifted * inv, 0.0)
    potential = jnp.where(match, dist_sq, reach * reach)
    weight = jnp.where(match, 2.0, -2.0 * jnp.maximum(inv - 1.0, 0.0))
    return potential, weight


def spread_kernel(pay_ref, copy_ref, own_ref, xb, yb):
    dim = xb.shape[0]
    full = xb.shape[1:]
    copy_ref[...] = pay_ref[...]
    own = pay_ref[dim : dim + 8, :]
    own = point_tile(own[:, :128], own[:, 128:])
    own_ref[...] = own
    for c in range(dim):
        xb[c] = jnp.broadcast_to(pay_ref[c : c + 1, :], full)
        yb[c] = jnp.broadcast_to(own[:, c : c + 1], full)


def pair_sums(pay_ref, own, ref, xb, yb, hit_acc, point_acc):
    dim = xb.shape[0]
    full = xb.shape[1:]
    label_b = jnp.broadcast_to(pay_ref[dim + 1 : dim + 2, :], full)
    index_b = jnp.broadcast_to(own[:, dim + 1 : dim + 2], full)
    zero = jnp.zeros(full, jnp.float32)

    def hit_side(j, acc):
        tile = ref[j, dim : dim + 8, :]
        tile = point_tile(tile[:, :128], tile[:, 128:])
        diffs = []
        dist_sq = zero
        for c in range(dim):
            diff = xb[c] - tile[:, c : c + 1]
            diffs.append(diff)
            dist_sq = dist_sq + diff * diff
        point_q = tile[:, dim : dim + 1]
        potential, weight = pair_weights(dist_sq, label_b == tile[:, dim + 1 : dim + 2])
        weight = weight * point_q
        terms = [weight * diff for diff in diffs] + [potential * point_q]
        return tuple(s + term for s, term in zip(acc, terms))

    def point_side(j, acc):
        diffs = []
        dist_sq = zero
        for c in range(dim):
            diff = yb[c] - ref[j, c : c + 1, :]
            diffs.append(diff)
            dist_sq = dist_sq + diff * diff
        hit_q = ref[j, dim : dim + 1, :]
        potential, weight = pair_weights(dist_sq, index_b == ref[j, dim + 1 : dim + 2, :])
        weight = weight * hit_q
        terms = [weight * diff for diff in diffs] + [potential * hit_q]
        return tuple(s + term[:, :128] + term[:, 128:] for s, term in zip(acc, terms))

    count = ref.shape[0]
    unroll = min(count, UNROLL)
    hit_acc = lax.fori_loop(0, count, hit_side, hit_acc, unroll=unroll)
    point_acc = lax.fori_loop(0, count, point_side, point_acc, unroll=unroll)
    return hit_acc, point_acc


def near_kernel(pay_ref, own_ref, xb, yb, rows_ref, hit_ref, point_ref):
    dim = xb.shape[0]
    own = own_ref[...]
    hit_acc = (jnp.zeros(hit_ref.shape[1:], jnp.float32),) * (dim + 1)
    point_acc = (jnp.zeros(point_ref.shape[1:], jnp.float32),) * (dim + 1)
    hit_acc, point_acc = pair_sums(pay_ref, own, rows_ref, xb, yb, hit_acc, point_acc)
    for c in range(dim + 1):
        hit_ref[c] = hit_acc[c]
        point_ref[c] = point_acc[c]


def backward_kernel(
    sizes, hits_all, points_all,
    pay_ref, own_ref, xb, yb, aux_ref, slope_ref, ht_ref, last_ref, wt_ref, head_ref, rows_ref, hit_ref, point_ref,
    keep_ref, send_ref, gx_ref, stack, ext,
):
    dim = xb.shape[0]
    hits = pay_ref.shape[1]
    layers = slope_ref.shape[0]
    points = own_ref.shape[0]
    own = own_ref[...]
    q_row = pay_ref[dim : dim + 1, :]
    hit_acc = tuple(hit_ref[c] for c in range(dim + 1))
    point_acc = tuple(point_ref[c] for c in range(dim + 1))
    hit_acc, point_acc = pair_sums(pay_ref, own, rows_ref, xb, yb, hit_acc, point_acc)

    pot_row = jnp.sum(hit_acc[dim], axis=0, keepdims=True)
    scaled = q_row * (1.0 / hits_all)
    for c in range(dim):
        gx_ref[c : c + 1, :] = jnp.sum(hit_acc[c], axis=0, keepdims=True) * scaled
    lane = iota((8, 128), 1)
    own_q = own[:, dim : dim + 1] * (1.0 / hits_all)
    grads = jnp.where(lane == dim + 1, 1.0, 0.0)
    for c in range(dim):
        v = jnp.sum(point_acc[c], axis=1, keepdims=True) * own_q
        grads = jnp.where(lane == c, v, grads)
    v = jnp.sum(point_acc[dim], axis=1, keepdims=True) * (1.0 / hits_all)
    grads = jnp.where(lane == dim, v, grads)
    added = matmul(grads, aux_ref[8:16, :], 0, 0, HIGH)

    beta = aux_ref[0:1, :]
    noise = aux_ref[2:3, :]
    count = added[dim + 1 : dim + 2]
    grad_q = pot_row * (1.0 / hits_all) + added[dim : dim + 1]
    grad_b = noise * (1.0 / hits_all) - count * (1.0 / points_all)
    grad_z = grad_q * aux_ref[1:2, :] + grad_b * beta * (1.0 - beta)
    per_hit = q_row * pot_row * (1.0 / hits_all) + noise * beta * (1.0 / hits_all)
    per_hit = per_hit - count * beta * (1.0 / points_all)
    loss = jnp.sum(per_hit, axis=1, keepdims=True) + points * 1.0 / points_all

    grad_x = gx_ref[...] + added[0:dim]
    tail = jnp.where(iota((dim, hits), 0) == 0, grad_z, 0.0)
    low = jnp.concatenate([grad_x, tail], 0).astype(jnp.bfloat16)
    head = head_ref[...]
    grad_head = matmul(low, last_ref[...])
    up = matmul(low, head, 0, 0)
    ext[...] = jnp.zeros(ext.shape, jnp.float32)
    cols = [slice(0, 128), slice(128, 256)]
    base = 2 * layers
    for h, col in enumerate(cols):
        ext[base + h * dim : base + (h + 1) * dim, :] = grad_head[0:dim, col]
        ext[base + 2 * dim + h : base + 2 * dim + h + 1, :] = grad_head[dim : dim + 1, col]
    ext[base + 2 * dim + 2 : base + 2 * dim + 3, :] = jnp.broadcast_to(loss, (1, 128))
    blocks = stack.shape[0]
    rows = layers * hits // blocks
    per_layer = blocks // layers
    for l in range(layers - 1, -1, -1):
        err = (up * slope_ref[l]).astype(jnp.bfloat16)
        if l > 0:
            up = matmul(err, wt_ref[l - 1])
        grad_w = matmul(ht_ref[l], err)
        bias = jnp.sum(err.astype(jnp.float32), axis=0, keepdims=True)
        for h, col in enumerate(cols):
            ext[h * layers + l : h * layers + l + 1, :] = bias[:, col]
            for s in range(per_layer):
                stack[l * per_layer + s, h * rows : (h + 1) * rows, :] = grad_w[
                    s * rows : (s + 1) * rows, col
                ]
    for b in range(blocks):
        stack[b, 2 * rows : 2 * rows + 8, :] = ext[8 * b : 8 * b + 8, :]
    for out_ref, (first, place) in zip((keep_ref, send_ref), block_places(sizes)):
        for j in range(blocks // 2):
            out_ref[j] = stack[first + jnp.bitwise_xor(place, j)]


def place_copies(blocks, first, place, gw_ref, sems):
    rows = gw_ref.shape[1]
    copies = []
    for r, block in enumerate(blocks):
        slot = first + jnp.bitwise_xor(place, r)
        for h in range(2):
            copies.append(
                pltpu.make_async_copy(
                    block.at[pl.ds(h * rows, rows)],
                    gw_ref.at[slot, :, pl.ds(h * 128, 128)],
                    sems.at[2 * r + h],
                )
            )
    for copy in copies:
        copy.start()
    return copies


def place_near_kernel(sizes, *refs):
    blocks = refs[:4]
    gw_ref, ext_ref, sems = refs[4:]
    rows = gw_ref.shape[1]
    copies = place_copies(blocks, *block_places(sizes)[0], gw_ref, sems)
    for r, block in enumerate(blocks):
        ext_ref[r] = block[2 * rows :, :]
    for copy in copies:
        copy.wait()


def place_far_kernel(
    sizes, far_ref, near_ref, gw_in, gw_ref, *rest
):
    outs, scratch, (ext, sems, small_sems) = rest[:4], rest[4:8], rest[8:]
    gb_ref, gc_ref, gbeta_ref, loss_ref = scratch
    rows = gw_ref.shape[1]
    half = far_ref.shape[0]
    dim = gc_ref.shape[0]
    layers = gb_ref.shape[0]
    blocks = [far_ref.at[r] for r in range(half)]
    (near_first, near_place), (far_first, far_place) = block_places(sizes)
    copies = place_copies(blocks, far_first, far_place, gw_ref, sems)
    for r in range(half):
        ext[near_first + jnp.bitwise_xor(near_place, r)] = near_ref[r]
        ext[far_first + jnp.bitwise_xor(far_place, r)] = far_ref[r, 2 * rows :, :]
    flat = jnp.concatenate([ext[b] for b in range(2 * half)], 0)
    base = 2 * layers
    for h, col in enumerate([slice(0, 128), slice(128, 256)]):
        gb_ref[:, col] = flat[h * layers : (h + 1) * layers]
        gc_ref[:, col] = flat[base + h * dim : base + (h + 1) * dim]
        gbeta_ref[:, col] = flat[base + 2 * dim + h : base + 2 * dim + h + 1]
    loss_ref[...] = flat[base + 2 * dim + 2 : base + 2 * dim + 3, 0:1]
    for i in range(4):
        copies.append(pltpu.make_async_copy(scratch[i], outs[i], small_sems.at[i]))
        copies[-1].start()
    for copy in copies:
        copy.wait()


def bits_of(size):
    return [1 << t for t in range(size.bit_length() - 1)]


def on_device(layer_size, phi_size, features, w_layers, b_layers, w_coord, w_beta, point_hit, track, noise):
    ndev = layer_size * phi_size
    hits, width = features.shape
    layers = w_layers.shape[0]
    dim = w_coord.shape[0]
    points = point_hit.shape[0]
    hits_all = hits * ndev * 1.0
    points_all = points * ndev * 1.0
    f32 = jnp.float32
    core = phi_size
    plane = [1, 2 * phi_size]
    others = [b for b in bits_of(ndev) if b != core and b not in plane]

    line = others[:2]
    others = others[2:]
    flat_masks = [plane[0], plane[1], plane[0] ^ plane[1]]
    line_masks = [line[0], line[1], line[0] ^ line[1]]

    def swap(x, mask, other=None):
        masks = (mask, mask if other is None else other)
        return lax.ppermute(x, AXES, [(i, i ^ masks[i // core & 1]) for i in range(ndev)])

    sizes = (layer_size, phi_size)
    track = track.reshape(1, hits)
    noise = noise.reshape(1, hits)
    low = jnp.bfloat16

    pay, aux = pl.pallas_call(
        functools.partial(embed_kernel, sizes),
        out_shape=(
            jax.ShapeDtypeStruct((dim + 8, hits), f32),
            jax.ShapeDtypeStruct((16, hits), f32),
        ),
        in_specs=[HBM] * 8,
        out_specs=(VMEM,) * 2,
        scratch_shapes=[
            pltpu.SMEM((points,), jnp.int32),
            pltpu.VMEM((hits, width), low),
            pltpu.VMEM((layers, width, width), low),
            pltpu.VMEM((layers, width), f32),
            pltpu.VMEM((dim, width), low),
            pltpu.VMEM(w_beta.shape, low),
            pltpu.VMEM((1, hits), jnp.int32),
            pltpu.VMEM((1, hits), jnp.int32),
            pltpu.SemaphoreType.DMA((layers + 7,)),
        ],
        compiler_params=pltpu.CompilerParams(vmem_limit_bytes=EMBED_VMEM),
        name="embed",
    )(point_hit, features, w_layers, b_layers, w_coord, w_beta, track, noise)

    def residuals(early):
        return pl.pallas_call(
            residual_kernel,
            out_shape=(
                jax.ShapeDtypeStruct((layers, hits, width), f32),
                jax.ShapeDtypeStruct((layers, width, hits), low),
                jax.ShapeDtypeStruct((hits, width), low),
                jax.ShapeDtypeStruct((layers - 1, width, width), low),
                jax.ShapeDtypeStruct((2 * dim, width), low),
            ),
            in_specs=[VMEM] * 5,
            out_specs=(VMEM,) * 5,
            compiler_params=PARAMS,
            cost_estimate=pl.CostEstimate(
                flops=20 * layers * hits * width, bytes_accessed=6 * layers * hits * width,
                transcendentals=layers * hits * width,
            ),
            name="residuals",
        )(*early)

    pay_own, own, xb, yb = pl.pallas_call(
        spread_kernel,
        out_shape=(
            jax.ShapeDtypeStruct((dim + 8, hits), f32),
            jax.ShapeDtypeStruct((8, 128), f32),
            jax.ShapeDtypeStruct((dim, 8, hits), f32),
            jax.ShapeDtypeStruct((dim, 8, hits), f32),
        ),
        in_specs=[VMEM],
        out_specs=(VMEM,) * 4,
        compiler_params=PARAMS,
        cost_estimate=pl.CostEstimate(flops=0, bytes_accessed=80 * dim * hits, transcendentals=0),
        name="spread",
    )(pay)
    rows_all = pay[None]
    kept = pay_own[None]
    for m in others:
        kept = rows_all = jnp.concatenate([kept, swap(rows_all, m)], 0)
    arrived = [swap(rows_all, m) for m in (line[0], line[0] ^ line[1], line[1])]
    rows_all = jnp.concatenate([kept] + arrived, 0)
    rows_all, *early = lax.optimization_barrier((rows_all, features, w_layers, b_layers))
    arrived = [swap(rows_all, m) for m in (plane[0], plane[0] ^ plane[1], plane[1])]
    rows_all = jnp.concatenate([rows_all] + arrived, 0)
    slope, ht, last, wt, head = residuals(early + [w_coord, w_beta])
    rows_all, slope = lax.optimization_barrier((rows_all, slope))
    rows_far = swap(rows_all, core)

    partial_sums = (
        jax.ShapeDtypeStruct((dim + 1, 8, hits), f32),
        jax.ShapeDtypeStruct((dim + 1, 8, 128), f32),
    )
    hit_sums, point_sums = pl.pallas_call(
        near_kernel,
        out_shape=partial_sums,
        in_specs=[VMEM] * 5,
        out_specs=(VMEM, VMEM),
        compiler_params=PARAMS,
        cost_estimate=pl.CostEstimate(
            flops=200 * points * hits * ndev, bytes_accessed=ndev * hits * 64,
            transcendentals=2 * points * hits * ndev,
        ),
        name="near_pairs",
    )(pay_own, own, xb, yb, rows_all)

    blocks = 8
    block_rows = 2 * (layers * width // blocks) + 8
    half = jax.ShapeDtypeStruct((blocks // 2, block_rows, 128), f32)
    keep, send = pl.pallas_call(
        functools.partial(backward_kernel, sizes, hits_all, points_all),
        out_shape=(half, half),
        in_specs=[VMEM] * 13,
        out_specs=(VMEM, VMEM),
        scratch_shapes=[
            pltpu.VMEM((dim, hits), f32),
            pltpu.VMEM((blocks, block_rows, 128), f32),
            pltpu.VMEM((8 * blocks, 128), f32),
        ],
        compiler_params=PARAMS,
        name="pairs_backward",
    )(pay_own, own, xb, yb, aux, slope, ht, last, wt, head, rows_far, hit_sums, point_sums)

    total = keep + swap(send, core)
    mine = total[0]
    arrived = [swap(total[r + 1], a, b) for r, (a, b) in enumerate(zip(flat_masks, line_masks))]
    mine = (mine + arrived[0]) + (arrived[1] + arrived[2])
    mine = mine + swap(mine, line[0], plane[0])
    mine = mine + swap(mine, line[0] ^ line[1], plane[1])
    for m in others:
        mine = mine + swap(mine, m)
    quarter = [mine] + [swap(mine, a, b) for a, b in zip(flat_masks, line_masks)]
    far = swap(jnp.stack(quarter), core)

    weights = jax.ShapeDtypeStruct((blocks, layers * width // blocks, width), f32)
    gw, near_ext = pl.pallas_call(
        functools.partial(place_near_kernel, sizes),
        out_shape=(weights, jax.ShapeDtypeStruct((blocks // 2, 8, 128), f32)),
        in_specs=[VMEM] * 4,
        out_specs=(HBM, VMEM),
        scratch_shapes=[pltpu.SemaphoreType.DMA((blocks,))],
        compiler_params=PARAMS,
        cost_estimate=pl.CostEstimate(flops=0, bytes_accessed=4 * layers * width * width, transcendentals=0),
        name="place_near",
    )(*quarter)
    gw, gb, gc, gbeta, loss = pl.pallas_call(
        functools.partial(place_far_kernel, sizes),
        out_shape=(
            weights,
            jax.ShapeDtypeStruct((layers, width), f32),
            jax.ShapeDtypeStruct((dim, width), f32),
            jax.ShapeDtypeStruct((1, width), f32),
            jax.ShapeDtypeStruct((1, 1), f32),
        ),
        in_specs=[VMEM, VMEM, HBM],
        out_specs=(HBM,) * 5,
        scratch_shapes=[
            pltpu.VMEM((layers, width), f32),
            pltpu.VMEM((dim, width), f32),
            pltpu.VMEM((1, width), f32),
            pltpu.VMEM((1, 1), f32),
            pltpu.VMEM((blocks, 8, 128), f32),
            pltpu.SemaphoreType.DMA((blocks,)),
            pltpu.SemaphoreType.DMA((4,)),
        ],
        input_output_aliases={2: 0},
        compiler_params=PARAMS,
        name="place_far",
    )(far, near_ext, gw)
    return (
        gw.reshape(layers, width, width),
        gb,
        gc,
        gbeta.reshape(width),
        loss.reshape(()),
    )


def solution(mesh):
    split = P(AXES)
    return jax.shard_map(
        functools.partial(on_device, mesh.shape["layer"], mesh.shape["phi"]),
        mesh=mesh,
        in_specs=(P(AXES, None), P(), P(), P(), P(), split, split, split),
        out_specs=(P(), P(), P(), P(), P()),
        check_vma=False,
    )
```

```python
import functools

import jax
import jax.numpy as jnp
from jax import lax
from jax.experimental import pallas as pl
from jax.experimental.pallas import tpu as pltpu
from jax.sharding import PartitionSpec as P

dist_eps = 0.0001
charge_floor = 0.5
AXES = ("layer", "phi")
VMEM = pl.BlockSpec(memory_space=pltpu.VMEM)
HBM = pl.BlockSpec(memory_space=pltpu.HBM)
UNROLL = 16
EMBED_VMEM = 63400000
HIGH = lax.Precision.HIGHEST
PARAMS = pltpu.CompilerParams(vmem_limit_bytes=48 * 1024 * 1024)


def matmul(a, b, ca=1, cb=0, precision=None):
    return lax.dot_general(
        a, b, (((ca,), (cb,)), ((), ())), precision=precision, preferred_element_type=jnp.float32
    )


def iota(shape, dim):
    return lax.broadcasted_iota(jnp.int32, shape, dim)


def head_rows(wc_ref, wb_ref):
    dim = wc_ref.shape[0]
    width = wc_ref.shape[1]
    beta_row = jnp.broadcast_to(wb_ref[...].astype(jnp.float32).reshape(1, width), (dim, width))
    tail = jnp.where(iota((dim, width), 0) == 0, beta_row, 0.0).astype(jnp.bfloat16)
    return jnp.concatenate([wc_ref[...], tail], 0)


def flat_index(axis_sizes):
    return lax.axis_index("layer") * axis_sizes[1] + lax.axis_index("phi")


def block_places(axis_sizes):
    me = flat_index(axis_sizes)
    shift = axis_sizes[1].bit_length() - 1
    core = lax.shift_right_logical(me, shift) & 1
    flat = (lax.shift_right_logical(me, shift + 1) & 1) * 2 + (me & 1)
    line = lax.shift_right_logical(me, 1) & 3
    mine = flat + core * (line - flat)
    return (core * 4, mine), (4 - core * 4, flat + line - mine)


def embed_kernel(
    sizes,
    hit_hbm, feat_hbm, w_hbm, b_hbm, wc_hbm, wb_hbm, track_hbm, noise_hbm,
    pay_ref, aux_ref,
    hit_ref, feat_ref, w_ref, b_ref, wc_ref, wb_ref, track_ref, noise_ref, sems,
):
    dim = wc_ref.shape[0]
    hits = feat_ref.shape[0]
    points = hit_ref.shape[0]
    layers = w_ref.shape[0]
    pairs = [(feat_hbm, feat_ref)] + [(w_hbm.at[l], w_ref.at[l]) for l in range(layers)]
    pairs = pairs[:2] + [(b_hbm, b_ref)] + pairs[2:]
    pairs += [(wc_hbm, wc_ref), (wb_hbm, wb_ref), (track_hbm, track_ref)]
    pairs += [(noise_hbm, noise_ref), (hit_hbm, hit_ref)]
    copies = [
        pltpu.make_async_copy(src, dst, sems.at[i]) for i, (src, dst) in enumerate(pairs)
    ]
    for copy in copies:
        copy.start()
    for copy in copies[:3]:
        copy.wait()
    h = feat_ref[...]
    for l in range(layers):
        if l > 0:
            copies[l + 2].wait()
        a = matmul(h, w_ref[l]) + b_ref[l : l + 1, :]
        h = (a * jax.nn.sigmoid(a)).astype(jnp.bfloat16)
    for copy in copies[layers + 2 :]:
        copy.wait()
    xz = matmul(head_rows(wc_ref, wb_ref), h, 1, 1)
    z = xz[dim : dim + 1]
    expz = jnp.exp(z)
    spread = jnp.log1p(2.0 * expz)
    q = 0.25 * spread * spread + charge_floor
    slope = 0.5 * spread * (2.0 * expz / (1.0 + 2.0 * expz))
    beta = jax.nn.sigmoid(z)
    noise = noise_ref[...]
    label = jnp.where(noise == 0, track_ref[...], -1).astype(jnp.float32)
    rows8 = iota((8, hits), 0)
    aux_ref[0:8, :] = jnp.where(
        rows8 == 0, beta, jnp.where(rows8 == 1, slope, noise.astype(jnp.float32))
    )
    col = jnp.zeros((points, hits), jnp.int32)
    for p in range(points):
        col = jnp.where(rows8 == (p + 2) % points, hit_ref[p], col)
    sel = iota((points, hits), 1) == col
    aux_ref[8:16, :] = jnp.where(sel, 1.0, 0.0)
    lane = iota((points, 128), 1)
    row = iota((points, 128), 0)
    order = jnp.where(row < 2, row + points - 2, row - 2)
    pts = jnp.where(lane == dim + 1, (flat_index(sizes) * points + order).astype(jnp.float32), 0.0)
    for c in range(dim):
        v = jnp.sum(jnp.where(sel, xz[c : c + 1], 0.0), axis=1, keepdims=True)
        pts = jnp.where(lane == c, v, pts)
    v = jnp.sum(jnp.where(sel, q, 0.0), axis=1, keepdims=True)
    pts = jnp.where(lane == dim, v, pts)
    moved = pltpu.roll(pts, 2, 0)
    left = jnp.where(row == 0, q[:, :128], jnp.where(row == 1, label[:, :128], pts))
    right = jnp.where(row == 0, q[:, 128:], jnp.where(row == 1, label[:, 128:], moved))
    pay_ref[0:dim, :] = xz[0:dim]
    pay_ref[dim : dim + 8, 0:128] = left
    pay_ref[dim : dim + 8, 128:256] = right


def residual_kernel(
    feat_ref, w_ref, b_ref, wc_ref, wb_ref, slope_ref, ht_ref, last_ref, wt_ref, head_ref
):
    head_ref[...] = head_rows(wc_ref, wb_ref)
    layers = w_ref.shape[0]
    h = feat_ref[...]
    ht_ref[0] = h.T
    for l in range(layers):
        a = matmul(h, w_ref[l]) + b_ref[l : l + 1, :]
        sig = jax.nn.sigmoid(a)
        slope_ref[l] = sig * (1.0 + a * (1.0 - sig))
        h = (a * sig).astype(jnp.bfloat16)
        if l < layers - 1:
            ht_ref[l + 1] = h.T
            wt_ref[l] = w_ref[l + 1].T
        else:
            last_ref[...] = h


def point_tile(left, right):
    rows = iota(left.shape, 0)
    return jnp.where(rows < 2, pltpu.roll(right, 6, 0), left)


def pair_weights(dist_sq, match):
    shifted = dist_sq + dist_eps
    inv = lax.rsqrt(shifted)
    reach = jnp.maximum(1.0 - shifted * inv, 0.0)
    potential = jnp.where(match, dist_sq, reach * reach)
    weight = jnp.where(match, 2.0, -2.0 * jnp.maximum(inv - 1.0, 0.0))
    return potential, weight


def spread_kernel(pay_ref, copy_ref, own_ref, xb, yb):
    dim = xb.shape[0]
    full = xb.shape[1:]
    copy_ref[...] = pay_ref[...]
    own = pay_ref[dim : dim + 8, :]
    own = point_tile(own[:, :128], own[:, 128:])
    own_ref[...] = own
    for c in range(dim):
        xb[c] = jnp.broadcast_to(pay_ref[c : c + 1, :], full)
        yb[c] = jnp.broadcast_to(own[:, c : c + 1], full)


def pair_sums(pay_ref, own, ref, xb, yb, hit_acc, point_acc):
    dim = xb.shape[0]
    full = xb.shape[1:]
    label_b = jnp.broadcast_to(pay_ref[dim + 1 : dim + 2, :], full)
    index_b = jnp.broadcast_to(own[:, dim + 1 : dim + 2], full)
    zero = jnp.zeros(full, jnp.float32)

    def hit_side(j, acc):
        tile = ref[j, dim : dim + 8, :]
        tile = point_tile(tile[:, :128], tile[:, 128:])
        diffs = []
        dist_sq = zero
        for c in range(dim):
            diff = xb[c] - tile[:, c : c + 1]
            diffs.append(diff)
            dist_sq = dist_sq + diff * diff
        point_q = tile[:, dim : dim + 1]
        potential, weight = pair_weights(dist_sq, label_b == tile[:, dim + 1 : dim + 2])
        weight = weight * point_q
        terms = [weight * diff for diff in diffs] + [potential * point_q]
        return tuple(s + term for s, term in zip(acc, terms))

    def point_side(j, acc):
        diffs = []
        dist_sq = zero
        for c in range(dim):
            diff = yb[c] - ref[j, c : c + 1, :]
            diffs.append(diff)
            dist_sq = dist_sq + diff * diff
        hit_q = ref[j, dim : dim + 1, :]
        potential, weight = pair_weights(dist_sq, index_b == ref[j, dim + 1 : dim + 2, :])
        weight = weight * hit_q
        terms = [weight * diff for diff in diffs] + [potential * hit_q]
        return tuple(s + term[:, :128] + term[:, 128:] for s, term in zip(acc, terms))

    count = ref.shape[0]
    unroll = min(count, UNROLL)
    hit_acc = lax.fori_loop(0, count, hit_side, hit_acc, unroll=unroll)
    point_acc = lax.fori_loop(0, count, point_side, point_acc, unroll=unroll)
    return hit_acc, point_acc


def near_kernel(pay_ref, own_ref, xb, yb, rows_ref, hit_ref, point_ref):
    dim = xb.shape[0]
    own = own_ref[...]
    hit_acc = (jnp.zeros(hit_ref.shape[1:], jnp.float32),) * (dim + 1)
    point_acc = (jnp.zeros(point_ref.shape[1:], jnp.float32),) * (dim + 1)
    hit_acc, point_acc = pair_sums(pay_ref, own, rows_ref, xb, yb, hit_acc, point_acc)
    for c in range(dim + 1):
        hit_ref[c] = hit_acc[c]
        point_ref[c] = point_acc[c]


def backward_kernel(
    sizes, hits_all, points_all,
    pay_ref, own_ref, xb, yb, aux_ref, slope_ref, ht_ref, last_ref, wt_ref, head_ref, rows_ref, hit_ref, point_ref,
    keep_ref, send_ref, gx_ref, stack, ext,
):
    dim = xb.shape[0]
    hits = pay_ref.shape[1]
    layers = slope_ref.shape[0]
    points = own_ref.shape[0]
    own = own_ref[...]
    q_row = pay_ref[dim : dim + 1, :]
    hit_acc = tuple(hit_ref[c] for c in range(dim + 1))
    point_acc = tuple(point_ref[c] for c in range(dim + 1))
    hit_acc, point_acc = pair_sums(pay_ref, own, rows_ref, xb, yb, hit_acc, point_acc)

    pot_row = jnp.sum(hit_acc[dim], axis=0, keepdims=True)
    scaled = q_row * (1.0 / hits_all)
    for c in range(dim):
        gx_ref[c : c + 1, :] = jnp.sum(hit_acc[c], axis=0, keepdims=True) * scaled
    lane = iota((8, 128), 1)
    own_q = own[:, dim : dim + 1] * (1.0 / hits_all)
    grads = jnp.where(lane == dim + 1, 1.0, 0.0)
    for c in range(dim):
        v = jnp.sum(point_acc[c], axis=1, keepdims=True) * own_q
        grads = jnp.where(lane == c, v, grads)
    v = jnp.sum(point_acc[dim], axis=1, keepdims=True) * (1.0 / hits_all)
    grads = jnp.where(lane == dim, v, grads)
    added = matmul(grads, aux_ref[8:16, :], 0, 0, HIGH)

    beta = aux_ref[0:1, :]
    noise = aux_ref[2:3, :]
    count = added[dim + 1 : dim + 2]
    grad_q = pot_row * (1.0 / hits_all) + added[dim : dim + 1]
    grad_b = noise * (1.0 / hits_all) - count * (1.0 / points_all)
    grad_z = grad_q * aux_ref[1:2, :] + grad_b * beta * (1.0 - beta)
    per_hit = q_row * pot_row * (1.0 / hits_all) + noise * beta * (1.0 / hits_all)
    per_hit = per_hit - count * beta * (1.0 / points_all)
    loss = jnp.sum(per_hit, axis=1, keepdims=True) + points * 1.0 / points_all

    grad_x = gx_ref[...] + added[0:dim]
    tail = jnp.where(iota((dim, hits), 0) == 0, grad_z, 0.0)
    low = jnp.concatenate([grad_x, tail], 0).astype(jnp.bfloat16)
    head = head_ref[...]
    grad_head = matmul(low, last_ref[...])
    up = matmul(low, head, 0, 0)
    ext[...] = jnp.zeros(ext.shape, jnp.float32)
    cols = [slice(0, 128), slice(128, 256)]
    base = 2 * layers
    for h, col in enumerate(cols):
        ext[base + h * dim : base + (h + 1) * dim, :] = grad_head[0:dim, col]
        ext[base + 2 * dim + h : base + 2 * dim + h + 1, :] = grad_head[dim : dim + 1, col]
    ext[base + 2 * dim + 2 : base + 2 * dim + 3, :] = jnp.broadcast_to(loss, (1, 128))
    blocks = stack.shape[0]
    rows = layers * hits // blocks
    per_layer = blocks // layers
    for l in range(layers - 1, -1, -1):
        err = (up * slope_ref[l]).astype(jnp.bfloat16)
        if l > 0:
            up = matmul(err, wt_ref[l - 1])
        grad_w = matmul(ht_ref[l], err)
        bias = jnp.sum(err.astype(jnp.float32), axis=0, keepdims=True)
        for h, col in enumerate(cols):
            ext[h * layers + l : h * layers + l + 1, :] = bias[:, col]
            for s in range(per_layer):
                stack[l * per_layer + s, h * rows : (h + 1) * rows, :] = grad_w[
                    s * rows : (s + 1) * rows, col
                ]
    for b in range(blocks):
        stack[b, 2 * rows : 2 * rows + 8, :] = ext[8 * b : 8 * b + 8, :]
    for out_ref, (first, place) in zip((keep_ref, send_ref), block_places(sizes)):
        for j in range(blocks // 2):
            out_ref[j] = stack[first + jnp.bitwise_xor(place, j)]


def place_copies(blocks, first, place, gw_ref, sems):
    rows = gw_ref.shape[1]
    copies = []
    for r, block in enumerate(blocks):
        slot = first + jnp.bitwise_xor(place, r)
        for h in range(2):
            copies.append(
                pltpu.make_async_copy(
                    block.at[pl.ds(h * rows, rows)],
                    gw_ref.at[slot, :, pl.ds(h * 128, 128)],
                    sems.at[2 * r + h],
                )
            )
    for copy in copies:
        copy.start()
    return copies


def place_near_kernel(sizes, *refs):
    blocks = refs[:4]
    gw_ref, ext_ref, sems = refs[4:]
    rows = gw_ref.shape[1]
    copies = place_copies(blocks, *block_places(sizes)[0], gw_ref, sems)
    for r, block in enumerate(blocks):
        ext_ref[r] = block[2 * rows :, :]
    for copy in copies:
        copy.wait()


def place_far_kernel(
    sizes, far_ref, near_ref, gw_in, gw_ref, *rest
):
    outs, scratch, (ext, sems, small_sems) = rest[:4], rest[4:8], rest[8:]
    gb_ref, gc_ref, gbeta_ref, loss_ref = scratch
    rows = gw_ref.shape[1]
    half = far_ref.shape[0]
    dim = gc_ref.shape[0]
    layers = gb_ref.shape[0]
    blocks = [far_ref.at[r] for r in range(half)]
    (near_first, near_place), (far_first, far_place) = block_places(sizes)
    copies = place_copies(blocks, far_first, far_place, gw_ref, sems)
    for r in range(half):
        ext[near_first + jnp.bitwise_xor(near_place, r)] = near_ref[r]
        ext[far_first + jnp.bitwise_xor(far_place, r)] = far_ref[r, 2 * rows :, :]
    flat = jnp.concatenate([ext[b] for b in range(2 * half)], 0)
    base = 2 * layers
    for h, col in enumerate([slice(0, 128), slice(128, 256)]):
        gb_ref[:, col] = flat[h * layers : (h + 1) * layers]
        gc_ref[:, col] = flat[base + h * dim : base + (h + 1) * dim]
        gbeta_ref[:, col] = flat[base + 2 * dim + h : base + 2 * dim + h + 1]
    loss_ref[...] = flat[base + 2 * dim + 2 : base + 2 * dim + 3, 0:1]
    for i in range(4):
        copies.append(pltpu.make_async_copy(scratch[i], outs[i], small_sems.at[i]))
        copies[-1].start()
    for copy in copies:
        copy.wait()


def bits_of(size):
    return [1 << t for t in range(size.bit_length() - 1)]


def on_device(layer_size, phi_size, features, w_layers, b_layers, w_coord, w_beta, point_hit, track, noise):
    ndev = layer_size * phi_size
    hits, width = features.shape
    layers = w_layers.shape[0]
    dim = w_coord.shape[0]
    points = point_hit.shape[0]
    hits_all = hits * ndev * 1.0
    points_all = points * ndev * 1.0
    f32 = jnp.float32
    core = phi_size
    plane = [1, 2 * phi_size]
    others = [b for b in bits_of(ndev) if b != core and b not in plane]

    line = others[:2]
    others = others[2:]
    flat_masks = [plane[0], plane[1], plane[0] ^ plane[1]]
    line_masks = [line[0], line[1], line[0] ^ line[1]]

    def swap(x, mask, other=None):
        masks = (mask, mask if other is None else other)
        return lax.ppermute(x, AXES, [(i, i ^ masks[i // core & 1]) for i in range(ndev)])

    sizes = (layer_size, phi_size)
    track = track.reshape(1, hits)
    noise = noise.reshape(1, hits)
    low = jnp.bfloat16

    pay, aux = pl.pallas_call(
        functools.partial(embed_kernel, sizes),
        out_shape=(
            jax.ShapeDtypeStruct((dim + 8, hits), f32),
            jax.ShapeDtypeStruct((16, hits), f32),
        ),
        in_specs=[HBM] * 8,
        out_specs=(VMEM,) * 2,
        scratch_shapes=[
            pltpu.SMEM((points,), jnp.int32),
            pltpu.VMEM((hits, width), low),
            pltpu.VMEM((layers, width, width), low),
            pltpu.VMEM((layers, width), f32),
            pltpu.VMEM((dim, width), low),
            pltpu.VMEM(w_beta.shape, low),
            pltpu.VMEM((1, hits), jnp.int32),
            pltpu.VMEM((1, hits), jnp.int32),
            pltpu.SemaphoreType.DMA((layers + 7,)),
        ],
        compiler_params=pltpu.CompilerParams(vmem_limit_bytes=EMBED_VMEM),
        name="embed",
    )(point_hit, features, w_layers, b_layers, w_coord, w_beta, track, noise)

    def residuals(early):
        return pl.pallas_call(
            residual_kernel,
            out_shape=(
                jax.ShapeDtypeStruct((layers, hits, width), f32),
                jax.ShapeDtypeStruct((layers, width, hits), low),
                jax.ShapeDtypeStruct((hits, width), low),
                jax.ShapeDtypeStruct((layers - 1, width, width), low),
                jax.ShapeDtypeStruct((2 * dim, width), low),
            ),
            in_specs=[VMEM] * 5,
            out_specs=(VMEM,) * 5,
            compiler_params=PARAMS,
            cost_estimate=pl.CostEstimate(
                flops=20 * layers * hits * width, bytes_accessed=6 * layers * hits * width,
                transcendentals=layers * hits * width,
            ),
            name="residuals",
        )(*early)

    pay_own, own, xb, yb = pl.pallas_call(
        spread_kernel,
        out_shape=(
            jax.ShapeDtypeStruct((dim + 8, hits), f32),
            jax.ShapeDtypeStruct((8, 128), f32),
            jax.ShapeDtypeStruct((dim, 8, hits), f32),
            jax.ShapeDtypeStruct((dim, 8, hits), f32),
        ),
        in_specs=[VMEM],
        out_specs=(VMEM,) * 4,
        compiler_params=PARAMS,
        cost_estimate=pl.CostEstimate(flops=0, bytes_accessed=80 * dim * hits, transcendentals=0),
        name="spread",
    )(pay)
    rows_all = pay[None]
    kept = pay_own[None]
    for m in others:
        kept = rows_all = jnp.concatenate([kept, swap(rows_all, m)], 0)
    arrived = [swap(rows_all, m) for m in (line[0], line[0] ^ line[1], line[1])]
    rows_all = jnp.concatenate([kept] + arrived, 0)
    rows_all, *early = lax.optimization_barrier((rows_all, features, w_layers, b_layers))
    arrived = [swap(rows_all, m) for m in (plane[0], plane[0] ^ plane[1], plane[1])]
    rows_all = jnp.concatenate([rows_all] + arrived, 0)
    slope, ht, last, wt, head = residuals(early + [w_coord, w_beta])
    rows_all, slope = lax.optimization_barrier((rows_all, slope))
    rows_far = swap(rows_all, core)

    partial_sums = (
        jax.ShapeDtypeStruct((dim + 1, 8, hits), f32),
        jax.ShapeDtypeStruct((dim + 1, 8, 128), f32),
    )
    hit_sums, point_sums = pl.pallas_call(
        near_kernel,
        out_shape=partial_sums,
        in_specs=[VMEM] * 5,
        out_specs=(VMEM, VMEM),
        compiler_params=PARAMS,
        cost_estimate=pl.CostEstimate(
            flops=200 * points * hits * ndev, bytes_accessed=ndev * hits * 64,
            transcendentals=2 * points * hits * ndev,
        ),
        name="near_pairs",
    )(pay_own, own, xb, yb, rows_all)

    blocks = 8
    block_rows = 2 * (layers * width // blocks) + 8
    half = jax.ShapeDtypeStruct((blocks // 2, block_rows, 128), f32)
    keep, send = pl.pallas_call(
        functools.partial(backward_kernel, sizes, hits_all, points_all),
        out_shape=(half, half),
        in_specs=[VMEM] * 13,
        out_specs=(VMEM, VMEM),
        scratch_shapes=[
            pltpu.VMEM((dim, hits), f32),
            pltpu.VMEM((blocks, block_rows, 128), f32),
            pltpu.VMEM((8 * blocks, 128), f32),
        ],
        compiler_params=PARAMS,
        name="pairs_backward",
    )(pay_own, own, xb, yb, aux, slope, ht, last, wt, head, rows_far, hit_sums, point_sums)

    total = keep + swap(send, core)
    mine = total[0]
    arrived = [swap(total[r + 1], a, b) for r, (a, b) in enumerate(zip(flat_masks, line_masks))]
    mine = (mine + arrived[0]) + (arrived[1] + arrived[2])
    arrived = [swap(mine, line_masks[r], flat_masks[r]) for r in (1, 0, 2)]
    mine = (mine + arrived[0]) + (arrived[1] + arrived[2])
    for m in others:
        mine = mine + swap(mine, m)
    quarter = [mine] + [swap(mine, a, b) for a, b in zip(flat_masks, line_masks)]
    far = swap(jnp.stack(quarter), core)

    weights = jax.ShapeDtypeStruct((blocks, layers * width // blocks, width), f32)
    gw, near_ext = pl.pallas_call(
        functools.partial(place_near_kernel, sizes),
        out_shape=(weights, jax.ShapeDtypeStruct((blocks // 2, 8, 128), f32)),
        in_specs=[VMEM] * 4,
        out_specs=(HBM, VMEM),
        scratch_shapes=[pltpu.SemaphoreType.DMA((blocks,))],
        compiler_params=PARAMS,
        cost_estimate=pl.CostEstimate(flops=0, bytes_accessed=4 * layers * width * width, transcendentals=0),
        name="place_near",
    )(*quarter)
    gw, gb, gc, gbeta, loss = pl.pallas_call(
        functools.partial(place_far_kernel, sizes),
        out_shape=(
            weights,
            jax.ShapeDtypeStruct((layers, width), f32),
            jax.ShapeDtypeStruct((dim, width), f32),
            jax.ShapeDtypeStruct((1, width), f32),
            jax.ShapeDtypeStruct((1, 1), f32),
        ),
        in_specs=[VMEM, VMEM, HBM],
        out_specs=(HBM,) * 5,
        scratch_shapes=[
            pltpu.VMEM((layers, width), f32),
            pltpu.VMEM((dim, width), f32),
            pltpu.VMEM((1, width), f32),
            pltpu.VMEM((1, 1), f32),
            pltpu.VMEM((blocks, 8, 128), f32),
            pltpu.SemaphoreType.DMA((blocks,)),
            pltpu.SemaphoreType.DMA((4,)),
        ],
        input_output_aliases={2: 0},
        compiler_params=PARAMS,
        name="place_far",
    )(far, near_ext, gw)
    return (
        gw.reshape(layers, width, width),
        gb,
        gc,
        gbeta.reshape(width),
        loss.reshape(()),
    )


def solution(mesh):
    split = P(AXES)
    return jax.shard_map(
        functools.partial(on_device, mesh.shape["layer"], mesh.shape["phi"]),
        mesh=mesh,
        in_specs=(P(AXES, None), P(), P(), P(), P(), split, split, split),
        out_specs=(P(), P(), P(), P(), P()),
        check_vma=False,
    )
```

```python
import functools

import jax
import jax.numpy as jnp
from jax import lax
from jax.experimental import pallas as pl
from jax.experimental.pallas import tpu as pltpu
from jax.sharding import PartitionSpec as P

dist_eps = 0.0001
charge_floor = 0.5
AXES = ("layer", "phi")
VMEM = pl.BlockSpec(memory_space=pltpu.VMEM)
HBM = pl.BlockSpec(memory_space=pltpu.HBM)
UNROLL = 16
EMBED_VMEM = 63400000
HIGH = lax.Precision.HIGHEST
PARAMS = pltpu.CompilerParams(vmem_limit_bytes=48 * 1024 * 1024)


def matmul(a, b, ca=1, cb=0, precision=None):
    return lax.dot_general(
        a, b, (((ca,), (cb,)), ((), ())), precision=precision, preferred_element_type=jnp.float32
    )


def iota(shape, dim):
    return lax.broadcasted_iota(jnp.int32, shape, dim)


def head_rows(wc_ref, wb_ref):
    dim = wc_ref.shape[0]
    width = wc_ref.shape[1]
    beta_row = jnp.broadcast_to(wb_ref[...].astype(jnp.float32).reshape(1, width), (dim, width))
    tail = jnp.where(iota((dim, width), 0) == 0, beta_row, 0.0).astype(jnp.bfloat16)
    return jnp.concatenate([wc_ref[...], tail], 0)


def flat_index(axis_sizes):
    return lax.axis_index("layer") * axis_sizes[1] + lax.axis_index("phi")


def block_places(axis_sizes):
    me = flat_index(axis_sizes)
    shift = axis_sizes[1].bit_length() - 1
    core = lax.shift_right_logical(me, shift) & 1
    flat = (lax.shift_right_logical(me, shift + 1) & 1) * 2 + (me & 1)
    line = lax.shift_right_logical(me, 1) & 3
    mine = flat + core * (line - flat)
    return (core * 4, mine), (4 - core * 4, flat + line - mine)


def embed_kernel(
    sizes,
    hit_hbm, feat_hbm, w_hbm, b_hbm, wc_hbm, wb_hbm, track_hbm, noise_hbm,
    pay_ref, aux_ref,
    hit_ref, feat_ref, w_ref, b_ref, wc_ref, wb_ref, track_ref, noise_ref, sems,
):
    dim = wc_ref.shape[0]
    hits = feat_ref.shape[0]
    points = hit_ref.shape[0]
    layers = w_ref.shape[0]
    pairs = [(feat_hbm, feat_ref)] + [(w_hbm.at[l], w_ref.at[l]) for l in range(layers)]
    pairs = pairs[:2] + [(b_hbm, b_ref)] + pairs[2:]
    pairs += [(wc_hbm, wc_ref), (wb_hbm, wb_ref), (track_hbm, track_ref)]
    pairs += [(noise_hbm, noise_ref), (hit_hbm, hit_ref)]
    copies = [
        pltpu.make_async_copy(src, dst, sems.at[i]) for i, (src, dst) in enumerate(pairs)
    ]
    for copy in copies:
        copy.start()
    for copy in copies[:3]:
        copy.wait()
    h = feat_ref[...]
    for l in range(layers):
        if l > 0:
            copies[l + 2].wait()
        a = matmul(h, w_ref[l]) + b_ref[l : l + 1, :]
        h = (a * jax.nn.sigmoid(a)).astype(jnp.bfloat16)
    for copy in copies[layers + 2 :]:
        copy.wait()
    xz = matmul(head_rows(wc_ref, wb_ref), h, 1, 1)
    z = xz[dim : dim + 1]
    expz = jnp.exp(z)
    spread = jnp.log1p(2.0 * expz)
    q = 0.25 * spread * spread + charge_floor
    slope = 0.5 * spread * (2.0 * expz / (1.0 + 2.0 * expz))
    beta = jax.nn.sigmoid(z)
    noise = noise_ref[...]
    label = jnp.where(noise == 0, track_ref[...], -1).astype(jnp.float32)
    rows8 = iota((8, hits), 0)
    aux_ref[0:8, :] = jnp.where(
        rows8 == 0, beta, jnp.where(rows8 == 1, slope, noise.astype(jnp.float32))
    )
    col = jnp.zeros((points, hits), jnp.int32)
    for p in range(points):
        col = jnp.where(rows8 == (p + 2) % points, hit_ref[p], col)
    sel = iota((points, hits), 1) == col
    aux_ref[8:16, :] = jnp.where(sel, 1.0, 0.0)
    lane = iota((points, 128), 1)
    row = iota((points, 128), 0)
    order = jnp.where(row < 2, row + points - 2, row - 2)
    pts = jnp.where(lane == dim + 1, (flat_index(sizes) * points + order).astype(jnp.float32), 0.0)
    for c in range(dim):
        v = jnp.sum(jnp.where(sel, xz[c : c + 1], 0.0), axis=1, keepdims=True)
        pts = jnp.where(lane == c, v, pts)
    v = jnp.sum(jnp.where(sel, q, 0.0), axis=1, keepdims=True)
    pts = jnp.where(lane == dim, v, pts)
    moved = pltpu.roll(pts, 2, 0)
    left = jnp.where(row == 0, q[:, :128], jnp.where(row == 1, label[:, :128], pts))
    right = jnp.where(row == 0, q[:, 128:], jnp.where(row == 1, label[:, 128:], moved))
    pay_ref[0:dim, :] = xz[0:dim]
    pay_ref[dim : dim + 8, 0:128] = left
    pay_ref[dim : dim + 8, 128:256] = right


def residual_kernel(
    feat_ref, w_ref, b_ref, wc_ref, wb_ref, slope_ref, ht_ref, last_ref, wt_ref, head_ref
):
    head_ref[...] = head_rows(wc_ref, wb_ref)
    layers = w_ref.shape[0]
    h = feat_ref[...]
    ht_ref[0] = h.T
    for l in range(layers):
        a = matmul(h, w_ref[l]) + b_ref[l : l + 1, :]
        sig = jax.nn.sigmoid(a)
        slope_ref[l] = sig * (1.0 + a * (1.0 - sig))
        h = (a * sig).astype(jnp.bfloat16)
        if l < layers - 1:
            ht_ref[l + 1] = h.T
            wt_ref[l] = w_ref[l + 1].T
        else:
            last_ref[...] = h


def point_tile(left, right):
    rows = iota(left.shape, 0)
    return jnp.where(rows < 2, pltpu.roll(right, 6, 0), left)


def pair_weights(dist_sq, match):
    shifted = dist_sq + dist_eps
    inv = lax.rsqrt(shifted)
    reach = jnp.maximum(1.0 - shifted * inv, 0.0)
    potential = jnp.where(match, dist_sq, reach * reach)
    weight = jnp.where(match, 2.0, -2.0 * jnp.maximum(inv - 1.0, 0.0))
    return potential, weight


def spread_kernel(pay_ref, copy_ref, own_ref, xb, yb):
    dim = xb.shape[0]
    full = xb.shape[1:]
    copy_ref[...] = pay_ref[...]
    own = pay_ref[dim : dim + 8, :]
    own = point_tile(own[:, :128], own[:, 128:])
    own_ref[...] = own
    for c in range(dim):
        xb[c] = jnp.broadcast_to(pay_ref[c : c + 1, :], full)
        yb[c] = jnp.broadcast_to(own[:, c : c + 1], full)


def pair_sums(pay_ref, own, ref, xb, yb, hit_acc, point_acc):
    dim = xb.shape[0]
    full = xb.shape[1:]
    label_b = jnp.broadcast_to(pay_ref[dim + 1 : dim + 2, :], full)
    index_b = jnp.broadcast_to(own[:, dim + 1 : dim + 2], full)
    zero = jnp.zeros(full, jnp.float32)

    def hit_side(j, acc):
        tile = ref[j, dim : dim + 8, :]
        tile = point_tile(tile[:, :128], tile[:, 128:])
        diffs = []
        dist_sq = zero
        for c in range(dim):
            diff = xb[c] - tile[:, c : c + 1]
            diffs.append(diff)
            dist_sq = dist_sq + diff * diff
        point_q = tile[:, dim : dim + 1]
        potential, weight = pair_weights(dist_sq, label_b == tile[:, dim + 1 : dim + 2])
        weight = weight * point_q
        terms = [weight * diff for diff in diffs] + [potential * point_q]
        return tuple(s + term for s, term in zip(acc, terms))

    def point_side(j, acc):
        diffs = []
        dist_sq = zero
        for c in range(dim):
            diff = yb[c] - ref[j, c : c + 1, :]
            diffs.append(diff)
            dist_sq = dist_sq + diff * diff
        hit_q = ref[j, dim : dim + 1, :]
        potential, weight = pair_weights(dist_sq, index_b == ref[j, dim + 1 : dim + 2, :])
        weight = weight * hit_q
        terms = [weight * diff for diff in diffs] + [potential * hit_q]
        return tuple(s + term[:, :128] + term[:, 128:] for s, term in zip(acc, terms))

    count = ref.shape[0]
    unroll = min(count, UNROLL)
    hit_acc = lax.fori_loop(0, count, hit_side, hit_acc, unroll=unroll)
    point_acc = lax.fori_loop(0, count, point_side, point_acc, unroll=unroll)
    return hit_acc, point_acc


def near_kernel(pay_ref, own_ref, xb, yb, rows_ref, hit_ref, point_ref):
    dim = xb.shape[0]
    own = own_ref[...]
    hit_acc = (jnp.zeros(hit_ref.shape[1:], jnp.float32),) * (dim + 1)
    point_acc = (jnp.zeros(point_ref.shape[1:], jnp.float32),) * (dim + 1)
    hit_acc, point_acc = pair_sums(pay_ref, own, rows_ref, xb, yb, hit_acc, point_acc)
    for c in range(dim + 1):
        hit_ref[c] = hit_acc[c]
        point_ref[c] = point_acc[c]


def backward_kernel(
    sizes, hits_all, points_all,
    pay_ref, own_ref, xb, yb, aux_ref, slope_ref, ht_ref, last_ref, wt_ref, head_ref, rows_ref, hit_ref, point_ref,
    keep_ref, send_ref, gx_ref, stack, ext,
):
    dim = xb.shape[0]
    hits = pay_ref.shape[1]
    layers = slope_ref.shape[0]
    points = own_ref.shape[0]
    own = own_ref[...]
    q_row = pay_ref[dim : dim + 1, :]
    hit_acc = tuple(hit_ref[c] for c in range(dim + 1))
    point_acc = tuple(point_ref[c] for c in range(dim + 1))
    hit_acc, point_acc = pair_sums(pay_ref, own, rows_ref, xb, yb, hit_acc, point_acc)

    pot_row = jnp.sum(hit_acc[dim], axis=0, keepdims=True)
    scaled = q_row * (1.0 / hits_all)
    for c in range(dim):
        gx_ref[c : c + 1, :] = jnp.sum(hit_acc[c], axis=0, keepdims=True) * scaled
    lane = iota((8, 128), 1)
    own_q = own[:, dim : dim + 1] * (1.0 / hits_all)
    grads = jnp.where(lane == dim + 1, 1.0, 0.0)
    for c in range(dim):
        v = jnp.sum(point_acc[c], axis=1, keepdims=True) * own_q
        grads = jnp.where(lane == c, v, grads)
    v = jnp.sum(point_acc[dim], axis=1, keepdims=True) * (1.0 / hits_all)
    grads = jnp.where(lane == dim, v, grads)
    added = matmul(grads, aux_ref[8:16, :], 0, 0, HIGH)

    beta = aux_ref[0:1, :]
    noise = aux_ref[2:3, :]
    count = added[dim + 1 : dim + 2]
    grad_q = pot_row * (1.0 / hits_all) + added[dim : dim + 1]
    grad_b = noise * (1.0 / hits_all) - count * (1.0 / points_all)
    grad_z = grad_q * aux_ref[1:2, :] + grad_b * beta * (1.0 - beta)
    per_hit = q_row * pot_row * (1.0 / hits_all) + noise * beta * (1.0 / hits_all)
    per_hit = per_hit - count * beta * (1.0 / points_all)
    loss = jnp.sum(per_hit, axis=1, keepdims=True) + points * 1.0 / points_all

    grad_x = gx_ref[...] + added[0:dim]
    tail = jnp.where(iota((dim, hits), 0) == 0, grad_z, 0.0)
    low = jnp.concatenate([grad_x, tail], 0).astype(jnp.bfloat16)
    head = head_ref[...]
    grad_head = matmul(low, last_ref[...])
    up = matmul(low, head, 0, 0)
    ext[...] = jnp.zeros(ext.shape, jnp.float32)
    cols = [slice(0, 128), slice(128, 256)]
    base = 2 * layers
    for h, col in enumerate(cols):
        ext[base + h * dim : base + (h + 1) * dim, :] = grad_head[0:dim, col]
        ext[base + 2 * dim + h : base + 2 * dim + h + 1, :] = grad_head[dim : dim + 1, col]
    ext[base + 2 * dim + 2 : base + 2 * dim + 3, :] = jnp.broadcast_to(loss, (1, 128))
    blocks = stack.shape[0]
    rows = layers * hits // blocks
    per_layer = blocks // layers
    for l in range(layers - 1, -1, -1):
        err = (up * slope_ref[l]).astype(jnp.bfloat16)
        if l > 0:
            up = matmul(err, wt_ref[l - 1])
        grad_w = matmul(ht_ref[l], err)
        bias = jnp.sum(err.astype(jnp.float32), axis=0, keepdims=True)
        for h, col in enumerate(cols):
            ext[h * layers + l : h * layers + l + 1, :] = bias[:, col]
            for s in range(per_layer):
                stack[l * per_layer + s, h * rows : (h + 1) * rows, :] = grad_w[
                    s * rows : (s + 1) * rows, col
                ]
    for b in range(blocks):
        stack[b, 2 * rows : 2 * rows + 8, :] = ext[8 * b : 8 * b + 8, :]
    for out_ref, (first, place) in zip((keep_ref, send_ref), block_places(sizes)):
        for j in range(blocks // 2):
            out_ref[j] = stack[first + jnp.bitwise_xor(place, j)]


def place_copies(blocks, first, place, gw_ref, sems):
    rows = gw_ref.shape[1]
    copies = []
    for r, block in enumerate(blocks):
        slot = first + jnp.bitwise_xor(place, r)
        for h in range(2):
            copies.append(
                pltpu.make_async_copy(
                    block.at[pl.ds(h * rows, rows)],
                    gw_ref.at[slot, :, pl.ds(h * 128, 128)],
                    sems.at[2 * r + h],
                )
            )
    for copy in copies:
        copy.start()
    return copies


def place_near_kernel(sizes, *refs):
    blocks = refs[:4]
    gw_ref, ext_ref, sems = refs[4:]
    rows = gw_ref.shape[1]
    copies = place_copies(blocks, *block_places(sizes)[0], gw_ref, sems)
    for r, block in enumerate(blocks):
        ext_ref[r] = block[2 * rows :, :]
    for copy in copies:
        copy.wait()


def place_far_kernel(sizes, *refs):
    blocks, (near_ref, _, gw_ref), rest = refs[:4], refs[4:7], refs[7:]
    outs, scratch, (ext, sems, small_sems) = rest[:4], rest[4:8], rest[8:]
    gb_ref, gc_ref, gbeta_ref, loss_ref = scratch
    rows = gw_ref.shape[1]
    half = len(blocks)
    dim = gc_ref.shape[0]
    layers = gb_ref.shape[0]
    (near_first, near_place), (far_first, far_place) = block_places(sizes)
    copies = place_copies(blocks, far_first, far_place, gw_ref, sems)
    for r in range(half):
        ext[near_first + jnp.bitwise_xor(near_place, r)] = near_ref[r]
        ext[far_first + jnp.bitwise_xor(far_place, r)] = blocks[r][2 * rows :, :]
    flat = jnp.concatenate([ext[b] for b in range(2 * half)], 0)
    base = 2 * layers
    for h, col in enumerate([slice(0, 128), slice(128, 256)]):
        gb_ref[:, col] = flat[h * layers : (h + 1) * layers]
        gc_ref[:, col] = flat[base + h * dim : base + (h + 1) * dim]
        gbeta_ref[:, col] = flat[base + 2 * dim + h : base + 2 * dim + h + 1]
    loss_ref[...] = flat[base + 2 * dim + 2 : base + 2 * dim + 3, 0:1]
    for i in range(4):
        copies.append(pltpu.make_async_copy(scratch[i], outs[i], small_sems.at[i]))
        copies[-1].start()
    for copy in copies:
        copy.wait()


def bits_of(size):
    return [1 << t for t in range(size.bit_length() - 1)]


def on_device(layer_size, phi_size, features, w_layers, b_layers, w_coord, w_beta, point_hit, track, noise):
    ndev = layer_size * phi_size
    hits, width = features.shape
    layers = w_layers.shape[0]
    dim = w_coord.shape[0]
    points = point_hit.shape[0]
    hits_all = hits * ndev * 1.0
    points_all = points * ndev * 1.0
    f32 = jnp.float32
    core = phi_size
    plane = [1, 2 * phi_size]
    others = [b for b in bits_of(ndev) if b != core and b not in plane]

    line = others[:2]
    others = others[2:]
    flat_masks = [plane[0], plane[1], plane[0] ^ plane[1]]
    line_masks = [line[0], line[1], line[0] ^ line[1]]

    def swap(x, mask, other=None):
        masks = (mask, mask if other is None else other)
        return lax.ppermute(x, AXES, [(i, i ^ masks[i // core & 1]) for i in range(ndev)])

    sizes = (layer_size, phi_size)
    track = track.reshape(1, hits)
    noise = noise.reshape(1, hits)
    low = jnp.bfloat16

    pay, aux = pl.pallas_call(
        functools.partial(embed_kernel, sizes),
        out_shape=(
            jax.ShapeDtypeStruct((dim + 8, hits), f32),
            jax.ShapeDtypeStruct((16, hits), f32),
        ),
        in_specs=[HBM] * 8,
        out_specs=(VMEM,) * 2,
        scratch_shapes=[
            pltpu.SMEM((points,), jnp.int32),
            pltpu.VMEM((hits, width), low),
            pltpu.VMEM((layers, width, width), low),
            pltpu.VMEM((layers, width), f32),
            pltpu.VMEM((dim, width), low),
            pltpu.VMEM(w_beta.shape, low),
            pltpu.VMEM((1, hits), jnp.int32),
            pltpu.VMEM((1, hits), jnp.int32),
            pltpu.SemaphoreType.DMA((layers + 7,)),
        ],
        compiler_params=pltpu.CompilerParams(vmem_limit_bytes=EMBED_VMEM),
        name="embed",
    )(point_hit, features, w_layers, b_layers, w_coord, w_beta, track, noise)

    def residuals(early):
        return pl.pallas_call(
            residual_kernel,
            out_shape=(
                jax.ShapeDtypeStruct((layers, hits, width), f32),
                jax.ShapeDtypeStruct((layers, width, hits), low),
                jax.ShapeDtypeStruct((hits, width), low),
                jax.ShapeDtypeStruct((layers - 1, width, width), low),
                jax.ShapeDtypeStruct((2 * dim, width), low),
            ),
            in_specs=[VMEM] * 5,
            out_specs=(VMEM,) * 5,
            compiler_params=PARAMS,
            cost_estimate=pl.CostEstimate(
                flops=20 * layers * hits * width, bytes_accessed=6 * layers * hits * width,
                transcendentals=layers * hits * width,
            ),
            name="residuals",
        )(*early)

    pay_own, own, xb, yb = pl.pallas_call(
        spread_kernel,
        out_shape=(
            jax.ShapeDtypeStruct((dim + 8, hits), f32),
            jax.ShapeDtypeStruct((8, 128), f32),
            jax.ShapeDtypeStruct((dim, 8, hits), f32),
            jax.ShapeDtypeStruct((dim, 8, hits), f32),
        ),
        in_specs=[VMEM],
        out_specs=(VMEM,) * 4,
        compiler_params=PARAMS,
        cost_estimate=pl.CostEstimate(flops=0, bytes_accessed=80 * dim * hits, transcendentals=0),
        name="spread",
    )(pay)
    rows_all = pay[None]
    kept = pay_own[None]
    for m in others:
        kept = rows_all = jnp.concatenate([kept, swap(rows_all, m)], 0)
    arrived = [swap(rows_all, m) for m in (line[0], line[0] ^ line[1], line[1])]
    rows_all = jnp.concatenate([kept] + arrived, 0)
    rows_all, *early = lax.optimization_barrier((rows_all, features, w_layers, b_layers))
    arrived = [swap(rows_all, m) for m in (plane[0], plane[0] ^ plane[1], plane[1])]
    rows_all = jnp.concatenate([rows_all] + arrived, 0)
    slope, ht, last, wt, head = residuals(early + [w_coord, w_beta])
    rows_all, slope = lax.optimization_barrier((rows_all, slope))
    rows_far = swap(rows_all, core)

    partial_sums = (
        jax.ShapeDtypeStruct((dim + 1, 8, hits), f32),
        jax.ShapeDtypeStruct((dim + 1, 8, 128), f32),
    )
    hit_sums, point_sums = pl.pallas_call(
        near_kernel,
        out_shape=partial_sums,
        in_specs=[VMEM] * 5,
        out_specs=(VMEM, VMEM),
        compiler_params=PARAMS,
        cost_estimate=pl.CostEstimate(
            flops=200 * points * hits * ndev, bytes_accessed=ndev * hits * 64,
            transcendentals=2 * points * hits * ndev,
        ),
        name="near_pairs",
    )(pay_own, own, xb, yb, rows_all)

    blocks = 8
    block_rows = 2 * (layers * width // blocks) + 8
    half = jax.ShapeDtypeStruct((blocks // 2, block_rows, 128), f32)
    keep, send = pl.pallas_call(
        functools.partial(backward_kernel, sizes, hits_all, points_all),
        out_shape=(half, half),
        in_specs=[VMEM] * 13,
        out_specs=(VMEM, VMEM),
        scratch_shapes=[
            pltpu.VMEM((dim, hits), f32),
            pltpu.VMEM((blocks, block_rows, 128), f32),
            pltpu.VMEM((8 * blocks, 128), f32),
        ],
        compiler_params=PARAMS,
        name="pairs_backward",
    )(pay_own, own, xb, yb, aux, slope, ht, last, wt, head, rows_far, hit_sums, point_sums)

    total = keep + swap(send, core)
    mine = total[0]
    arrived = [swap(total[r + 1], a, b) for r, (a, b) in enumerate(zip(flat_masks, line_masks))]
    mine = (mine + arrived[0]) + (arrived[1] + arrived[2])
    arrived = [swap(mine, line_masks[r], flat_masks[r]) for r in (1, 0, 2)]
    mine = (mine + arrived[0]) + (arrived[1] + arrived[2])
    for m in others:
        mine = mine + swap(mine, m)
    quarter = [mine] + [swap(mine, a, b) for a, b in zip(flat_masks, line_masks)]
    far = [swap(block, core) for block in quarter]

    weights = jax.ShapeDtypeStruct((blocks, layers * width // blocks, width), f32)
    gw, near_ext = pl.pallas_call(
        functools.partial(place_near_kernel, sizes),
        out_shape=(weights, jax.ShapeDtypeStruct((blocks // 2, 8, 128), f32)),
        in_specs=[VMEM] * 4,
        out_specs=(HBM, VMEM),
        scratch_shapes=[pltpu.SemaphoreType.DMA((blocks,))],
        compiler_params=PARAMS,
        cost_estimate=pl.CostEstimate(flops=0, bytes_accessed=4 * layers * width * width, transcendentals=0),
        name="place_near",
    )(*quarter)
    gw, gb, gc, gbeta, loss = pl.pallas_call(
        functools.partial(place_far_kernel, sizes),
        out_shape=(
            weights,
            jax.ShapeDtypeStruct((layers, width), f32),
            jax.ShapeDtypeStruct((dim, width), f32),
            jax.ShapeDtypeStruct((1, width), f32),
            jax.ShapeDtypeStruct((1, 1), f32),
        ),
        in_specs=[VMEM] * 5 + [HBM],
        out_specs=(HBM,) * 5,
        scratch_shapes=[
            pltpu.VMEM((layers, width), f32),
            pltpu.VMEM((dim, width), f32),
            pltpu.VMEM((1, width), f32),
            pltpu.VMEM((1, 1), f32),
            pltpu.VMEM((blocks, 8, 128), f32),
            pltpu.SemaphoreType.DMA((blocks,)),
            pltpu.SemaphoreType.DMA((4,)),
        ],
        input_output_aliases={5: 0},
        compiler_params=PARAMS,
        name="place_far",
    )(*far, near_ext, gw)
    return (
        gw.reshape(layers, width, width),
        gb,
        gc,
        gbeta.reshape(width),
        loss.reshape(()),
    )


def solution(mesh):
    split = P(AXES)
    return jax.shard_map(
        functools.partial(on_device, mesh.shape["layer"], mesh.shape["phi"]),
        mesh=mesh,
        in_specs=(P(AXES, None), P(), P(), P(), P(), split, split, split),
        out_specs=(P(), P(), P(), P(), P()),
        check_vma=False,
    )
```

```python
import functools

import jax
import jax.numpy as jnp
from jax import lax
from jax.experimental import pallas as pl
from jax.experimental.pallas import tpu as pltpu
from jax.sharding import PartitionSpec as P

dist_eps = 0.0001
charge_floor = 0.5
AXES = ("layer", "phi")
VMEM = pl.BlockSpec(memory_space=pltpu.VMEM)
HBM = pl.BlockSpec(memory_space=pltpu.HBM)
UNROLL = 16
EMBED_VMEM = 63400000
HIGH = lax.Precision.HIGHEST
PARAMS = pltpu.CompilerParams(vmem_limit_bytes=48 * 1024 * 1024)


def matmul(a, b, ca=1, cb=0, precision=None):
    return lax.dot_general(
        a, b, (((ca,), (cb,)), ((), ())), precision=precision, preferred_element_type=jnp.float32
    )


def iota(shape, dim):
    return lax.broadcasted_iota(jnp.int32, shape, dim)


def head_rows(wc_ref, wb_ref):
    dim = wc_ref.shape[0]
    width = wc_ref.shape[1]
    beta_row = jnp.broadcast_to(wb_ref[...].astype(jnp.float32).reshape(1, width), (dim, width))
    tail = jnp.where(iota((dim, width), 0) == 0, beta_row, 0.0).astype(jnp.bfloat16)
    return jnp.concatenate([wc_ref[...], tail], 0)


def flat_index(axis_sizes):
    return lax.axis_index("layer") * axis_sizes[1] + lax.axis_index("phi")


def block_places(axis_sizes):
    me = flat_index(axis_sizes)
    shift = axis_sizes[1].bit_length() - 1
    core = lax.shift_right_logical(me, shift) & 1
    flat = (lax.shift_right_logical(me, shift + 1) & 1) * 2 + (me & 1)
    line = lax.shift_right_logical(me, 1) & 3
    mine = flat + core * (line - flat)
    return (core * 4, mine), (4 - core * 4, flat + line - mine)


def embed_kernel(
    sizes,
    hit_hbm, feat_hbm, w_hbm, b_hbm, wc_hbm, wb_hbm, track_hbm, noise_hbm,
    pay_ref, aux_ref,
    hit_ref, feat_ref, w_ref, b_ref, wc_ref, wb_ref, track_ref, noise_ref, sems,
):
    dim = wc_ref.shape[0]
    hits = feat_ref.shape[0]
    points = hit_ref.shape[0]
    layers = w_ref.shape[0]
    pairs = [(feat_hbm, feat_ref), (w_hbm, w_ref), (b_hbm, b_ref), (wc_hbm, wc_ref), (wb_hbm, wb_ref)]
    pairs += [(track_hbm, track_ref), (noise_hbm, noise_ref), (hit_hbm, hit_ref)]
    copies = [
        pltpu.make_async_copy(src, dst, sems.at[i]) for i, (src, dst) in enumerate(pairs)
    ]
    for copy in copies:
        copy.start()
    for copy in copies[:3]:
        copy.wait()
    h = feat_ref[...]
    for l in range(layers):
        a = matmul(h, w_ref[l]) + b_ref[l : l + 1, :]
        h = (a * jax.nn.sigmoid(a)).astype(jnp.bfloat16)
    for copy in copies[3:]:
        copy.wait()
    xz = matmul(head_rows(wc_ref, wb_ref), h, 1, 1)
    z = xz[dim : dim + 1]
    expz = jnp.exp(z)
    spread = jnp.log1p(2.0 * expz)
    q = 0.25 * spread * spread + charge_floor
    slope = 0.5 * spread * (2.0 * expz / (1.0 + 2.0 * expz))
    beta = jax.nn.sigmoid(z)
    noise = noise_ref[...]
    label = jnp.where(noise == 0, track_ref[...], -1).astype(jnp.float32)
    rows8 = iota((8, hits), 0)
    aux_ref[0:8, :] = jnp.where(
        rows8 == 0, beta, jnp.where(rows8 == 1, slope, noise.astype(jnp.float32))
    )
    col = jnp.zeros((points, hits), jnp.int32)
    for p in range(points):
        col = jnp.where(rows8 == (p + 2) % points, hit_ref[p], col)
    sel = iota((points, hits), 1) == col
    aux_ref[8:16, :] = jnp.where(sel, 1.0, 0.0)
    lane = iota((points, 128), 1)
    row = iota((points, 128), 0)
    order = jnp.where(row < 2, row + points - 2, row - 2)
    pts = jnp.where(lane == dim + 1, (flat_index(sizes) * points + order).astype(jnp.float32), 0.0)
    for c in range(dim):
        v = jnp.sum(jnp.where(sel, xz[c : c + 1], 0.0), axis=1, keepdims=True)
        pts = jnp.where(lane == c, v, pts)
    v = jnp.sum(jnp.where(sel, q, 0.0), axis=1, keepdims=True)
    pts = jnp.where(lane == dim, v, pts)
    moved = pltpu.roll(pts, 2, 0)
    left = jnp.where(row == 0, q[:, :128], jnp.where(row == 1, label[:, :128], pts))
    right = jnp.where(row == 0, q[:, 128:], jnp.where(row == 1, label[:, 128:], moved))
    pay_ref[0:dim, :] = xz[0:dim]
    pay_ref[dim : dim + 8, 0:128] = left
    pay_ref[dim : dim + 8, 128:256] = right


def residual_kernel(
    feat_ref, w_ref, b_ref, wc_ref, wb_ref, slope_ref, ht_ref, last_ref, wt_ref, head_ref
):
    head_ref[...] = head_rows(wc_ref, wb_ref)
    layers = w_ref.shape[0]
    h = feat_ref[...]
    ht_ref[0] = h.T
    for l in range(layers):
        a = matmul(h, w_ref[l]) + b_ref[l : l + 1, :]
        sig = jax.nn.sigmoid(a)
        slope_ref[l] = sig * (1.0 + a * (1.0 - sig))
        h = (a * sig).astype(jnp.bfloat16)
        if l < layers - 1:
            ht_ref[l + 1] = h.T
            wt_ref[l] = w_ref[l + 1].T
        else:
            last_ref[...] = h


def point_tile(left, right):
    rows = iota(left.shape, 0)
    return jnp.where(rows < 2, pltpu.roll(right, 6, 0), left)


def pair_weights(dist_sq, match):
    shifted = dist_sq + dist_eps
    inv = lax.rsqrt(shifted)
    reach = jnp.maximum(1.0 - shifted * inv, 0.0)
    potential = jnp.where(match, dist_sq, reach * reach)
    weight = jnp.where(match, 2.0, -2.0 * jnp.maximum(inv - 1.0, 0.0))
    return potential, weight


def spread_kernel(pay_ref, copy_ref, own_ref, xb, yb):
    dim = xb.shape[0]
    full = xb.shape[1:]
    copy_ref[...] = pay_ref[...]
    own = pay_ref[dim : dim + 8, :]
    own = point_tile(own[:, :128], own[:, 128:])
    own_ref[...] = own
    for c in range(dim):
        xb[c] = jnp.broadcast_to(pay_ref[c : c + 1, :], full)
        yb[c] = jnp.broadcast_to(own[:, c : c + 1], full)


def pair_sums(pay_ref, own, ref, xb, yb, hit_acc, point_acc):
    dim = xb.shape[0]
    full = xb.shape[1:]
    label_b = jnp.broadcast_to(pay_ref[dim + 1 : dim + 2, :], full)
    index_b = jnp.broadcast_to(own[:, dim + 1 : dim + 2], full)
    zero = jnp.zeros(full, jnp.float32)

    def hit_side(j, acc):
        tile = ref[j, dim : dim + 8, :]
        tile = point_tile(tile[:, :128], tile[:, 128:])
        diffs = []
        dist_sq = zero
        for c in range(dim):
            diff = xb[c] - tile[:, c : c + 1]
            diffs.append(diff)
            dist_sq = dist_sq + diff * diff
        point_q = tile[:, dim : dim + 1]
        potential, weight = pair_weights(dist_sq, label_b == tile[:, dim + 1 : dim + 2])
        weight = weight * point_q
        terms = [weight * diff for diff in diffs] + [potential * point_q]
        return tuple(s + term for s, term in zip(acc, terms))

    def point_side(j, acc):
        diffs = []
        dist_sq = zero
        for c in range(dim):
            diff = yb[c] - ref[j, c : c + 1, :]
            diffs.append(diff)
            dist_sq = dist_sq + diff * diff
        hit_q = ref[j, dim : dim + 1, :]
        potential, weight = pair_weights(dist_sq, index_b == ref[j, dim + 1 : dim + 2, :])
        weight = weight * hit_q
        terms = [weight * diff for diff in diffs] + [potential * hit_q]
        return tuple(s + term[:, :128] + term[:, 128:] for s, term in zip(acc, terms))

    count = ref.shape[0]
    unroll = min(count, UNROLL)
    hit_acc = lax.fori_loop(0, count, hit_side, hit_acc, unroll=unroll)
    point_acc = lax.fori_loop(0, count, point_side, point_acc, unroll=unroll)
    return hit_acc, point_acc


def pair_kernel(parts, pay_ref, own_ref, xb, yb, *rest):
    rows, rest = rest[:parts], rest[parts:]
    hit_ref, point_ref = rest[-2:]
    if len(rest) > 2:
        sums = [tuple(ref[c] for c in range(ref.shape[0])) for ref in rest[:2]]
    else:
        sums = [(jnp.zeros(ref.shape[1:], jnp.float32),) * ref.shape[0] for ref in rest]
    own = own_ref[...]
    for ref in rows:
        sums = pair_sums(pay_ref, own, ref, xb, yb, *sums)
    for ref, values in zip((hit_ref, point_ref), sums):
        for c, value in enumerate(values):
            ref[c] = value


def backward_kernel(
    sizes, hits_all, points_all,
    pay_ref, own_ref, xb, yb, aux_ref, slope_ref, ht_ref, last_ref, wt_ref, head_ref, rows_ref, hit_ref, point_ref,
    keep_ref, send_ref, gx_ref, stack, ext,
):
    dim = xb.shape[0]
    hits = pay_ref.shape[1]
    layers = slope_ref.shape[0]
    points = own_ref.shape[0]
    own = own_ref[...]
    q_row = pay_ref[dim : dim + 1, :]
    hit_acc = tuple(hit_ref[c] for c in range(dim + 1))
    point_acc = tuple(point_ref[c] for c in range(dim + 1))
    hit_acc, point_acc = pair_sums(pay_ref, own, rows_ref, xb, yb, hit_acc, point_acc)

    pot_row = jnp.sum(hit_acc[dim], axis=0, keepdims=True)
    scaled = q_row * (1.0 / hits_all)
    for c in range(dim):
        gx_ref[c : c + 1, :] = jnp.sum(hit_acc[c], axis=0, keepdims=True) * scaled
    lane = iota((8, 128), 1)
    own_q = own[:, dim : dim + 1] * (1.0 / hits_all)
    grads = jnp.where(lane == dim + 1, 1.0, 0.0)
    for c in range(dim):
        v = jnp.sum(point_acc[c], axis=1, keepdims=True) * own_q
        grads = jnp.where(lane == c, v, grads)
    v = jnp.sum(point_acc[dim], axis=1, keepdims=True) * (1.0 / hits_all)
    grads = jnp.where(lane == dim, v, grads)
    added = matmul(grads, aux_ref[8:16, :], 0, 0, HIGH)

    beta = aux_ref[0:1, :]
    noise = aux_ref[2:3, :]
    count = added[dim + 1 : dim + 2]
    grad_q = pot_row * (1.0 / hits_all) + added[dim : dim + 1]
    grad_b = noise * (1.0 / hits_all) - count * (1.0 / points_all)
    grad_z = grad_q * aux_ref[1:2, :] + grad_b * beta * (1.0 - beta)
    per_hit = q_row * pot_row * (1.0 / hits_all) + noise * beta * (1.0 / hits_all)
    per_hit = per_hit - count * beta * (1.0 / points_all)
    loss = jnp.sum(per_hit, axis=1, keepdims=True) + points * 1.0 / points_all

    grad_x = gx_ref[...] + added[0:dim]
    tail = jnp.where(iota((dim, hits), 0) == 0, grad_z, 0.0)
    low = jnp.concatenate([grad_x, tail], 0).astype(jnp.bfloat16)
    head = head_ref[...]
    grad_head = matmul(low, last_ref[...])
    up = matmul(low, head, 0, 0)
    ext[...] = jnp.zeros(ext.shape, jnp.float32)
    cols = [slice(0, 128), slice(128, 256)]
    base = 2 * layers
    for h, col in enumerate(cols):
        ext[base + h * dim : base + (h + 1) * dim, :] = grad_head[0:dim, col]
        ext[base + 2 * dim + h : base + 2 * dim + h + 1, :] = grad_head[dim : dim + 1, col]
    ext[base + 2 * dim + 2 : base + 2 * dim + 3, :] = jnp.broadcast_to(loss, (1, 128))
    blocks = stack.shape[0]
    rows = layers * hits // blocks
    per_layer = blocks // layers
    for l in range(layers - 1, -1, -1):
        err = (up * slope_ref[l]).astype(jnp.bfloat16)
        if l > 0:
            up = matmul(err, wt_ref[l - 1])
        grad_w = matmul(ht_ref[l], err)
        bias = jnp.sum(err.astype(jnp.float32), axis=0, keepdims=True)
        for h, col in enumerate(cols):
            ext[h * layers + l : h * layers + l + 1, :] = bias[:, col]
            for s in range(per_layer):
                stack[l * per_layer + s, h * rows : (h + 1) * rows, :] = grad_w[
                    s * rows : (s + 1) * rows, col
                ]
    for b in range(blocks):
        stack[b, 2 * rows : 2 * rows + 8, :] = ext[8 * b : 8 * b + 8, :]
    for out_ref, (first, place) in zip((keep_ref, send_ref), block_places(sizes)):
        for j in range(blocks // 2):
            out_ref[j] = stack[first + jnp.bitwise_xor(place, j)]


def place_copies(blocks, first, place, gw_ref, sems):
    rows = gw_ref.shape[1]
    copies = []
    for r, block in enumerate(blocks):
        slot = first + jnp.bitwise_xor(place, r)
        for h in range(2):
            copies.append(
                pltpu.make_async_copy(
                    block.at[pl.ds(h * rows, rows)],
                    gw_ref.at[slot, :, pl.ds(h * 128, 128)],
                    sems.at[2 * r + h],
                )
            )
    for copy in copies:
        copy.start()
    return copies


def place_near_kernel(sizes, *refs):
    blocks = refs[:4]
    gw_ref, ext_ref, sems = refs[4:]
    rows = gw_ref.shape[1]
    copies = place_copies(blocks, *block_places(sizes)[0], gw_ref, sems)
    for r, block in enumerate(blocks):
        ext_ref[r] = block[2 * rows :, :]
    for copy in copies:
        copy.wait()


def place_far_kernel(sizes, *refs):
    blocks, (near_ref, _, gw_ref), rest = refs[:4], refs[4:7], refs[7:]
    outs, scratch, (ext, sems, small_sems) = rest[:4], rest[4:8], rest[8:]
    gb_ref, gc_ref, gbeta_ref, loss_ref = scratch
    rows = gw_ref.shape[1]
    half = len(blocks)
    dim = gc_ref.shape[0]
    layers = gb_ref.shape[0]
    (near_first, near_place), (far_first, far_place) = block_places(sizes)
    copies = place_copies(blocks, far_first, far_place, gw_ref, sems)
    for r in range(half):
        ext[near_first + jnp.bitwise_xor(near_place, r)] = near_ref[r]
        ext[far_first + jnp.bitwise_xor(far_place, r)] = blocks[r][2 * rows :, :]
    flat = jnp.concatenate([ext[b] for b in range(2 * half)], 0)
    base = 2 * layers
    for h, col in enumerate([slice(0, 128), slice(128, 256)]):
        gb_ref[:, col] = flat[h * layers : (h + 1) * layers]
        gc_ref[:, col] = flat[base + h * dim : base + (h + 1) * dim]
        gbeta_ref[:, col] = flat[base + 2 * dim + h : base + 2 * dim + h + 1]
    loss_ref[...] = flat[base + 2 * dim + 2 : base + 2 * dim + 3, 0:1]
    for i in range(4):
        copies.append(pltpu.make_async_copy(scratch[i], outs[i], small_sems.at[i]))
        copies[-1].start()
    for copy in copies:
        copy.wait()


def bits_of(size):
    return [1 << t for t in range(size.bit_length() - 1)]


def on_device(layer_size, phi_size, features, w_layers, b_layers, w_coord, w_beta, point_hit, track, noise):
    ndev = layer_size * phi_size
    hits, width = features.shape
    layers = w_layers.shape[0]
    dim = w_coord.shape[0]
    points = point_hit.shape[0]
    hits_all = hits * ndev * 1.0
    points_all = points * ndev * 1.0
    f32 = jnp.float32
    core = phi_size
    plane = [1, 2 * phi_size]
    others = [b for b in bits_of(ndev) if b != core and b not in plane]

    line = others[:2]
    others = others[2:]
    flat_masks = [plane[0], plane[1], plane[0] ^ plane[1]]
    line_masks = [line[0], line[1], line[0] ^ line[1]]

    def swap(x, mask, other=None):
        masks = (mask, mask if other is None else other)
        return lax.ppermute(x, AXES, [(i, i ^ masks[i // core & 1]) for i in range(ndev)])

    sizes = (layer_size, phi_size)
    track = track.reshape(1, hits)
    noise = noise.reshape(1, hits)
    low = jnp.bfloat16

    pay, aux = pl.pallas_call(
        functools.partial(embed_kernel, sizes),
        out_shape=(
            jax.ShapeDtypeStruct((dim + 8, hits), f32),
            jax.ShapeDtypeStruct((16, hits), f32),
        ),
        in_specs=[HBM] * 8,
        out_specs=(VMEM,) * 2,
        scratch_shapes=[
            pltpu.SMEM((points,), jnp.int32),
            pltpu.VMEM((hits, width), low),
            pltpu.VMEM((layers, width, width), low),
            pltpu.VMEM((layers, width), f32),
            pltpu.VMEM((dim, width), low),
            pltpu.VMEM(w_beta.shape, low),
            pltpu.VMEM((1, hits), jnp.int32),
            pltpu.VMEM((1, hits), jnp.int32),
            pltpu.SemaphoreType.DMA((8,)),
        ],
        compiler_params=pltpu.CompilerParams(vmem_limit_bytes=EMBED_VMEM),
        name="embed",
    )(point_hit, features, w_layers, b_layers, w_coord, w_beta, track, noise)

    def residuals(early):
        return pl.pallas_call(
            residual_kernel,
            out_shape=(
                jax.ShapeDtypeStruct((layers, hits, width), f32),
                jax.ShapeDtypeStruct((layers, width, hits), low),
                jax.ShapeDtypeStruct((hits, width), low),
                jax.ShapeDtypeStruct((layers - 1, width, width), low),
                jax.ShapeDtypeStruct((2 * dim, width), low),
            ),
            in_specs=[VMEM] * 5,
            out_specs=(VMEM,) * 5,
            compiler_params=PARAMS,
            cost_estimate=pl.CostEstimate(
                flops=20 * layers * hits * width, bytes_accessed=6 * layers * hits * width,
                transcendentals=layers * hits * width,
            ),
            name="residuals",
        )(*early)

    pay_own, own, xb, yb = pl.pallas_call(
        spread_kernel,
        out_shape=(
            jax.ShapeDtypeStruct((dim + 8, hits), f32),
            jax.ShapeDtypeStruct((8, 128), f32),
            jax.ShapeDtypeStruct((dim, 8, hits), f32),
            jax.ShapeDtypeStruct((dim, 8, hits), f32),
        ),
        in_specs=[VMEM],
        out_specs=(VMEM,) * 4,
        compiler_params=PARAMS,
        cost_estimate=pl.CostEstimate(flops=0, bytes_accessed=80 * dim * hits, transcendentals=0),
        name="spread",
    )(pay)
    rows_all = pay[None]
    kept = pay_own[None]
    for m in others:
        kept = rows_all = jnp.concatenate([kept, swap(rows_all, m)], 0)
    arrived = [swap(rows_all, m) for m in (line[0], line[0] ^ line[1], line[1])]
    rows_all = jnp.concatenate([kept] + arrived, 0)
    rows_all, *early = lax.optimization_barrier((rows_all, features, w_layers, b_layers))
    arrived = [swap(rows_all, m) for m in (plane[0], plane[0] ^ plane[1], plane[1])]
    first_far = swap(rows_all, core)
    rows = jnp.concatenate(arrived, 0)
    slope, ht, last, wt, head = residuals(early + [w_coord, w_beta])
    rows, first_far, slope = lax.optimization_barrier((rows, first_far, slope))
    rows_far = swap(rows, core)

    partial_sums = (
        jax.ShapeDtypeStruct((dim + 1, 8, hits), f32),
        jax.ShapeDtypeStruct((dim + 1, 8, 128), f32),
    )

    def pairs(rows, sums=()):
        count = sum(r.shape[0] for r in rows)
        return pl.pallas_call(
            functools.partial(pair_kernel, len(rows)),
            out_shape=partial_sums,
            in_specs=[VMEM] * (4 + len(rows) + len(sums)),
            out_specs=(VMEM, VMEM),
            compiler_params=PARAMS,
            cost_estimate=pl.CostEstimate(
                flops=200 * points * hits * count, bytes_accessed=count * hits * 64,
                transcendentals=2 * points * hits * count,
            ),
            name="pairs",
        )(pay_own, own, xb, yb, *rows, *sums)

    sums = pairs([rows_all, first_far, rows])

    blocks = 8
    block_rows = 2 * (layers * width // blocks) + 8
    half = jax.ShapeDtypeStruct((blocks // 2, block_rows, 128), f32)
    keep, send = pl.pallas_call(
        functools.partial(backward_kernel, sizes, hits_all, points_all),
        out_shape=(half, half),
        in_specs=[VMEM] * 13,
        out_specs=(VMEM, VMEM),
        scratch_shapes=[
            pltpu.VMEM((dim, hits), f32),
            pltpu.VMEM((blocks, block_rows, 128), f32),
            pltpu.VMEM((8 * blocks, 128), f32),
        ],
        compiler_params=PARAMS,
        name="pairs_backward",
    )(pay_own, own, xb, yb, aux, slope, ht, last, wt, head, rows_far, *sums)

    total = keep + swap(send, core)
    mine = total[0]
    arrived = [swap(total[r + 1], a, b) for r, (a, b) in enumerate(zip(flat_masks, line_masks))]
    mine = (mine + arrived[0]) + (arrived[1] + arrived[2])
    arrived = [swap(mine, line_masks[r], flat_masks[r]) for r in (1, 0, 2)]
    mine = (mine + arrived[0]) + (arrived[1] + arrived[2])
    for m in others:
        mine = mine + swap(mine, m)
    quarter = [mine] + [swap(mine, a, b) for a, b in zip(flat_masks, line_masks)]
    far = [swap(block, core) for block in quarter]

    weights = jax.ShapeDtypeStruct((blocks, layers * width // blocks, width), f32)
    gw, near_ext = pl.pallas_call(
        functools.partial(place_near_kernel, sizes),
        out_shape=(weights, jax.ShapeDtypeStruct((blocks // 2, 8, 128), f32)),
        in_specs=[VMEM] * 4,
        out_specs=(HBM, VMEM),
        scratch_shapes=[pltpu.SemaphoreType.DMA((blocks,))],
        compiler_params=PARAMS,
        cost_estimate=pl.CostEstimate(flops=0, bytes_accessed=4 * layers * width * width, transcendentals=0),
        name="place_near",
    )(*quarter)
    gw, gb, gc, gbeta, loss = pl.pallas_call(
        functools.partial(place_far_kernel, sizes),
        out_shape=(
            weights,
            jax.ShapeDtypeStruct((layers, width), f32),
            jax.ShapeDtypeStruct((dim, width), f32),
            jax.ShapeDtypeStruct((1, width), f32),
            jax.ShapeDtypeStruct((1, 1), f32),
        ),
        in_specs=[VMEM] * 5 + [HBM],
        out_specs=(HBM,) * 5,
        scratch_shapes=[
            pltpu.VMEM((layers, width), f32),
            pltpu.VMEM((dim, width), f32),
            pltpu.VMEM((1, width), f32),
            pltpu.VMEM((1, 1), f32),
            pltpu.VMEM((blocks, 8, 128), f32),
            pltpu.SemaphoreType.DMA((blocks,)),
            pltpu.SemaphoreType.DMA((4,)),
        ],
        input_output_aliases={5: 0},
        compiler_params=PARAMS,
        name="place_far",
    )(*far, near_ext, gw)
    return (
        gw.reshape(layers, width, width),
        gb,
        gc,
        gbeta.reshape(width),
        loss.reshape(()),
    )


def solution(mesh):
    split = P(AXES)
    return jax.shard_map(
        functools.partial(on_device, mesh.shape["layer"], mesh.shape["phi"]),
        mesh=mesh,
        in_specs=(P(AXES, None), P(), P(), P(), P(), split, split, split),
        out_specs=(P(), P(), P(), P(), P()),
        check_vma=False,
    )
```

```python
import functools

import jax
import jax.numpy as jnp
from jax import lax
from jax.experimental import pallas as pl
from jax.experimental.pallas import tpu as pltpu
from jax.sharding import PartitionSpec as P

dist_eps = 0.0001
charge_floor = 0.5
AXES = ("layer", "phi")
VMEM = pl.BlockSpec(memory_space=pltpu.VMEM)
SMEM = pl.BlockSpec(memory_space=pltpu.SMEM)
HBM = pl.BlockSpec(memory_space=pltpu.HBM)
UNROLL = 16
EMBED_VMEM = 63400000
HIGH = lax.Precision.HIGHEST
PARAMS = pltpu.CompilerParams(vmem_limit_bytes=48 * 1024 * 1024)


def matmul(a, b, ca=1, cb=0, precision=None):
    return lax.dot_general(
        a, b, (((ca,), (cb,)), ((), ())), precision=precision, preferred_element_type=jnp.float32
    )


def iota(shape, dim):
    return lax.broadcasted_iota(jnp.int32, shape, dim)


def head_rows(wc_ref, wb_ref):
    dim = wc_ref.shape[0]
    width = wc_ref.shape[1]
    beta_row = jnp.broadcast_to(wb_ref[...].astype(jnp.float32).reshape(1, width), (dim, width))
    tail = jnp.where(iota((dim, width), 0) == 0, beta_row, 0.0).astype(jnp.bfloat16)
    return jnp.concatenate([wc_ref[...], tail], 0)


def flat_index(axis_sizes):
    return lax.axis_index("layer") * axis_sizes[1] + lax.axis_index("phi")


def block_places(axis_sizes):
    me = flat_index(axis_sizes)
    shift = axis_sizes[1].bit_length() - 1
    core = lax.shift_right_logical(me, shift) & 1
    flat = (lax.shift_right_logical(me, shift + 1) & 1) * 2 + (me & 1)
    line = lax.shift_right_logical(me, 1) & 3
    mine = flat + core * (line - flat)
    return (core * 4, mine), (4 - core * 4, flat + line - mine)


def embed_kernel(
    sizes,
    hit_ref, feat_ref, w_ref, b_ref, wc_ref, wb_ref, track_ref, noise_ref, pay_ref, aux_ref,
):
    dim = wc_ref.shape[0]
    hits = feat_ref.shape[0]
    points = hit_ref.shape[0]
    layers = w_ref.shape[0]
    h = feat_ref[...]
    for l in range(layers):
        a = matmul(h, w_ref[l]) + b_ref[l : l + 1, :]
        h = (a * jax.nn.sigmoid(a)).astype(jnp.bfloat16)
    xz = matmul(head_rows(wc_ref, wb_ref), h, 1, 1)
    z = xz[dim : dim + 1]
    expz = jnp.exp(z)
    spread = jnp.log1p(2.0 * expz)
    q = 0.25 * spread * spread + charge_floor
    slope = 0.5 * spread * (2.0 * expz / (1.0 + 2.0 * expz))
    beta = jax.nn.sigmoid(z)
    noise = noise_ref[...]
    label = jnp.where(noise == 0, track_ref[...], -1).astype(jnp.float32)
    rows8 = iota((8, hits), 0)
    aux_ref[0:8, :] = jnp.where(
        rows8 == 0, beta, jnp.where(rows8 == 1, slope, noise.astype(jnp.float32))
    )
    col = jnp.zeros((points, hits), jnp.int32)
    for p in range(points):
        col = jnp.where(rows8 == (p + 2) % points, hit_ref[p], col)
    sel = iota((points, hits), 1) == col
    aux_ref[8:16, :] = jnp.where(sel, 1.0, 0.0)
    lane = iota((points, 128), 1)
    row = iota((points, 128), 0)
    order = jnp.where(row < 2, row + points - 2, row - 2)
    pts = jnp.where(lane == dim + 1, (flat_index(sizes) * points + order).astype(jnp.float32), 0.0)
    for c in range(dim):
        v = jnp.sum(jnp.where(sel, xz[c : c + 1], 0.0), axis=1, keepdims=True)
        pts = jnp.where(lane == c, v, pts)
    v = jnp.sum(jnp.where(sel, q, 0.0), axis=1, keepdims=True)
    pts = jnp.where(lane == dim, v, pts)
    moved = pltpu.roll(pts, 2, 0)
    left = jnp.where(row == 0, q[:, :128], jnp.where(row == 1, label[:, :128], pts))
    right = jnp.where(row == 0, q[:, 128:], jnp.where(row == 1, label[:, 128:], moved))
    pay_ref[0:dim, :] = xz[0:dim]
    pay_ref[dim : dim + 8, 0:128] = left
    pay_ref[dim : dim + 8, 128:256] = right


def residual_kernel(
    feat_ref, w_ref, b_ref, wc_ref, wb_ref, slope_ref, ht_ref, last_ref, wt_ref, head_ref
):
    head_ref[...] = head_rows(wc_ref, wb_ref)
    layers = w_ref.shape[0]
    h = feat_ref[...]
    ht_ref[0] = h.T
    for l in range(layers):
        a = matmul(h, w_ref[l]) + b_ref[l : l + 1, :]
        sig = jax.nn.sigmoid(a)
        slope_ref[l] = sig * (1.0 + a * (1.0 - sig))
        h = (a * sig).astype(jnp.bfloat16)
        if l < layers - 1:
            ht_ref[l + 1] = h.T
            wt_ref[l] = w_ref[l + 1].T
        else:
            last_ref[...] = h


def point_tile(left, right):
    rows = iota(left.shape, 0)
    return jnp.where(rows < 2, pltpu.roll(right, 6, 0), left)


def pair_weights(dist_sq, match):
    shifted = dist_sq + dist_eps
    inv = lax.rsqrt(shifted)
    reach = jnp.maximum(1.0 - shifted * inv, 0.0)
    potential = jnp.where(match, dist_sq, reach * reach)
    weight = jnp.where(match, 2.0, -2.0 * jnp.maximum(inv - 1.0, 0.0))
    return potential, weight


def spread_kernel(pay_ref, copy_ref, own_ref, xb, yb):
    dim = xb.shape[0]
    full = xb.shape[1:]
    copy_ref[...] = pay_ref[...]
    own = pay_ref[dim : dim + 8, :]
    own = point_tile(own[:, :128], own[:, 128:])
    own_ref[...] = own
    for c in range(dim):
        xb[c] = jnp.broadcast_to(pay_ref[c : c + 1, :], full)
        yb[c] = jnp.broadcast_to(own[:, c : c + 1], full)


def pair_sums(pay_ref, own, ref, xb, yb, hit_acc, point_acc):
    dim = xb.shape[0]
    full = xb.shape[1:]
    label_b = jnp.broadcast_to(pay_ref[dim + 1 : dim + 2, :], full)
    index_b = jnp.broadcast_to(own[:, dim + 1 : dim + 2], full)
    zero = jnp.zeros(full, jnp.float32)

    def hit_side(j, acc):
        tile = ref[j, dim : dim + 8, :]
        tile = point_tile(tile[:, :128], tile[:, 128:])
        diffs = []
        dist_sq = zero
        for c in range(dim):
            diff = xb[c] - tile[:, c : c + 1]
            diffs.append(diff)
            dist_sq = dist_sq + diff * diff
        point_q = tile[:, dim : dim + 1]
        potential, weight = pair_weights(dist_sq, label_b == tile[:, dim + 1 : dim + 2])
        weight = weight * point_q
        terms = [weight * diff for diff in diffs] + [potential * point_q]
        return tuple(s + term for s, term in zip(acc, terms))

    def point_side(j, acc):
        diffs = []
        dist_sq = zero
        for c in range(dim):
            diff = yb[c] - ref[j, c : c + 1, :]
            diffs.append(diff)
            dist_sq = dist_sq + diff * diff
        hit_q = ref[j, dim : dim + 1, :]
        potential, weight = pair_weights(dist_sq, index_b == ref[j, dim + 1 : dim + 2, :])
        weight = weight * hit_q
        terms = [weight * diff for diff in diffs] + [potential * hit_q]
        return tuple(s + term[:, :128] + term[:, 128:] for s, term in zip(acc, terms))

    count = ref.shape[0]
    unroll = min(count, UNROLL)
    hit_acc = lax.fori_loop(0, count, hit_side, hit_acc, unroll=unroll)
    point_acc = lax.fori_loop(0, count, point_side, point_acc, unroll=unroll)
    return hit_acc, point_acc


def pair_kernel(parts, pay_ref, own_ref, xb, yb, *rest):
    rows, rest = rest[:parts], rest[parts:]
    hit_ref, point_ref = rest[-2:]
    if len(rest) > 2:
        sums = [tuple(ref[c] for c in range(ref.shape[0])) for ref in rest[:2]]
    else:
        sums = [(jnp.zeros(ref.shape[1:], jnp.float32),) * ref.shape[0] for ref in rest]
    own = own_ref[...]
    for ref in rows:
        sums = pair_sums(pay_ref, own, ref, xb, yb, *sums)
    for ref, values in zip((hit_ref, point_ref), sums):
        for c, value in enumerate(values):
            ref[c] = value


def backward_kernel(
    sizes, hits_all, points_all,
    pay_ref, own_ref, xb, yb, aux_ref, slope_ref, ht_ref, last_ref, wt_ref, head_ref, rows_ref, hit_ref, point_ref,
    keep_ref, send_ref, gx_ref, stack, ext,
):
    dim = xb.shape[0]
    hits = pay_ref.shape[1]
    layers = slope_ref.shape[0]
    points = own_ref.shape[0]
    own = own_ref[...]
    q_row = pay_ref[dim : dim + 1, :]
    hit_acc = tuple(hit_ref[c] for c in range(dim + 1))
    point_acc = tuple(point_ref[c] for c in range(dim + 1))
    hit_acc, point_acc = pair_sums(pay_ref, own, rows_ref, xb, yb, hit_acc, point_acc)

    pot_row = jnp.sum(hit_acc[dim], axis=0, keepdims=True)
    scaled = q_row * (1.0 / hits_all)
    for c in range(dim):
        gx_ref[c : c + 1, :] = jnp.sum(hit_acc[c], axis=0, keepdims=True) * scaled
    lane = iota((8, 128), 1)
    own_q = own[:, dim : dim + 1] * (1.0 / hits_all)
    grads = jnp.where(lane == dim + 1, 1.0, 0.0)
    for c in range(dim):
        v = jnp.sum(point_acc[c], axis=1, keepdims=True) * own_q
        grads = jnp.where(lane == c, v, grads)
    v = jnp.sum(point_acc[dim], axis=1, keepdims=True) * (1.0 / hits_all)
    grads = jnp.where(lane == dim, v, grads)
    added = matmul(grads, aux_ref[8:16, :], 0, 0, HIGH)

    beta = aux_ref[0:1, :]
    noise = aux_ref[2:3, :]
    count = added[dim + 1 : dim + 2]
    grad_q = pot_row * (1.0 / hits_all) + added[dim : dim + 1]
    grad_b = noise * (1.0 / hits_all) - count * (1.0 / points_all)
    grad_z = grad_q * aux_ref[1:2, :] + grad_b * beta * (1.0 - beta)
    per_hit = q_row * pot_row * (1.0 / hits_all) + noise * beta * (1.0 / hits_all)
    per_hit = per_hit - count * beta * (1.0 / points_all)
    loss = jnp.sum(per_hit, axis=1, keepdims=True) + points * 1.0 / points_all

    grad_x = gx_ref[...] + added[0:dim]
    tail = jnp.where(iota((dim, hits), 0) == 0, grad_z, 0.0)
    low = jnp.concatenate([grad_x, tail], 0).astype(jnp.bfloat16)
    head = head_ref[...]
    grad_head = matmul(low, last_ref[...])
    up = matmul(low, head, 0, 0)
    ext[...] = jnp.zeros(ext.shape, jnp.float32)
    cols = [slice(0, 128), slice(128, 256)]
    base = 2 * layers
    for h, col in enumerate(cols):
        ext[base + h * dim : base + (h + 1) * dim, :] = grad_head[0:dim, col]
        ext[base + 2 * dim + h : base + 2 * dim + h + 1, :] = grad_head[dim : dim + 1, col]
    ext[base + 2 * dim + 2 : base + 2 * dim + 3, :] = jnp.broadcast_to(loss, (1, 128))
    blocks = stack.shape[0]
    rows = layers * hits // blocks
    per_layer = blocks // layers
    for l in range(layers - 1, -1, -1):
        err = (up * slope_ref[l]).astype(jnp.bfloat16)
        if l > 0:
            up = matmul(err, wt_ref[l - 1])
        grad_w = matmul(ht_ref[l], err)
        bias = jnp.sum(err.astype(jnp.float32), axis=0, keepdims=True)
        for h, col in enumerate(cols):
            ext[h * layers + l : h * layers + l + 1, :] = bias[:, col]
            for s in range(per_layer):
                stack[l * per_layer + s, h * rows : (h + 1) * rows, :] = grad_w[
                    s * rows : (s + 1) * rows, col
                ]
    for b in range(blocks):
        stack[b, 2 * rows : 2 * rows + 8, :] = ext[8 * b : 8 * b + 8, :]
    for out_ref, (first, place) in zip((keep_ref, send_ref), block_places(sizes)):
        for j in range(blocks // 2):
            out_ref[j] = stack[first + jnp.bitwise_xor(place, j)]


def place_copies(blocks, first, place, gw_ref, sems):
    rows = gw_ref.shape[1]
    copies = []
    for r, block in enumerate(blocks):
        slot = first + jnp.bitwise_xor(place, r)
        for h in range(2):
            copies.append(
                pltpu.make_async_copy(
                    block.at[pl.ds(h * rows, rows)],
                    gw_ref.at[slot, :, pl.ds(h * 128, 128)],
                    sems.at[2 * r + h],
                )
            )
    for copy in copies:
        copy.start()
    return copies


def place_near_kernel(sizes, *refs):
    blocks = refs[:4]
    gw_ref, ext_ref, sems = refs[4:]
    rows = gw_ref.shape[1]
    copies = place_copies(blocks, *block_places(sizes)[0], gw_ref, sems)
    for r, block in enumerate(blocks):
        ext_ref[r] = block[2 * rows :, :]
    for copy in copies:
        copy.wait()


def place_far_kernel(sizes, *refs):
    blocks, (near_ref, _, gw_ref), rest = refs[:4], refs[4:7], refs[7:]
    outs, scratch, (ext, sems, small_sems) = rest[:4], rest[4:8], rest[8:]
    gb_ref, gc_ref, gbeta_ref, loss_ref = scratch
    rows = gw_ref.shape[1]
    half = len(blocks)
    dim = gc_ref.shape[0]
    layers = gb_ref.shape[0]
    (near_first, near_place), (far_first, far_place) = block_places(sizes)
    copies = place_copies(blocks, far_first, far_place, gw_ref, sems)
    for r in range(half):
        ext[near_first + jnp.bitwise_xor(near_place, r)] = near_ref[r]
        ext[far_first + jnp.bitwise_xor(far_place, r)] = blocks[r][2 * rows :, :]
    flat = jnp.concatenate([ext[b] for b in range(2 * half)], 0)
    base = 2 * layers
    for h, col in enumerate([slice(0, 128), slice(128, 256)]):
        gb_ref[:, col] = flat[h * layers : (h + 1) * layers]
        gc_ref[:, col] = flat[base + h * dim : base + (h + 1) * dim]
        gbeta_ref[:, col] = flat[base + 2 * dim + h : base + 2 * dim + h + 1]
    loss_ref[...] = flat[base + 2 * dim + 2 : base + 2 * dim + 3, 0:1]
    for i in range(4):
        copies.append(pltpu.make_async_copy(scratch[i], outs[i], small_sems.at[i]))
        copies[-1].start()
    for copy in copies:
        copy.wait()


def bits_of(size):
    return [1 << t for t in range(size.bit_length() - 1)]


def on_device(layer_size, phi_size, features, w_layers, b_layers, w_coord, w_beta, point_hit, track, noise):
    ndev = layer_size * phi_size
    hits, width = features.shape
    layers = w_layers.shape[0]
    dim = w_coord.shape[0]
    points = point_hit.shape[0]
    hits_all = hits * ndev * 1.0
    points_all = points * ndev * 1.0
    f32 = jnp.float32
    core = phi_size
    plane = [1, 2 * phi_size]
    others = [b for b in bits_of(ndev) if b != core and b not in plane]

    line = others[:2]
    others = others[2:]
    flat_masks = [plane[0], plane[1], plane[0] ^ plane[1]]
    line_masks = [line[0], line[1], line[0] ^ line[1]]

    def swap(x, mask, other=None):
        masks = (mask, mask if other is None else other)
        return lax.ppermute(x, AXES, [(i, i ^ masks[i // core & 1]) for i in range(ndev)])

    sizes = (layer_size, phi_size)
    track = track.reshape(1, hits)
    noise = noise.reshape(1, hits)
    low = jnp.bfloat16

    pay, aux = pl.pallas_call(
        functools.partial(embed_kernel, sizes),
        out_shape=(
            jax.ShapeDtypeStruct((dim + 8, hits), f32),
            jax.ShapeDtypeStruct((16, hits), f32),
        ),
        in_specs=[SMEM] + [VMEM] * 7,
        out_specs=(VMEM,) * 2,
        compiler_params=pltpu.CompilerParams(vmem_limit_bytes=EMBED_VMEM),
        name="embed",
    )(point_hit, features, w_layers, b_layers, w_coord, w_beta, track, noise)

    def residuals(early):
        return pl.pallas_call(
            residual_kernel,
            out_shape=(
                jax.ShapeDtypeStruct((layers, hits, width), f32),
                jax.ShapeDtypeStruct((layers, width, hits), low),
                jax.ShapeDtypeStruct((hits, width), low),
                jax.ShapeDtypeStruct((layers - 1, width, width), low),
                jax.ShapeDtypeStruct((2 * dim, width), low),
            ),
            in_specs=[VMEM] * 5,
            out_specs=(VMEM,) * 5,
            compiler_params=PARAMS,
            cost_estimate=pl.CostEstimate(
                flops=20 * layers * hits * width, bytes_accessed=6 * layers * hits * width,
                transcendentals=layers * hits * width,
            ),
            name="residuals",
        )(*early)

    pay_own, own, xb, yb = pl.pallas_call(
        spread_kernel,
        out_shape=(
            jax.ShapeDtypeStruct((dim + 8, hits), f32),
            jax.ShapeDtypeStruct((8, 128), f32),
            jax.ShapeDtypeStruct((dim, 8, hits), f32),
            jax.ShapeDtypeStruct((dim, 8, hits), f32),
        ),
        in_specs=[VMEM],
        out_specs=(VMEM,) * 4,
        compiler_params=PARAMS,
        cost_estimate=pl.CostEstimate(flops=0, bytes_accessed=80 * dim * hits, transcendentals=0),
        name="spread",
    )(pay)
    rows_all = pay[None]
    kept = pay_own[None]
    for m in others:
        kept = rows_all = jnp.concatenate([kept, swap(rows_all, m)], 0)
    arrived = [swap(rows_all, m) for m in (line[0], line[0] ^ line[1], line[1])]
    rows_all = jnp.concatenate([kept] + arrived, 0)
    rows_all, *early = lax.optimization_barrier((rows_all, features, w_layers, b_layers))
    arrived = [swap(rows_all, m) for m in (plane[0], plane[0] ^ plane[1], plane[1])]
    first_far = swap(rows_all, core)
    rows = jnp.concatenate(arrived, 0)
    slope, ht, last, wt, head = residuals(early + [w_coord, w_beta])
    rows, first_far, slope = lax.optimization_barrier((rows, first_far, slope))
    rows_far = swap(rows, core)

    partial_sums = (
        jax.ShapeDtypeStruct((dim + 1, 8, hits), f32),
        jax.ShapeDtypeStruct((dim + 1, 8, 128), f32),
    )

    def pairs(rows, sums=()):
        count = sum(r.shape[0] for r in rows)
        return pl.pallas_call(
            functools.partial(pair_kernel, len(rows)),
            out_shape=partial_sums,
            in_specs=[VMEM] * (4 + len(rows) + len(sums)),
            out_specs=(VMEM, VMEM),
            compiler_params=PARAMS,
            cost_estimate=pl.CostEstimate(
                flops=200 * points * hits * count, bytes_accessed=count * hits * 64,
                transcendentals=2 * points * hits * count,
            ),
            name="pairs",
        )(pay_own, own, xb, yb, *rows, *sums)

    sums = pairs([rows_all, first_far, rows])

    blocks = 8
    block_rows = 2 * (layers * width // blocks) + 8
    half = jax.ShapeDtypeStruct((blocks // 2, block_rows, 128), f32)
    keep, send = pl.pallas_call(
        functools.partial(backward_kernel, sizes, hits_all, points_all),
        out_shape=(half, half),
        in_specs=[VMEM] * 13,
        out_specs=(VMEM, VMEM),
        scratch_shapes=[
            pltpu.VMEM((dim, hits), f32),
            pltpu.VMEM((blocks, block_rows, 128), f32),
            pltpu.VMEM((8 * blocks, 128), f32),
        ],
        compiler_params=PARAMS,
        name="pairs_backward",
    )(pay_own, own, xb, yb, aux, slope, ht, last, wt, head, rows_far, *sums)

    total = keep + swap(send, core)
    mine = total[0]
    arrived = [swap(total[r + 1], a, b) for r, (a, b) in enumerate(zip(flat_masks, line_masks))]
    mine = (mine + arrived[0]) + (arrived[1] + arrived[2])
    arrived = [swap(mine, line_masks[r], flat_masks[r]) for r in (1, 0, 2)]
    mine = (mine + arrived[0]) + (arrived[1] + arrived[2])
    for m in others:
        mine = mine + swap(mine, m)
    quarter = [mine] + [swap(mine, a, b) for a, b in zip(flat_masks, line_masks)]
    far = [swap(block, core) for block in quarter]

    weights = jax.ShapeDtypeStruct((blocks, layers * width // blocks, width), f32)
    gw, near_ext = pl.pallas_call(
        functools.partial(place_near_kernel, sizes),
        out_shape=(weights, jax.ShapeDtypeStruct((blocks // 2, 8, 128), f32)),
        in_specs=[VMEM] * 4,
        out_specs=(HBM, VMEM),
        scratch_shapes=[pltpu.SemaphoreType.DMA((blocks,))],
        compiler_params=PARAMS,
        cost_estimate=pl.CostEstimate(flops=0, bytes_accessed=4 * layers * width * width, transcendentals=0),
        name="place_near",
    )(*quarter)
    gw, gb, gc, gbeta, loss = pl.pallas_call(
        functools.partial(place_far_kernel, sizes),
        out_shape=(
            weights,
            jax.ShapeDtypeStruct((layers, width), f32),
            jax.ShapeDtypeStruct((dim, width), f32),
            jax.ShapeDtypeStruct((1, width), f32),
            jax.ShapeDtypeStruct((1, 1), f32),
        ),
        in_specs=[VMEM] * 5 + [HBM],
        out_specs=(HBM,) * 5,
        scratch_shapes=[
            pltpu.VMEM((layers, width), f32),
            pltpu.VMEM((dim, width), f32),
            pltpu.VMEM((1, width), f32),
            pltpu.VMEM((1, 1), f32),
            pltpu.VMEM((blocks, 8, 128), f32),
            pltpu.SemaphoreType.DMA((blocks,)),
            pltpu.SemaphoreType.DMA((4,)),
        ],
        input_output_aliases={5: 0},
        compiler_params=PARAMS,
        name="place_far",
    )(*far, near_ext, gw)
    return (
        gw.reshape(layers, width, width),
        gb,
        gc,
        gbeta.reshape(width),
        loss.reshape(()),
    )


def solution(mesh):
    split = P(AXES)
    return jax.shard_map(
        functools.partial(on_device, mesh.shape["layer"], mesh.shape["phi"]),
        mesh=mesh,
        in_specs=(P(AXES, None), P(), P(), P(), P(), split, split, split),
        out_specs=(P(), P(), P(), P(), P()),
        check_vma=False,
    )
```

```python
import functools

import jax
import jax.numpy as jnp
from jax import lax
from jax.experimental import pallas as pl
from jax.experimental.pallas import tpu as pltpu
from jax.sharding import PartitionSpec as P

dist_eps = 0.0001
charge_floor = 0.5
AXES = ("layer", "phi")
VMEM = pl.BlockSpec(memory_space=pltpu.VMEM)
SMEM = pl.BlockSpec(memory_space=pltpu.SMEM)
HBM = pl.BlockSpec(memory_space=pltpu.HBM)
UNROLL = 16
EMBED_VMEM = 63400000
HIGH = lax.Precision.HIGHEST
PARAMS = pltpu.CompilerParams(vmem_limit_bytes=48 * 1024 * 1024)


def matmul(a, b, ca=1, cb=0, precision=None):
    return lax.dot_general(
        a, b, (((ca,), (cb,)), ((), ())), precision=precision, preferred_element_type=jnp.float32
    )


def iota(shape, dim):
    return lax.broadcasted_iota(jnp.int32, shape, dim)


def head_rows(wc_ref, wb_ref):
    dim = wc_ref.shape[0]
    width = wc_ref.shape[1]
    beta_row = jnp.broadcast_to(wb_ref[...].astype(jnp.float32).reshape(1, width), (dim, width))
    tail = jnp.where(iota((dim, width), 0) == 0, beta_row, 0.0).astype(jnp.bfloat16)
    return jnp.concatenate([wc_ref[...], tail], 0)


def flat_index(axis_sizes):
    return lax.axis_index("layer") * axis_sizes[1] + lax.axis_index("phi")


def block_places(axis_sizes):
    me = flat_index(axis_sizes)
    shift = axis_sizes[1].bit_length() - 1
    core = lax.shift_right_logical(me, shift) & 1
    flat = (lax.shift_right_logical(me, shift + 1) & 1) * 2 + (me & 1)
    line = lax.shift_right_logical(me, 1) & 3
    mine = flat + core * (line - flat)
    return (core * 4, mine), (4 - core * 4, flat + line - mine)


def embed_kernel(
    sizes,
    hit_ref, feat_ref, w_ref, b_ref, wc_ref, wb_ref, track_ref, noise_ref, pay_ref, aux_ref,
):
    dim = wc_ref.shape[0]
    hits = feat_ref.shape[0]
    points = hit_ref.shape[0]
    layers = w_ref.shape[0]
    h = feat_ref[...]
    for l in range(layers):
        a = matmul(h, w_ref[l]) + b_ref[l : l + 1, :]
        h = (a * jax.nn.sigmoid(a)).astype(jnp.bfloat16)
    xz = matmul(head_rows(wc_ref, wb_ref), h, 1, 1)
    z = xz[dim : dim + 1]
    expz = jnp.exp(z)
    spread = jnp.log1p(2.0 * expz)
    q = 0.25 * spread * spread + charge_floor
    slope = 0.5 * spread * (2.0 * expz / (1.0 + 2.0 * expz))
    beta = jax.nn.sigmoid(z)
    noise = noise_ref[...]
    label = jnp.where(noise == 0, track_ref[...], -1).astype(jnp.float32)
    rows8 = iota((8, hits), 0)
    aux_ref[0:8, :] = jnp.where(
        rows8 == 0, beta, jnp.where(rows8 == 1, slope, noise.astype(jnp.float32))
    )
    col = jnp.zeros((points, hits), jnp.int32)
    for p in range(points):
        col = jnp.where(rows8 == (p + 2) % points, hit_ref[p], col)
    sel = iota((points, hits), 1) == col
    aux_ref[8:16, :] = jnp.where(sel, 1.0, 0.0)
    lane = iota((points, 128), 1)
    row = iota((points, 128), 0)
    order = jnp.where(row < 2, row + points - 2, row - 2)
    pts = jnp.where(lane == dim + 1, (flat_index(sizes) * points + order).astype(jnp.float32), 0.0)
    for c in range(dim):
        v = jnp.sum(jnp.where(sel, xz[c : c + 1], 0.0), axis=1, keepdims=True)
        pts = jnp.where(lane == c, v, pts)
    v = jnp.sum(jnp.where(sel, q, 0.0), axis=1, keepdims=True)
    pts = jnp.where(lane == dim, v, pts)
    moved = pltpu.roll(pts, 2, 0)
    left = jnp.where(row == 0, q[:, :128], jnp.where(row == 1, label[:, :128], pts))
    right = jnp.where(row == 0, q[:, 128:], jnp.where(row == 1, label[:, 128:], moved))
    pay_ref[0:dim, :] = xz[0:dim]
    pay_ref[dim : dim + 8, 0:128] = left
    pay_ref[dim : dim + 8, 128:256] = right


def residual_kernel(
    feat_ref, w_ref, b_ref, wc_ref, wb_ref, slope_ref, ht_ref, last_ref, wt_ref, head_ref
):
    head_ref[...] = head_rows(wc_ref, wb_ref)
    layers = w_ref.shape[0]
    h = feat_ref[...]
    ht_ref[0] = h.T
    for l in range(layers):
        a = matmul(h, w_ref[l]) + b_ref[l : l + 1, :]
        sig = jax.nn.sigmoid(a)
        slope_ref[l] = sig * (1.0 + a * (1.0 - sig))
        h = (a * sig).astype(jnp.bfloat16)
        if l < layers - 1:
            ht_ref[l + 1] = h.T
            wt_ref[l] = w_ref[l + 1].T
        else:
            last_ref[...] = h


def point_tile(left, right):
    rows = iota(left.shape, 0)
    return jnp.where(rows < 2, pltpu.roll(right, 6, 0), left)


def pair_weights(dist_sq, match):
    shifted = dist_sq + dist_eps
    inv = lax.rsqrt(shifted)
    reach = jnp.maximum(1.0 - shifted * inv, 0.0)
    potential = jnp.where(match, dist_sq, reach * reach)
    weight = jnp.where(match, 2.0, -2.0 * jnp.maximum(inv - 1.0, 0.0))
    return potential, weight


def spread_kernel(pay_ref, copy_ref, own_ref, xb, yb):
    dim = xb.shape[0]
    full = xb.shape[1:]
    copy_ref[...] = pay_ref[...]
    own = pay_ref[dim : dim + 8, :]
    own = point_tile(own[:, :128], own[:, 128:])
    own_ref[...] = own
    for c in range(dim):
        xb[c] = jnp.broadcast_to(pay_ref[c : c + 1, :], full)
        yb[c] = jnp.broadcast_to(own[:, c : c + 1], full)


def pair_sums(pay_ref, own, ref, xb, yb, hit_acc, point_acc):
    dim = xb.shape[0]
    full = xb.shape[1:]
    label_b = jnp.broadcast_to(pay_ref[dim + 1 : dim + 2, :], full)
    index_b = jnp.broadcast_to(own[:, dim + 1 : dim + 2], full)
    zero = jnp.zeros(full, jnp.float32)

    def hit_side(j, acc):
        tile = ref[j, dim : dim + 8, :]
        tile = point_tile(tile[:, :128], tile[:, 128:])
        diffs = []
        dist_sq = zero
        for c in range(dim):
            diff = xb[c] - tile[:, c : c + 1]
            diffs.append(diff)
            dist_sq = dist_sq + diff * diff
        point_q = tile[:, dim : dim + 1]
        potential, weight = pair_weights(dist_sq, label_b == tile[:, dim + 1 : dim + 2])
        weight = weight * point_q
        terms = [weight * diff for diff in diffs] + [potential * point_q]
        return tuple(s + term for s, term in zip(acc, terms))

    def point_side(j, acc):
        diffs = []
        dist_sq = zero
        for c in range(dim):
            diff = yb[c] - ref[j, c : c + 1, :]
            diffs.append(diff)
            dist_sq = dist_sq + diff * diff
        hit_q = ref[j, dim : dim + 1, :]
        potential, weight = pair_weights(dist_sq, index_b == ref[j, dim + 1 : dim + 2, :])
        weight = weight * hit_q
        terms = [weight * diff for diff in diffs] + [potential * hit_q]
        return tuple(s + term[:, :128] + term[:, 128:] for s, term in zip(acc, terms))

    count = ref.shape[0]
    unroll = min(count, UNROLL)
    hit_acc = lax.fori_loop(0, count, hit_side, hit_acc, unroll=unroll)
    point_acc = lax.fori_loop(0, count, point_side, point_acc, unroll=unroll)
    return hit_acc, point_acc


def pair_kernel(parts, pay_ref, own_ref, xb, yb, *rest):
    rows, rest = rest[:parts], rest[parts:]
    hit_ref, point_ref = rest[-2:]
    if len(rest) > 2:
        sums = [tuple(ref[c] for c in range(ref.shape[0])) for ref in rest[:2]]
    else:
        sums = [(jnp.zeros(ref.shape[1:], jnp.float32),) * ref.shape[0] for ref in rest]
    own = own_ref[...]
    for ref in rows:
        sums = pair_sums(pay_ref, own, ref, xb, yb, *sums)
    for ref, values in zip((hit_ref, point_ref), sums):
        for c, value in enumerate(values):
            ref[c] = value


def backward_kernel(
    sizes, hits_all, points_all,
    pay_ref, own_ref, xb, yb, aux_ref, slope_ref, ht_ref, last_ref, wt_ref, head_ref, rows_ref, hit_ref, point_ref,
    keep_ref, send_ref, gx_ref, stack, ext,
):
    dim = xb.shape[0]
    hits = pay_ref.shape[1]
    layers = slope_ref.shape[0]
    points = own_ref.shape[0]
    own = own_ref[...]
    q_row = pay_ref[dim : dim + 1, :]
    hit_acc = tuple(hit_ref[c] for c in range(dim + 1))
    point_acc = tuple(point_ref[c] for c in range(dim + 1))
    hit_acc, point_acc = pair_sums(pay_ref, own, rows_ref, xb, yb, hit_acc, point_acc)

    pot_row = jnp.sum(hit_acc[dim], axis=0, keepdims=True)
    scaled = q_row * (1.0 / hits_all)
    for c in range(dim):
        gx_ref[c : c + 1, :] = jnp.sum(hit_acc[c], axis=0, keepdims=True) * scaled
    lane = iota((8, 128), 1)
    own_q = own[:, dim : dim + 1] * (1.0 / hits_all)
    grads = jnp.where(lane == dim + 1, 1.0, 0.0)
    for c in range(dim):
        v = jnp.sum(point_acc[c], axis=1, keepdims=True) * own_q
        grads = jnp.where(lane == c, v, grads)
    v = jnp.sum(point_acc[dim], axis=1, keepdims=True) * (1.0 / hits_all)
    grads = jnp.where(lane == dim, v, grads)
    added = matmul(grads, aux_ref[8:16, :], 0, 0, HIGH)

    beta = aux_ref[0:1, :]
    noise = aux_ref[2:3, :]
    count = added[dim + 1 : dim + 2]
    grad_q = pot_row * (1.0 / hits_all) + added[dim : dim + 1]
    grad_b = noise * (1.0 / hits_all) - count * (1.0 / points_all)
    grad_z = grad_q * aux_ref[1:2, :] + grad_b * beta * (1.0 - beta)
    per_hit = q_row * pot_row * (1.0 / hits_all) + noise * beta * (1.0 / hits_all)
    per_hit = per_hit - count * beta * (1.0 / points_all)
    loss = jnp.sum(per_hit, axis=1, keepdims=True) + points * 1.0 / points_all

    grad_x = gx_ref[...] + added[0:dim]
    tail = jnp.where(iota((dim, hits), 0) == 0, grad_z, 0.0)
    low = jnp.concatenate([grad_x, tail], 0).astype(jnp.bfloat16)
    head = head_ref[...]
    grad_head = matmul(low, last_ref[...])
    up = matmul(low, head, 0, 0)
    ext[...] = jnp.zeros(ext.shape, jnp.float32)
    cols = [slice(0, 128), slice(128, 256)]
    base = 2 * layers
    for h, col in enumerate(cols):
        ext[base + h * dim : base + (h + 1) * dim, :] = grad_head[0:dim, col]
        ext[base + 2 * dim + h : base + 2 * dim + h + 1, :] = grad_head[dim : dim + 1, col]
    ext[base + 2 * dim + 2 : base + 2 * dim + 3, :] = jnp.broadcast_to(loss, (1, 128))
    blocks = stack.shape[0]
    rows = layers * hits // blocks
    per_layer = blocks // layers
    for l in range(layers - 1, -1, -1):
        err = (up * slope_ref[l]).astype(jnp.bfloat16)
        if l > 0:
            up = matmul(err, wt_ref[l - 1])
        grad_w = matmul(ht_ref[l], err)
        bias = jnp.sum(err.astype(jnp.float32), axis=0, keepdims=True)
        for h, col in enumerate(cols):
            ext[h * layers + l : h * layers + l + 1, :] = bias[:, col]
            for s in range(per_layer):
                stack[l * per_layer + s, h * rows : (h + 1) * rows, :] = grad_w[
                    s * rows : (s + 1) * rows, col
                ]
    for b in range(blocks):
        stack[b, 2 * rows : 2 * rows + 8, :] = ext[8 * b : 8 * b + 8, :]
    for out_ref, (first, place) in zip((keep_ref, send_ref), block_places(sizes)):
        for j in range(blocks // 2):
            out_ref[j] = stack[first + jnp.bitwise_xor(place, j)]


def place_copies(blocks, first, place, gw_ref, sems):
    rows = gw_ref.shape[1]
    copies = []
    for r, block in enumerate(blocks):
        slot = first + jnp.bitwise_xor(place, r)
        for h in range(2):
            copies.append(
                pltpu.make_async_copy(
                    block.at[pl.ds(h * rows, rows)],
                    gw_ref.at[slot, :, pl.ds(h * 128, 128)],
                    sems.at[2 * r + h],
                )
            )
    for copy in copies:
        copy.start()
    return copies


def place_near_kernel(sizes, *refs):
    blocks = refs[:4]
    gw_ref, ext_ref, sems = refs[4:]
    rows = gw_ref.shape[1]
    copies = place_copies(blocks, *block_places(sizes)[0], gw_ref, sems)
    for r, block in enumerate(blocks):
        ext_ref[r] = block[2 * rows :, :]
    for copy in copies:
        copy.wait()


def place_far_kernel(sizes, *refs):
    blocks, (near_ref, _, gw_ref), rest = refs[:4], refs[4:7], refs[7:]
    outs, scratch, (ext, sems, small_sems) = rest[:4], rest[4:8], rest[8:]
    gb_ref, gc_ref, gbeta_ref, loss_ref = scratch
    rows = gw_ref.shape[1]
    half = len(blocks)
    dim = gc_ref.shape[0]
    layers = gb_ref.shape[0]
    (near_first, near_place), (far_first, far_place) = block_places(sizes)
    copies = place_copies(blocks, far_first, far_place, gw_ref, sems)
    for r in range(half):
        ext[near_first + jnp.bitwise_xor(near_place, r)] = near_ref[r]
        ext[far_first + jnp.bitwise_xor(far_place, r)] = blocks[r][2 * rows :, :]
    flat = jnp.concatenate([ext[b] for b in range(2 * half)], 0)
    base = 2 * layers
    for h, col in enumerate([slice(0, 128), slice(128, 256)]):
        gb_ref[:, col] = flat[h * layers : (h + 1) * layers]
        gc_ref[:, col] = flat[base + h * dim : base + (h + 1) * dim]
        gbeta_ref[:, col] = flat[base + 2 * dim + h : base + 2 * dim + h + 1]
    loss_ref[...] = flat[base + 2 * dim + 2 : base + 2 * dim + 3, 0:1]
    for i in range(4):
        copies.append(pltpu.make_async_copy(scratch[i], outs[i], small_sems.at[i]))
        copies[-1].start()
    for copy in copies:
        copy.wait()


def bits_of(size):
    return [1 << t for t in range(size.bit_length() - 1)]


def on_device(layer_size, phi_size, features, w_layers, b_layers, w_coord, w_beta, point_hit, track, noise):
    ndev = layer_size * phi_size
    hits, width = features.shape
    layers = w_layers.shape[0]
    dim = w_coord.shape[0]
    points = point_hit.shape[0]
    hits_all = hits * ndev * 1.0
    points_all = points * ndev * 1.0
    f32 = jnp.float32
    core = phi_size
    plane = [1, 2 * phi_size]
    others = [b for b in bits_of(ndev) if b != core and b not in plane]

    line = others[:2]
    others = others[2:]
    flat_masks = [plane[0], plane[1], plane[0] ^ plane[1]]
    line_masks = [line[0], line[1], line[0] ^ line[1]]

    def swap(x, mask, other=None):
        masks = (mask, mask if other is None else other)
        return lax.ppermute(x, AXES, [(i, i ^ masks[i // core & 1]) for i in range(ndev)])

    sizes = (layer_size, phi_size)
    track = track.reshape(1, hits)
    noise = noise.reshape(1, hits)
    low = jnp.bfloat16

    pay, aux = pl.pallas_call(
        functools.partial(embed_kernel, sizes),
        out_shape=(
            jax.ShapeDtypeStruct((dim + 8, hits), f32),
            jax.ShapeDtypeStruct((16, hits), f32),
        ),
        in_specs=[SMEM] + [VMEM] * 7,
        out_specs=(VMEM,) * 2,
        compiler_params=pltpu.CompilerParams(vmem_limit_bytes=EMBED_VMEM),
        name="embed",
    )(point_hit, features, w_layers, b_layers, w_coord, w_beta, track, noise)

    def residuals(early):
        return pl.pallas_call(
            residual_kernel,
            out_shape=(
                jax.ShapeDtypeStruct((layers, hits, width), f32),
                jax.ShapeDtypeStruct((layers, width, hits), low),
                jax.ShapeDtypeStruct((hits, width), low),
                jax.ShapeDtypeStruct((layers - 1, width, width), low),
                jax.ShapeDtypeStruct((2 * dim, width), low),
            ),
            in_specs=[VMEM] * 5,
            out_specs=(VMEM,) * 5,
            compiler_params=PARAMS,
            cost_estimate=pl.CostEstimate(
                flops=20 * layers * hits * width, bytes_accessed=6 * layers * hits * width,
                transcendentals=layers * hits * width,
            ),
            name="residuals",
        )(*early)

    pay_own, own, xb, yb = pl.pallas_call(
        spread_kernel,
        out_shape=(
            jax.ShapeDtypeStruct((dim + 8, hits), f32),
            jax.ShapeDtypeStruct((8, 128), f32),
            jax.ShapeDtypeStruct((dim, 8, hits), f32),
            jax.ShapeDtypeStruct((dim, 8, hits), f32),
        ),
        in_specs=[VMEM],
        out_specs=(VMEM,) * 4,
        compiler_params=PARAMS,
        cost_estimate=pl.CostEstimate(flops=0, bytes_accessed=80 * dim * hits, transcendentals=0),
        name="spread",
    )(pay)
    rows_all = pay[None]
    kept = pay_own[None]
    for m in others:
        kept = rows_all = jnp.concatenate([kept, swap(rows_all, m)], 0)
    arrived = [swap(rows_all, m) for m in (line[0], line[0] ^ line[1], line[1])]
    rows_all = jnp.concatenate([kept] + arrived, 0)
    rows_all, *early = lax.optimization_barrier((rows_all, features, w_layers, b_layers))
    arrived = [swap(rows_all, m) for m in (plane[0], plane[0] ^ plane[1], plane[1])]
    first_far = swap(rows_all, core)
    rows = jnp.concatenate(arrived, 0)
    slope, ht, last, wt, head = residuals(early + [w_coord, w_beta])
    rows, first_far, slope = lax.optimization_barrier((rows, first_far, slope))
    rows_far = swap(rows, core)

    partial_sums = (
        jax.ShapeDtypeStruct((dim + 1, 8, hits), f32),
        jax.ShapeDtypeStruct((dim + 1, 8, 128), f32),
    )

    def pairs(rows, sums=()):
        count = sum(r.shape[0] for r in rows)
        return pl.pallas_call(
            functools.partial(pair_kernel, len(rows)),
            out_shape=partial_sums,
            in_specs=[VMEM] * (4 + len(rows) + len(sums)),
            out_specs=(VMEM, VMEM),
            compiler_params=PARAMS,
            cost_estimate=pl.CostEstimate(
                flops=200 * points * hits * count, bytes_accessed=count * hits * 64,
                transcendentals=2 * points * hits * count,
            ),
            name="pairs",
        )(pay_own, own, xb, yb, *rows, *sums)

    sums = pairs([rows_all, first_far, rows])

    blocks = 8
    block_rows = 2 * (layers * width // blocks) + 8
    half = jax.ShapeDtypeStruct((blocks // 2, block_rows, 128), f32)
    keep, send = pl.pallas_call(
        functools.partial(backward_kernel, sizes, hits_all, points_all),
        out_shape=(half, half),
        in_specs=[VMEM] * 13,
        out_specs=(VMEM, VMEM),
        scratch_shapes=[
            pltpu.VMEM((dim, hits), f32),
            pltpu.VMEM((blocks, block_rows, 128), f32),
            pltpu.VMEM((8 * blocks, 128), f32),
        ],
        compiler_params=PARAMS,
        name="pairs_backward",
    )(pay_own, own, xb, yb, aux, slope, ht, last, wt, head, rows_far, *sums)

    total = keep + swap(send, core)
    mine = total[0]
    arrived = [swap(total[r + 1], a, b) for r, (a, b) in enumerate(zip(flat_masks, line_masks))]
    mine = (mine + arrived[0]) + (arrived[1] + arrived[2])
    arrived = [swap(mine, line_masks[r], flat_masks[r]) for r in (0, 2, 1)]
    mine = (mine + arrived[0]) + (arrived[1] + arrived[2])
    for m in others:
        mine = mine + swap(mine, m)
    quarter = [mine] + [swap(mine, a, b) for a, b in zip(flat_masks, line_masks)]
    far = [swap(block, core) for block in quarter]

    weights = jax.ShapeDtypeStruct((blocks, layers * width // blocks, width), f32)
    gw, near_ext = pl.pallas_call(
        functools.partial(place_near_kernel, sizes),
        out_shape=(weights, jax.ShapeDtypeStruct((blocks // 2, 8, 128), f32)),
        in_specs=[VMEM] * 4,
        out_specs=(HBM, VMEM),
        scratch_shapes=[pltpu.SemaphoreType.DMA((blocks,))],
        compiler_params=PARAMS,
        cost_estimate=pl.CostEstimate(flops=0, bytes_accessed=4 * layers * width * width, transcendentals=0),
        name="place_near",
    )(*quarter)
    gw, gb, gc, gbeta, loss = pl.pallas_call(
        functools.partial(place_far_kernel, sizes),
        out_shape=(
            weights,
            jax.ShapeDtypeStruct((layers, width), f32),
            jax.ShapeDtypeStruct((dim, width), f32),
            jax.ShapeDtypeStruct((1, width), f32),
            jax.ShapeDtypeStruct((1, 1), f32),
        ),
        in_specs=[VMEM] * 5 + [HBM],
        out_specs=(HBM,) * 5,
        scratch_shapes=[
            pltpu.VMEM((layers, width), f32),
            pltpu.VMEM((dim, width), f32),
            pltpu.VMEM((1, width), f32),
            pltpu.VMEM((1, 1), f32),
            pltpu.VMEM((blocks, 8, 128), f32),
            pltpu.SemaphoreType.DMA((blocks,)),
            pltpu.SemaphoreType.DMA((4,)),
        ],
        input_output_aliases={5: 0},
        compiler_params=PARAMS,
        name="place_far",
    )(*far, near_ext, gw)
    return (
        gw.reshape(layers, width, width),
        gb,
        gc,
        gbeta.reshape(width),
        loss.reshape(()),
    )


def solution(mesh):
    split = P(AXES)
    return jax.shard_map(
        functools.partial(on_device, mesh.shape["layer"], mesh.shape["phi"]),
        mesh=mesh,
        in_specs=(P(AXES, None), P(), P(), P(), P(), split, split, split),
        out_specs=(P(), P(), P(), P(), P()),
        check_vma=False,
    )
```

```python
import functools

import jax
import jax.numpy as jnp
from jax import lax
from jax.experimental import pallas as pl
from jax.experimental.pallas import tpu as pltpu
from jax.sharding import PartitionSpec as P

dist_eps = 0.0001
charge_floor = 0.5
AXES = ("layer", "phi")
VMEM = pl.BlockSpec(memory_space=pltpu.VMEM)
SMEM = pl.BlockSpec(memory_space=pltpu.SMEM)
HBM = pl.BlockSpec(memory_space=pltpu.HBM)
UNROLL = 16
EMBED_VMEM = 63400000
HIGH = lax.Precision.HIGHEST
PARAMS = pltpu.CompilerParams(vmem_limit_bytes=48 * 1024 * 1024)


def matmul(a, b, ca=1, cb=0, precision=None):
    return lax.dot_general(
        a, b, (((ca,), (cb,)), ((), ())), precision=precision, preferred_element_type=jnp.float32
    )


def iota(shape, dim):
    return lax.broadcasted_iota(jnp.int32, shape, dim)


def head_rows(wc_ref, wb_ref):
    dim = wc_ref.shape[0]
    width = wc_ref.shape[1]
    beta_row = jnp.broadcast_to(wb_ref[...].astype(jnp.float32).reshape(1, width), (dim, width))
    tail = jnp.where(iota((dim, width), 0) == 0, beta_row, 0.0).astype(jnp.bfloat16)
    return jnp.concatenate([wc_ref[...], tail], 0)


def flat_index(axis_sizes):
    return lax.axis_index("layer") * axis_sizes[1] + lax.axis_index("phi")


def block_places(axis_sizes):
    me = flat_index(axis_sizes)
    shift = axis_sizes[1].bit_length() - 1
    core = lax.shift_right_logical(me, shift) & 1
    flat = (lax.shift_right_logical(me, shift + 1) & 1) * 2 + (me & 1)
    line = lax.shift_right_logical(me, 1) & 3
    mine = flat + core * (line - flat)
    return (core * 4, mine), (4 - core * 4, flat + line - mine)


def embed_kernel(
    sizes,
    hit_ref, feat_ref, w_ref, b_ref, wc_ref, wb_ref, track_ref, noise_ref, pay_ref, aux_ref,
):
    dim = wc_ref.shape[0]
    hits = feat_ref.shape[0]
    points = hit_ref.shape[0]
    layers = w_ref.shape[0]
    half = hits // 2
    parts = [feat_ref[0:half, :], feat_ref[half:, :]]
    for l in range(layers):
        pre = [matmul(h, w_ref[l]) + b_ref[l : l + 1, :] for h in parts]
        parts = [(a * jax.nn.sigmoid(a)).astype(jnp.bfloat16) for a in pre]
    h = jnp.concatenate(parts, 0)
    xz = matmul(head_rows(wc_ref, wb_ref), h, 1, 1)
    z = xz[dim : dim + 1]
    expz = jnp.exp(z)
    spread = jnp.log1p(2.0 * expz)
    q = 0.25 * spread * spread + charge_floor
    slope = 0.5 * spread * (2.0 * expz / (1.0 + 2.0 * expz))
    beta = jax.nn.sigmoid(z)
    noise = noise_ref[...]
    label = jnp.where(noise == 0, track_ref[...], -1).astype(jnp.float32)
    rows8 = iota((8, hits), 0)
    aux_ref[0:8, :] = jnp.where(
        rows8 == 0, beta, jnp.where(rows8 == 1, slope, noise.astype(jnp.float32))
    )
    col = jnp.zeros((points, hits), jnp.int32)
    for p in range(points):
        col = jnp.where(rows8 == (p + 2) % points, hit_ref[p], col)
    sel = iota((points, hits), 1) == col
    aux_ref[8:16, :] = jnp.where(sel, 1.0, 0.0)
    lane = iota((points, 128), 1)
    row = iota((points, 128), 0)
    order = jnp.where(row < 2, row + points - 2, row - 2)
    pts = jnp.where(lane == dim + 1, (flat_index(sizes) * points + order).astype(jnp.float32), 0.0)
    for c in range(dim):
        v = jnp.sum(jnp.where(sel, xz[c : c + 1], 0.0), axis=1, keepdims=True)
        pts = jnp.where(lane == c, v, pts)
    v = jnp.sum(jnp.where(sel, q, 0.0), axis=1, keepdims=True)
    pts = jnp.where(lane == dim, v, pts)
    moved = pltpu.roll(pts, 2, 0)
    left = jnp.where(row == 0, q[:, :128], jnp.where(row == 1, label[:, :128], pts))
    right = jnp.where(row == 0, q[:, 128:], jnp.where(row == 1, label[:, 128:], moved))
    pay_ref[0:dim, :] = xz[0:dim]
    pay_ref[dim : dim + 8, 0:128] = left
    pay_ref[dim : dim + 8, 128:256] = right


def residual_kernel(
    feat_ref, w_ref, b_ref, wc_ref, wb_ref, slope_ref, ht_ref, last_ref, wt_ref, head_ref
):
    head_ref[...] = head_rows(wc_ref, wb_ref)
    layers = w_ref.shape[0]
    h = feat_ref[...]
    ht_ref[0] = h.T
    for l in range(layers):
        a = matmul(h, w_ref[l]) + b_ref[l : l + 1, :]
        sig = jax.nn.sigmoid(a)
        slope_ref[l] = sig * (1.0 + a * (1.0 - sig))
        h = (a * sig).astype(jnp.bfloat16)
        if l < layers - 1:
            ht_ref[l + 1] = h.T
            wt_ref[l] = w_ref[l + 1].T
        else:
            last_ref[...] = h


def point_tile(left, right):
    rows = iota(left.shape, 0)
    return jnp.where(rows < 2, pltpu.roll(right, 6, 0), left)


def pair_weights(dist_sq, match):
    shifted = dist_sq + dist_eps
    inv = lax.rsqrt(shifted)
    reach = jnp.maximum(1.0 - shifted * inv, 0.0)
    potential = jnp.where(match, dist_sq, reach * reach)
    weight = jnp.where(match, 2.0, -2.0 * jnp.maximum(inv - 1.0, 0.0))
    return potential, weight


def spread_kernel(pay_ref, copy_ref, own_ref, xb, yb):
    dim = xb.shape[0]
    full = xb.shape[1:]
    copy_ref[...] = pay_ref[...]
    own = pay_ref[dim : dim + 8, :]
    own = point_tile(own[:, :128], own[:, 128:])
    own_ref[...] = own
    for c in range(dim):
        xb[c] = jnp.broadcast_to(pay_ref[c : c + 1, :], full)
        yb[c] = jnp.broadcast_to(own[:, c : c + 1], full)


def pair_sums(pay_ref, own, ref, xb, yb, hit_acc, point_acc):
    dim = xb.shape[0]
    full = xb.shape[1:]
    label_b = jnp.broadcast_to(pay_ref[dim + 1 : dim + 2, :], full)
    index_b = jnp.broadcast_to(own[:, dim + 1 : dim + 2], full)
    zero = jnp.zeros(full, jnp.float32)

    def hit_side(j, acc):
        tile = ref[j, dim : dim + 8, :]
        tile = point_tile(tile[:, :128], tile[:, 128:])
        diffs = []
        dist_sq = zero
        for c in range(dim):
            diff = xb[c] - tile[:, c : c + 1]
            diffs.append(diff)
            dist_sq = dist_sq + diff * diff
        point_q = tile[:, dim : dim + 1]
        potential, weight = pair_weights(dist_sq, label_b == tile[:, dim + 1 : dim + 2])
        weight = weight * point_q
        terms = [weight * diff for diff in diffs] + [potential * point_q]
        return tuple(s + term for s, term in zip(acc, terms))

    def point_side(j, acc):
        diffs = []
        dist_sq = zero
        for c in range(dim):
            diff = yb[c] - ref[j, c : c + 1, :]
            diffs.append(diff)
            dist_sq = dist_sq + diff * diff
        hit_q = ref[j, dim : dim + 1, :]
        potential, weight = pair_weights(dist_sq, index_b == ref[j, dim + 1 : dim + 2, :])
        weight = weight * hit_q
        terms = [weight * diff for diff in diffs] + [potential * hit_q]
        return tuple(s + term[:, :128] + term[:, 128:] for s, term in zip(acc, terms))

    count = ref.shape[0]
    unroll = min(count, UNROLL)
    hit_acc = lax.fori_loop(0, count, hit_side, hit_acc, unroll=unroll)
    point_acc = lax.fori_loop(0, count, point_side, point_acc, unroll=unroll)
    return hit_acc, point_acc


def pair_kernel(parts, pay_ref, own_ref, xb, yb, *rest):
    rows, rest = rest[:parts], rest[parts:]
    hit_ref, point_ref = rest[-2:]
    if len(rest) > 2:
        sums = [tuple(ref[c] for c in range(ref.shape[0])) for ref in rest[:2]]
    else:
        sums = [(jnp.zeros(ref.shape[1:], jnp.float32),) * ref.shape[0] for ref in rest]
    own = own_ref[...]
    for ref in rows:
        sums = pair_sums(pay_ref, own, ref, xb, yb, *sums)
    for ref, values in zip((hit_ref, point_ref), sums):
        for c, value in enumerate(values):
            ref[c] = value


def backward_kernel(
    sizes, hits_all, points_all,
    pay_ref, own_ref, xb, yb, aux_ref, slope_ref, ht_ref, last_ref, wt_ref, head_ref, rows_ref, hit_ref, point_ref,
    keep_ref, send_ref, gx_ref, stack, ext,
):
    dim = xb.shape[0]
    hits = pay_ref.shape[1]
    layers = slope_ref.shape[0]
    points = own_ref.shape[0]
    own = own_ref[...]
    q_row = pay_ref[dim : dim + 1, :]
    hit_acc = tuple(hit_ref[c] for c in range(dim + 1))
    point_acc = tuple(point_ref[c] for c in range(dim + 1))
    hit_acc, point_acc = pair_sums(pay_ref, own, rows_ref, xb, yb, hit_acc, point_acc)

    pot_row = jnp.sum(hit_acc[dim], axis=0, keepdims=True)
    scaled = q_row * (1.0 / hits_all)
    for c in range(dim):
        gx_ref[c : c + 1, :] = jnp.sum(hit_acc[c], axis=0, keepdims=True) * scaled
    lane = iota((8, 128), 1)
    own_q = own[:, dim : dim + 1] * (1.0 / hits_all)
    grads = jnp.where(lane == dim + 1, 1.0, 0.0)
    for c in range(dim):
        v = jnp.sum(point_acc[c], axis=1, keepdims=True) * own_q
        grads = jnp.where(lane == c, v, grads)
    v = jnp.sum(point_acc[dim], axis=1, keepdims=True) * (1.0 / hits_all)
    grads = jnp.where(lane == dim, v, grads)
    added = matmul(grads, aux_ref[8:16, :], 0, 0, HIGH)

    beta = aux_ref[0:1, :]
    noise = aux_ref[2:3, :]
    count = added[dim + 1 : dim + 2]
    grad_q = pot_row * (1.0 / hits_all) + added[dim : dim + 1]
    grad_b = noise * (1.0 / hits_all) - count * (1.0 / points_all)
    grad_z = grad_q * aux_ref[1:2, :] + grad_b * beta * (1.0 - beta)
    per_hit = q_row * pot_row * (1.0 / hits_all) + noise * beta * (1.0 / hits_all)
    per_hit = per_hit - count * beta * (1.0 / points_all)
    loss = jnp.sum(per_hit, axis=1, keepdims=True) + points * 1.0 / points_all

    grad_x = gx_ref[...] + added[0:dim]
    tail = jnp.where(iota((dim, hits), 0) == 0, grad_z, 0.0)
    low = jnp.concatenate([grad_x, tail], 0).astype(jnp.bfloat16)
    head = head_ref[...]
    grad_head = matmul(low, last_ref[...])
    up = matmul(low, head, 0, 0)
    ext[...] = jnp.zeros(ext.shape, jnp.float32)
    cols = [slice(0, 128), slice(128, 256)]
    base = 2 * layers
    for h, col in enumerate(cols):
        ext[base + h * dim : base + (h + 1) * dim, :] = grad_head[0:dim, col]
        ext[base + 2 * dim + h : base + 2 * dim + h + 1, :] = grad_head[dim : dim + 1, col]
    ext[base + 2 * dim + 2 : base + 2 * dim + 3, :] = jnp.broadcast_to(loss, (1, 128))
    blocks = stack.shape[0]
    rows = layers * hits // blocks
    per_layer = blocks // layers
    for l in range(layers - 1, -1, -1):
        err = (up * slope_ref[l]).astype(jnp.bfloat16)
        if l > 0:
            up = matmul(err, wt_ref[l - 1])
        grad_w = matmul(ht_ref[l], err)
        bias = jnp.sum(err.astype(jnp.float32), axis=0, keepdims=True)
        for h, col in enumerate(cols):
            ext[h * layers + l : h * layers + l + 1, :] = bias[:, col]
            for s in range(per_layer):
                stack[l * per_layer + s, h * rows : (h + 1) * rows, :] = grad_w[
                    s * rows : (s + 1) * rows, col
                ]
    for b in range(blocks):
        stack[b, 2 * rows : 2 * rows + 8, :] = ext[8 * b : 8 * b + 8, :]
    for out_ref, (first, place) in zip((keep_ref, send_ref), block_places(sizes)):
        for j in range(blocks // 2):
            out_ref[j] = stack[first + jnp.bitwise_xor(place, j)]


def place_copies(blocks, first, place, gw_ref, sems):
    rows = gw_ref.shape[1]
    copies = []
    for r, block in enumerate(blocks):
        slot = first + jnp.bitwise_xor(place, r)
        for h in range(2):
            copies.append(
                pltpu.make_async_copy(
                    block.at[pl.ds(h * rows, rows)],
                    gw_ref.at[slot, :, pl.ds(h * 128, 128)],
                    sems.at[2 * r + h],
                )
            )
    for copy in copies:
        copy.start()
    return copies


def place_near_kernel(sizes, *refs):
    blocks = refs[:4]
    gw_ref, ext_ref, sems = refs[4:]
    rows = gw_ref.shape[1]
    copies = place_copies(blocks, *block_places(sizes)[0], gw_ref, sems)
    for r, block in enumerate(blocks):
        ext_ref[r] = block[2 * rows :, :]
    for copy in copies:
        copy.wait()


def place_far_kernel(sizes, *refs):
    blocks, (near_ref, _, gw_ref), rest = refs[:4], refs[4:7], refs[7:]
    outs, scratch, (ext, sems, small_sems) = rest[:4], rest[4:8], rest[8:]
    gb_ref, gc_ref, gbeta_ref, loss_ref = scratch
    rows = gw_ref.shape[1]
    half = len(blocks)
    dim = gc_ref.shape[0]
    layers = gb_ref.shape[0]
    (near_first, near_place), (far_first, far_place) = block_places(sizes)
    copies = place_copies(blocks, far_first, far_place, gw_ref, sems)
    for r in range(half):
        ext[near_first + jnp.bitwise_xor(near_place, r)] = near_ref[r]
        ext[far_first + jnp.bitwise_xor(far_place, r)] = blocks[r][2 * rows :, :]
    flat = jnp.concatenate([ext[b] for b in range(2 * half)], 0)
    base = 2 * layers
    for h, col in enumerate([slice(0, 128), slice(128, 256)]):
        gb_ref[:, col] = flat[h * layers : (h + 1) * layers]
        gc_ref[:, col] = flat[base + h * dim : base + (h + 1) * dim]
        gbeta_ref[:, col] = flat[base + 2 * dim + h : base + 2 * dim + h + 1]
    loss_ref[...] = flat[base + 2 * dim + 2 : base + 2 * dim + 3, 0:1]
    for i in range(4):
        copies.append(pltpu.make_async_copy(scratch[i], outs[i], small_sems.at[i]))
        copies[-1].start()
    for copy in copies:
        copy.wait()


def bits_of(size):
    return [1 << t for t in range(size.bit_length() - 1)]


def on_device(layer_size, phi_size, features, w_layers, b_layers, w_coord, w_beta, point_hit, track, noise):
    ndev = layer_size * phi_size
    hits, width = features.shape
    layers = w_layers.shape[0]
    dim = w_coord.shape[0]
    points = point_hit.shape[0]
    hits_all = hits * ndev * 1.0
    points_all = points * ndev * 1.0
    f32 = jnp.float32
    core = phi_size
    plane = [1, 2 * phi_size]
    others = [b for b in bits_of(ndev) if b != core and b not in plane]

    line = others[:2]
    others = others[2:]
    flat_masks = [plane[0], plane[1], plane[0] ^ plane[1]]
    line_masks = [line[0], line[1], line[0] ^ line[1]]

    def swap(x, mask, other=None):
        masks = (mask, mask if other is None else other)
        return lax.ppermute(x, AXES, [(i, i ^ masks[i // core & 1]) for i in range(ndev)])

    sizes = (layer_size, phi_size)
    track = track.reshape(1, hits)
    noise = noise.reshape(1, hits)
    low = jnp.bfloat16

    pay, aux = pl.pallas_call(
        functools.partial(embed_kernel, sizes),
        out_shape=(
            jax.ShapeDtypeStruct((dim + 8, hits), f32),
            jax.ShapeDtypeStruct((16, hits), f32),
        ),
        in_specs=[SMEM] + [VMEM] * 7,
        out_specs=(VMEM,) * 2,
        compiler_params=pltpu.CompilerParams(vmem_limit_bytes=EMBED_VMEM),
        name="embed",
    )(point_hit, features, w_layers, b_layers, w_coord, w_beta, track, noise)

    def residuals(early):
        return pl.pallas_call(
            residual_kernel,
            out_shape=(
                jax.ShapeDtypeStruct((layers, hits, width), f32),
                jax.ShapeDtypeStruct((layers, width, hits), low),
                jax.ShapeDtypeStruct((hits, width), low),
                jax.ShapeDtypeStruct((layers - 1, width, width), low),
                jax.ShapeDtypeStruct((2 * dim, width), low),
            ),
            in_specs=[VMEM] * 5,
            out_specs=(VMEM,) * 5,
            compiler_params=PARAMS,
            cost_estimate=pl.CostEstimate(
                flops=20 * layers * hits * width, bytes_accessed=6 * layers * hits * width,
                transcendentals=layers * hits * width,
            ),
            name="residuals",
        )(*early)

    pay_own, own, xb, yb = pl.pallas_call(
        spread_kernel,
        out_shape=(
            jax.ShapeDtypeStruct((dim + 8, hits), f32),
            jax.ShapeDtypeStruct((8, 128), f32),
            jax.ShapeDtypeStruct((dim, 8, hits), f32),
            jax.ShapeDtypeStruct((dim, 8, hits), f32),
        ),
        in_specs=[VMEM],
        out_specs=(VMEM,) * 4,
        compiler_params=PARAMS,
        cost_estimate=pl.CostEstimate(flops=0, bytes_accessed=80 * dim * hits, transcendentals=0),
        name="spread",
    )(pay)
    rows_all = pay[None]
    kept = pay_own[None]
    for m in others:
        kept = rows_all = jnp.concatenate([kept, swap(rows_all, m)], 0)
    arrived = [swap(rows_all, m) for m in (line[0], line[0] ^ line[1], line[1])]
    rows_all = jnp.concatenate([kept] + arrived, 0)
    rows_all, *early = lax.optimization_barrier((rows_all, features, w_layers, b_layers))
    arrived = [swap(rows_all, m) for m in (plane[0], plane[0] ^ plane[1], plane[1])]
    first_far = swap(rows_all, core)
    rows = jnp.concatenate(arrived, 0)
    slope, ht, last, wt, head = residuals(early + [w_coord, w_beta])
    rows, first_far, slope = lax.optimization_barrier((rows, first_far, slope))
    rows_far = swap(rows, core)

    partial_sums = (
        jax.ShapeDtypeStruct((dim + 1, 8, hits), f32),
        jax.ShapeDtypeStruct((dim + 1, 8, 128), f32),
    )

    def pairs(rows, sums=()):
        count = sum(r.shape[0] for r in rows)
        return pl.pallas_call(
            functools.partial(pair_kernel, len(rows)),
            out_shape=partial_sums,
            in_specs=[VMEM] * (4 + len(rows) + len(sums)),
            out_specs=(VMEM, VMEM),
            compiler_params=PARAMS,
            cost_estimate=pl.CostEstimate(
                flops=200 * points * hits * count, bytes_accessed=count * hits * 64,
                transcendentals=2 * points * hits * count,
            ),
            name="pairs",
        )(pay_own, own, xb, yb, *rows, *sums)

    sums = pairs([rows_all, first_far, rows])

    blocks = 8
    block_rows = 2 * (layers * width // blocks) + 8
    half = jax.ShapeDtypeStruct((blocks // 2, block_rows, 128), f32)
    keep, send = pl.pallas_call(
        functools.partial(backward_kernel, sizes, hits_all, points_all),
        out_shape=(half, half),
        in_specs=[VMEM] * 13,
        out_specs=(VMEM, VMEM),
        scratch_shapes=[
            pltpu.VMEM((dim, hits), f32),
            pltpu.VMEM((blocks, block_rows, 128), f32),
            pltpu.VMEM((8 * blocks, 128), f32),
        ],
        compiler_params=PARAMS,
        name="pairs_backward",
    )(pay_own, own, xb, yb, aux, slope, ht, last, wt, head, rows_far, *sums)

    total = keep + swap(send, core)
    mine = total[0]
    arrived = [swap(total[r + 1], a, b) for r, (a, b) in enumerate(zip(flat_masks, line_masks))]
    mine = (mine + arrived[0]) + (arrived[1] + arrived[2])
    arrived = [swap(mine, line_masks[r], flat_masks[r]) for r in (0, 2, 1)]
    mine = (mine + arrived[0]) + (arrived[1] + arrived[2])
    for m in others:
        mine = mine + swap(mine, m)
    quarter = [mine] + [swap(mine, a, b) for a, b in zip(flat_masks, line_masks)]
    far = [swap(block, core) for block in quarter]

    weights = jax.ShapeDtypeStruct((blocks, layers * width // blocks, width), f32)
    gw, near_ext = pl.pallas_call(
        functools.partial(place_near_kernel, sizes),
        out_shape=(weights, jax.ShapeDtypeStruct((blocks // 2, 8, 128), f32)),
        in_specs=[VMEM] * 4,
        out_specs=(HBM, VMEM),
        scratch_shapes=[pltpu.SemaphoreType.DMA((blocks,))],
        compiler_params=PARAMS,
        cost_estimate=pl.CostEstimate(flops=0, bytes_accessed=4 * layers * width * width, transcendentals=0),
        name="place_near",
    )(*quarter)
    gw, gb, gc, gbeta, loss = pl.pallas_call(
        functools.partial(place_far_kernel, sizes),
        out_shape=(
            weights,
            jax.ShapeDtypeStruct((layers, width), f32),
            jax.ShapeDtypeStruct((dim, width), f32),
            jax.ShapeDtypeStruct((1, width), f32),
            jax.ShapeDtypeStruct((1, 1), f32),
        ),
        in_specs=[VMEM] * 5 + [HBM],
        out_specs=(HBM,) * 5,
        scratch_shapes=[
            pltpu.VMEM((layers, width), f32),
            pltpu.VMEM((dim, width), f32),
            pltpu.VMEM((1, width), f32),
            pltpu.VMEM((1, 1), f32),
            pltpu.VMEM((blocks, 8, 128), f32),
            pltpu.SemaphoreType.DMA((blocks,)),
            pltpu.SemaphoreType.DMA((4,)),
        ],
        input_output_aliases={5: 0},
        compiler_params=PARAMS,
        name="place_far",
    )(*far, near_ext, gw)
    return (
        gw.reshape(layers, width, width),
        gb,
        gc,
        gbeta.reshape(width),
        loss.reshape(()),
    )


def solution(mesh):
    split = P(AXES)
    return jax.shard_map(
        functools.partial(on_device, mesh.shape["layer"], mesh.shape["phi"]),
        mesh=mesh,
        in_specs=(P(AXES, None), P(), P(), P(), P(), split, split, split),
        out_specs=(P(), P(), P(), P(), P()),
        check_vma=False,
    )
```
